32 devices in a mesh: gx: 2 (over y), gy: 4 (over z), gz: 4 (over x, core).
Axes of the slice: x: 2, y: 2, z: 4, core: 2. Of those that a mesh axis runs over, the one named last changes fastest.
Arguments:
- e_adjoint: float32 [3, 64, 64, 1024], P(None, 'gx', 'gy', 'gz'), may hold values from -6 to 6
- h_adjoint: float32 [3, 64, 64, 1024], P(None, 'gx', 'gy', 'gz'), may hold values from -6 to 6
- snapshots: bfloat16 [3, 3, 64, 64, 1024], P(None, None, 'gx', 'gy', 'gz'), may hold values from -6 to 6
- material: int32 [64, 64, 1024], P('gx', 'gy', 'gz'), may hold values from 0 to 7
- permittivity: float32 [8], replicated, may hold values from 1 to 12
- design_mask: int32 [64, 64], P('gx', 'gy'), may hold values from 0 to 1
- ports: int32 [3], replicated, may hold values from 0 to 4194303
- amplitudes: float32 [2, 3], replicated, may hold values from -8 to 8
Outputs:
- e_final: float32 [3, 64, 64, 1024], P(None, 'gx', 'gy', 'gz')
- h_final: float32 [3, 64, 64, 1024], P(None, 'gx', 'gy', 'gz')
- gradient: float32 [64, 64], P('gx', ('gy', 'gz'))
The draws below stay inside these ranges and needn't reach their ends.
All inputs are finite; a program needn't handle non-finite values.
Results may differ from the reference program's by a relative error of at most 0.0003.
Values sent between devices are 32-bit elements; how exact they have to be, the bound alone decides.
No kernel may reach another device: no remote copies, remote signals or barrier semaphores. Data moves between devices by JAX's collectives and lax.ppermute only.
A program may use at most 64 MiB of HBM per device.

```python
import math
import jax
import jax.numpy as jnp
from jax import lax

NMAT = 8
NPORT = 3
STEPS = 2
NX = 64
NY = 64
NZ = 1024


def with_ends(result, key, least, high):
    place = [jax.random.randint(jax.random.fold_in(key, axis), (), 0, length) for axis, length in enumerate(result.shape)]
    widest = result.shape.index(max(result.shape))
    beside = place[:widest] + [(place[widest] + 1) % result.shape[widest]] + place[widest + 1:]
    return result.at[tuple(place)].set(least).at[tuple(beside)].set(high)


def block_scale(own_key, extent, cuts, smallest, largest):
    gain, own = 1.0, jax.random.fold_in(own_key, 6)
    for axis_at, blocks in cuts:
        steps = jnp.exp(jax.random.uniform(jax.random.fold_in(own, axis_at), (blocks,), jnp.float32, smallest / len(cuts), largest / len(cuts)))
        gain = gain * jnp.repeat(steps, extent[axis_at] // blocks).reshape([-1 if axis == axis_at else 1 for axis in range(len(extent))])
    return gain


def scatter_about(own_key, extent, deviation, most, split=(), held_as=jnp.bfloat16):
    loudness = block_scale(own_key, extent, split, -0.22, 0.18) if split else 1.0
    values = jax.random.normal(own_key, extent, jnp.float32) * deviation * loudness
    return jnp.minimum(jnp.maximum(values, -most), most).astype(held_as)


def setup_inputs(seed: int = 0) -> dict:
    splits = jax.random.split(jax.random.key(seed), 9)
    return {
        "e_adjoint": scatter_about(splits[0], (3, NX, NY, NZ), 1.0, 6.0, ((1, 2), (2, 4), (3, 4)), jnp.float32),
        "h_adjoint": scatter_about(splits[1], (3, NX, NY, NZ), 1.0, 6.0, ((1, 2), (2, 4), (3, 4)), jnp.float32),
        "snapshots": scatter_about(splits[2], (STEPS + 1, 3, NX, NY, NZ), 1.0, 6.0, ((2, 2), (3, 4), (4, 4))),
        "material": with_ends(jax.random.randint(splits[3], (NX, NY, NZ), 0, NMAT), jax.random.fold_in(splits[3], 1), 0, NMAT - 1).astype(jnp.int32),
        "permittivity": jnp.clip(jnp.exp(jax.random.uniform(splits[4], (NMAT,), jnp.float32, math.log(1.0), math.log(12.0))), 1.0, 12.0),
        "design_mask": with_ends(jax.random.randint(splits[5], (NX, NY), 0, 2), jax.random.fold_in(splits[5], 1), 0, 1).astype(jnp.int32),
        "ports": jax.random.randint(splits[6], (NPORT,), 0, NX * NY * NZ).astype(jnp.int32),
        "amplitudes": scatter_about(splits[7], (STEPS, NPORT), 2.0, 8.0, (), jnp.float32),
    }


magnetic_step = 0.5
electric_step = 0.5


def shifted_up(field, axis):
    widths = [(0, 0), (0, 0), (0, 0)]
    widths[axis] = (0, 1)
    return jnp.pad(lax.slice_in_dim(field, 1, field.shape[axis], axis=axis), widths)


def shifted_down(field, axis):
    widths = [(0, 0), (0, 0), (0, 0)]
    widths[axis] = (1, 0)
    return jnp.pad(lax.slice_in_dim(field, 0, field.shape[axis] - 1, axis=axis), widths)


def curl_electric(field):
    comp_x, comp_y, comp_z = field[0], field[1], field[2]
    out_x = (shifted_up(comp_z, 1) - comp_z) - (shifted_up(comp_y, 2) - comp_y)
    out_y = (shifted_up(comp_x, 2) - comp_x) - (shifted_up(comp_z, 0) - comp_z)
    out_z = (shifted_up(comp_y, 0) - comp_y) - (shifted_up(comp_x, 1) - comp_x)
    return jnp.stack([out_x, out_y, out_z])


def curl_magnetic(field):
    comp_x, comp_y, comp_z = field[0], field[1], field[2]
    out_x = (comp_z - shifted_down(comp_z, 1)) - (comp_y - shifted_down(comp_y, 2))
    out_y = (comp_x - shifted_down(comp_x, 2)) - (comp_z - shifted_down(comp_z, 0))
    out_z = (comp_y - shifted_down(comp_y, 0)) - (comp_x - shifted_down(comp_x, 1))
    return jnp.stack([out_x, out_y, out_z])


def reference(e_adjoint, h_adjoint, snapshots, material, permittivity, design_mask, ports, amplitudes):
    coef = (electric_step / permittivity)[material]
    plane = NY * NZ
    port_x = (ports // plane).astype(jnp.int32)
    port_y = ((ports // NZ) % NY).astype(jnp.int32)
    port_z = (ports % NZ).astype(jnp.int32)
    electric = e_adjoint
    magnetic = h_adjoint
    corr = jnp.zeros(material.shape, jnp.float32)
    for step_no in range(STEPS):
        magnetic = magnetic - magnetic_step * curl_electric(electric)
        electric = electric + coef[None] * curl_magnetic(magnetic)
        electric = electric.at[2, port_x, port_y, port_z].add(amplitudes[step_no])
        change = snapshots[step_no].astype(jnp.float32) - snapshots[step_no + 1].astype(jnp.float32)
        corr = corr + jnp.sum(electric * change, axis=0)
    gradient = design_mask.astype(jnp.float32) * jnp.sum(corr, axis=2)
    return electric, magnetic, gradient
```

```python
import functools

import jax
import jax.numpy as jnp
from jax import lax
from jax.experimental import pallas as pl
from jax.experimental.pallas import tpu as pltpu
from jax.sharding import PartitionSpec as P

STEPS = 2
FIELDS = 7
HALO = 8
HIGHEST = lax.Precision.HIGHEST

magnetic_step = 0.5
electric_step = 0.5

VM = pl.BlockSpec(memory_space=pltpu.VMEM)
SM = pl.BlockSpec(memory_space=pltpu.SMEM)


def in_vmem(array):
    return pltpu.with_memory_space_constraint(array, pltpu.VMEM)


def swap_table(size, odd):
    table = list(range(size))
    for i in range(odd, size - 1, 2):
        table[i], table[i + 1] = i + 1, i
    return table


def swaps(size):
    return [odd for odd in (0, 1) if odd + 1 < size]


def sends_up(index, odd):
    return lax.rem(index, 2) == odd


def has_partner(index, size, odd):
    up = sends_up(index, odd)
    return (up & (index + 1 < size)) | (jnp.logical_not(up) & (index >= 1))


def slots(axis):
    near = [(f, 0) for f in range(FIELDS)]
    far = [(f, 1) for f in range(3)] + [(3 + f, 1) for f in range(3) if f != axis]
    return near + far


def coef_of(material, perm_ref):
    count = perm_ref.shape[0]
    out = jnp.zeros(material.shape, jnp.float32)
    for i in range(count):
        value = electric_step / jnp.full((1, 1), perm_ref[i], jnp.float32)
        out = jnp.where(material == i, value, out)
    return out


def tiled(array):
    *lead, nx, ny, nz = array.shape
    n = len(lead)
    split = array.reshape(*lead, nx, ny // 8, 8, nz // 128, 128)
    order = tuple(range(n + 2)) + (n + 3, n + 2, n + 4)
    return split.transpose(order).reshape(*lead, nx * ny * nz // 128, 128)


def untiled(array, dims):
    nx, ny, nz = dims
    lead = array.shape[:-2]
    n = len(lead)
    split = array.reshape(*lead, nx, ny // 8, nz // 128, 8, 128)
    order = tuple(range(n + 2)) + (n + 3, n + 2, n + 4)
    return split.transpose(order).reshape(*lead, nx, ny, nz)


def pack_faces(dims, sizes, e_ref, h_ref, m_ref, perm_ref, *outs):
    nx, ny, nz = dims
    lanes = nz // 128
    plane = ny * lanes
    gx, gy = lax.axis_index("gx"), lax.axis_index("gy")
    xs, ys = swaps(sizes[0]), swaps(sizes[1])

    def rows(field, index):
        if field < 3:
            return e_ref[field, index, :]
        if field < 6:
            return h_ref[field - 3, index, :]
        return coef_of(m_ref[index, :], perm_ref)

    def y_row(y, z):
        return ((y // 8) * lanes + z) * 8 + y % 8

    def x_ends(odd):
        up = sends_up(gx, odd)
        return jnp.where(up, nx - 1, 0) * plane, jnp.where(up, nx - 2, 1) * plane

    def y_ends(odd, z):
        up = sends_up(gy, odd)
        return (
            jnp.where(up, y_row(ny - 1, z), y_row(0, z)),
            jnp.where(up, y_row(ny - 2, z), y_row(1, z)),
        )

    at = 0
    for odd in xs:
        place = x_ends(odd)
        for k, (f, far) in enumerate(slots(0)):
            outs[at][k] = rows(f, pl.ds(pl.multiple_of(place[far], 8), plane))
        at += 1
    for odd in ys:
        for z in range(lanes):
            place = y_ends(odd, z)
            for k, (f, far) in enumerate(slots(1)):
                outs[at][k, z] = rows(f, pl.ds(place[far], nx, stride=plane))
        at += 1
    for ox in xs:
        for oy in ys:
            px = x_ends(ox)
            for z in range(lanes):
                py = y_ends(oy, z)
                for f in range(FIELDS):
                    for k in range(4):
                        outs[at][z, pl.ds(4 * f + k, 1), :] = rows(f, pl.ds(px[k // 2] + py[k % 2], 1))
            at += 1


def gather_block(dims, sizes, e_ref, h_ref, m_ref, perm_ref, *refs):
    nx, ny, nz = dims
    lanes = nz // 128
    step = ny + HALO
    gx, gy = lax.axis_index("gx"), lax.axis_index("gy")
    xs, ys = swaps(sizes[0]), swaps(sizes[1])
    n_msgs = len(xs) + len(ys) + len(xs) * len(ys)
    msgs = refs[:n_msgs]
    ext, up_ref, down_ref, packed = refs[n_msgs:]

    def own_plane(x, carry):
        for f in range(FIELDS):
            for z in range(lanes):
                for t in range(ny // 8):
                    here = pl.ds(pl.multiple_of((x * (ny // 8) + t) * lanes * 8 + z * 8, 8), 8)
                    there = pl.ds(pl.multiple_of((x + 2) * step + t * 8, 8), 8)
                    if f < 3:
                        ext[f, z, there, :] = e_ref[f, here, :]
                    elif f < 6:
                        ext[f, z, there, :] = h_ref[f - 3, here, :]
                    else:
                        ext[f, z, there, :] = coef_of(m_ref[here, :], perm_ref)
                ext[f, z, pl.ds(pl.multiple_of((x + 2) * step + ny, 8), HALO), :] = jnp.zeros(
                    (HALO, 128), jnp.float32
                )
        return carry

    lax.fori_loop(0, nx, own_plane, 0)
    for f in range(FIELDS):
        for z in range(lanes):
            for p in (0, 1, nx + 2, nx + 3):
                ext[f, z, pl.ds(p * step, step), :] = jnp.zeros((step, 128), jnp.float32)

    def planes(odd):
        high = sends_up(gx, odd)
        return jnp.where(high, nx + 2, 1), jnp.where(high, nx + 3, 0)

    def lines(odd):
        high = sends_up(gy, odd)
        return jnp.where(high, ny, step - 1), jnp.where(high, ny + 1, step - 2)

    at = 0
    for odd in xs:
        ok = has_partner(gx, sizes[0], odd)
        place = planes(odd)
        for k, (f, far) in enumerate(slots(0)):
            for z in range(lanes):
                for t in range(ny // 8):
                    ext[f, z, pl.ds(pl.multiple_of(place[far] * step + t * 8, 8), 8), :] = jnp.where(
                        ok, msgs[at][k, pl.ds((t * lanes + z) * 8, 8), :], 0.0
                    )
        at += 1
    for odd in ys:
        ok = has_partner(gy, sizes[1], odd)
        place = lines(odd)
        for k, (f, far) in enumerate(slots(1)):
            for z in range(lanes):
                ext[f, z, pl.ds(2 * step + place[far], nx, stride=step), :] = jnp.where(
                    ok, msgs[at][k, z], 0.0
                )
        at += 1
    for ox in xs:
        for oy in ys:
            ok = has_partner(gx, sizes[0], ox) & has_partner(gy, sizes[1], oy)
            px, py = planes(ox), lines(oy)
            for z in range(lanes):
                for f in range(FIELDS):
                    for k in range(4):
                        ext[f, z, pl.ds(px[k // 2] * step + py[k % 2], 1), :] = jnp.where(
                            ok, msgs[at][z, pl.ds(4 * f + k, 1), :], 0.0
                        )
            at += 1

    total = (nx + 4) * step
    padded = packed.shape[0]
    lane = lax.broadcasted_iota(jnp.int32, (step, 128), 1)

    def pack_plane(p, carry):
        index = pl.ds(pl.multiple_of(p * step, 8), step)
        out = jnp.zeros((step, 128), jnp.float32)
        for f in range(FIELDS):
            both = jnp.where(lane < 64, ext[f, 0, index, :], ext[f, lanes - 1, index, :])
            turned = pltpu.roll(both, 4 * f + 2, 1)
            out = jnp.where((lane >= 4 * f) & (lane < 4 * f + 4), turned, out)
        packed[index, :] = out
        return carry

    lax.fori_loop(0, nx + 4, pack_plane, 0)
    if padded > total:
        packed[total:padded, :] = jnp.zeros((padded - total, 128), jnp.float32)
    for b in range(padded // 128):
        block = jnp.transpose(packed[b * 128 : (b + 1) * 128, :])
        for f in range(FIELDS):
            up_ref[f : f + 1, b * 128 : (b + 1) * 128] = block[4 * f + 1 : 4 * f + 2, :]
            up_ref[8 + f : 9 + f, b * 128 : (b + 1) * 128] = block[4 * f : 4 * f + 1, :]
            down_ref[f : f + 1, b * 128 : (b + 1) * 128] = block[4 * f + 2 : 4 * f + 3, :]
            down_ref[8 + f : 9 + f, b * 128 : (b + 1) * 128] = block[4 * f + 3 : 4 * f + 4, :]
    for row in (7, 15):
        up_ref[row : row + 1, :] = jnp.zeros((1, padded), jnp.float32)
        down_ref[row : row + 1, :] = jnp.zeros((1, padded), jnp.float32)


def march(
    dims, sizes, ext, low_ref, high_ref, snap_ref, mask_ref, ports_ref, amps_ref, *refs
):
    nx, ny, nz = dims
    step = ny + HALO
    lanes = nz // 128
    wide = nz + 128
    parts = sizes[2]
    e_out, h_out = refs[0], refs[1]
    grads = refs[2 : 2 + parts]
    ends, rows_ref, e1, h1, h2, half_ref, sums = refs[2 + parts :]
    gx, gy, gz = lax.axis_index("gx"), lax.axis_index("gy"), lax.axis_index("gz")
    padded = rows_ref.shape[1]

    rows_ref[...] = jnp.zeros(rows_ref.shape, jnp.float32)
    low_ok, high_ok = gz > 0, gz < sizes[2] - 1
    for f in range(FIELDS):
        rows_ref[4 * f : 4 * f + 1, :] = jnp.where(low_ok, low_ref[8 + f : 9 + f, :], 0.0)
        rows_ref[4 * f + 1 : 4 * f + 2, :] = jnp.where(low_ok, low_ref[f : f + 1, :], 0.0)
        rows_ref[4 * f + 2 : 4 * f + 3, :] = jnp.where(high_ok, high_ref[f : f + 1, :], 0.0)
        rows_ref[4 * f + 3 : 4 * f + 4, :] = jnp.where(high_ok, high_ref[8 + f : 9 + f, :], 0.0)
    for b in range(padded // 128):
        block = jnp.transpose(rows_ref[:, b * 128 : (b + 1) * 128])
        for f in range(FIELDS):
            ends[f, b * 128 : (b + 1) * 128, :] = pltpu.roll(block, 128 - (4 * f + 2), 1)

    row = lax.broadcasted_iota(jnp.int32, (step, wide), 0)
    lane = lax.broadcasted_iota(jnp.int32, (step, wide), 1)
    inside = (
        ((row < ny) | ((row < ny + 2) & (gy < sizes[1] - 1)) | ((row >= ny + 4) & (gy > 0)))
        & ((lane < nz) | ((lane < nz + 64) & high_ok) | ((lane >= nz + 64) & low_ok))
    )
    half_ref[...] = jnp.where(inside, magnetic_step, 0.0)

    plane_cells = (ny * sizes[1]) * (nz * sizes[2])
    line_cells = nz * sizes[2]
    spots = []
    for q in range(ports_ref.shape[0]):
        cell = ports_ref[q]
        sx = lax.div(cell, plane_cells) - gx * nx
        sy = lax.rem(lax.div(cell, line_cells), ny * sizes[1]) - gy * ny
        sz = lax.rem(cell, line_cells) - gz * nz
        near = (sy >= -2) & (sy < ny + 2) & (sz >= -2) & (sz < nz + 2)
        own = (sy >= 0) & (sy < ny) & (sz >= 0) & (sz < nz)
        spots.append(
            (sx + 2, jnp.where(sy < 0, sy + step, sy), jnp.where(sz < 0, sz + wide, sz), near, own)
        )

    def load(f, p):
        index = pl.ds(pl.multiple_of(p * step, 8), step)
        return jnp.concatenate(
            [ext[f, z, index, :] for z in range(lanes)] + [ends[f, index, :]], axis=1
        )

    def spot(x, t, z):
        return pl.ds(pl.multiple_of(((x * (ny // 8) + t) * lanes + z) * 8, 8), 8)

    def put(ref, f, x, v):
        for t in range(ny // 8):
            for z in range(lanes):
                ref[f, spot(x, t, z), :] = v[t * 8 : t * 8 + 8, z * 128 : z * 128 + 128]

    def take(ref, f, x):
        return jnp.concatenate(
            [
                jnp.concatenate([ref[f, spot(x, t, z), :] for z in range(lanes)], axis=1)
                for t in range(ny // 8)
            ],
            axis=0,
        )

    def y_up(v):
        return pltpu.roll(v, step - 1, 0)

    def y_down(v):
        return pltpu.roll(v, 1, 0)

    def z_up(v):
        return pltpu.roll(v, wide - 1, 1)

    def z_down(v):
        return pltpu.roll(v, 1, 1)

    def new_h(p, half, ex, ey, ez, ey_x, ez_x, hx, hy, hz):
        cx = (y_up(ez) - ez) - (z_up(ey) - ey)
        cy = (z_up(ex) - ex) - (ez_x - ez)
        cz = (ey_x - ey) - (y_up(ex) - ex)
        return hx - half * cx, hy - half * cy, hz - half * cz

    def new_e(coef, ex, ey, ez, hx, hy, hz, hy_x, hz_x):
        cx = (hz - y_down(hz)) - (hy - z_down(hy))
        cy = (hx - z_down(hx)) - (hz - hz_x)
        cz = (hy - hy_x) - (hx - y_down(hx))
        return ex + coef * cx, ey + coef * cy, ez + coef * cz

    def half_of(p):
        out = ((p < 2) & (gx == 0)) | ((p >= nx + 2) & (gx == sizes[0] - 1))
        return half_ref[...] * jnp.where(out, 0.0, 1.0)

    def first_h(p):
        e = [load(f, p) for f in range(3)]
        h = [load(3 + f, p) for f in range(3)]
        out = new_h(p, half_of(p), *e, load(1, p + 1), load(2, p + 1), *h)
        for f in range(3):
            h1[f, p] = out[f]

    def first_e(p):
        e = [load(f, p) for f in range(3)]
        h = [h1[f, p] for f in range(3)]
        out = new_e(load(6, p), *e, *h, h1[1, p - 1], h1[2, p - 1])
        for f in range(3):
            e1[f, p] = out[f]
        for q, (sx, sy, sz, near, own) in enumerate(spots):

            @pl.when(near & (sx == p))
            def _():
                e1[2, p] = e1[2, p] + jnp.where((row == sy) & (lane == sz), amps_ref[0, q], 0.0)

    def second_h(p):
        e = [e1[f, p] for f in range(3)]
        h = [h1[f, p] for f in range(3)]
        out = new_h(p, half_of(p), *e, e1[1, p + 1], e1[2, p + 1], *h)
        for f in range(3):
            h2[f, p] = out[f]
        return out

    def second_e(p):
        e = [e1[f, p] for f in range(3)]
        h = [h2[f, p] for f in range(3)]
        out = new_e(load(6, p), *e, *h, h2[1, p - 1], h2[2, p - 1])
        index = pl.ds(pl.multiple_of((p - 2) * ny, ny), ny)
        for f in range(3):
            put(e_out, f, p - 2, out[f])
            put(h_out, f, p - 2, h[f])
        for q, (sx, sy, sz, near, own) in enumerate(spots):

            @pl.when(own & (sx == p))
            def _():
                put(
                    e_out,
                    2,
                    p - 2,
                    take(e_out, 2, p - 2)
                    + jnp.where((row[:ny, :nz] == sy) & (lane[:ny, :nz] == sz), amps_ref[1, q], 0.0),
                )

        total = jnp.zeros((ny, nz), jnp.float32)
        for f in range(3):
            s = [snap_ref[t, f, index, :].astype(jnp.float32) for t in range(STEPS + 1)]
            total = total + e[f][:ny, :nz] * (s[0] - s[1])
            total = total + take(e_out, f, p - 2) * (s[1] - s[2])
        folded = total[:, 0:128]
        for at in range(128, nz, 128):
            folded = folded + total[:, at : at + 128]
        sums[index, :] = folded

    first_h(0)
    first_h(1)
    first_e(1)
    first_h(2)
    first_e(2)
    second_h(1)

    def body(p, carry):
        first_h(p)
        first_e(p)
        second_h(p - 1)
        second_e(p - 1)
        return carry

    lax.fori_loop(3, nx + 3, body, 0)

    cells = nx * ny
    nt = (((1,), (1,)), ((), ()))
    nn = (((1,), (0,)), ((), ()))
    lined = lax.dot_general(jnp.ones((8, 128), jnp.float32), sums[...], nt, precision=HIGHEST)
    spread = jnp.where(
        lax.broadcasted_iota(jnp.int32, (nx, cells), 1) // ny
        == lax.broadcasted_iota(jnp.int32, (nx, cells), 0),
        lined[0:1, :],
        0.0,
    )
    pick = (
        lax.rem(lax.broadcasted_iota(jnp.int32, (cells, ny), 0), ny)
        == lax.broadcasted_iota(jnp.int32, (cells, ny), 1)
    ).astype(jnp.float32)
    column = lax.dot_general(spread, pick, nn, precision=HIGHEST) * mask_ref[...].astype(jnp.float32)
    width = ny // parts
    for shift in range(parts):
        owner = lax.rem(gz + shift, parts)
        choose = (
            lax.broadcasted_iota(jnp.int32, (ny, width), 0)
            == owner * width + lax.broadcasted_iota(jnp.int32, (ny, width), 1)
        ).astype(jnp.float32)
        grads[shift][...] = lax.dot_general(column, choose, nn, precision=HIGHEST)


def params(limit=12):
    return pltpu.CompilerParams(vmem_limit_bytes=limit * 1024 * 1024)


def body(sizes, e_adjoint, h_adjoint, snapshots, material, permittivity, design_mask, ports, amplitudes):
    dims = material.shape
    nx, ny, nz = dims
    lanes = nz // 128
    step = ny + HALO
    total = (nx + 4) * step
    padded = -(-total // 128) * 128
    f32 = jnp.float32
    cells = nx * ny
    e = in_vmem(tiled(e_adjoint))
    h = in_vmem(tiled(h_adjoint))
    m = in_vmem(tiled(material))
    s = in_vmem(snapshots.reshape(STEPS + 1, 3, cells, nz))
    xs, ys = swaps(sizes[0]), swaps(sizes[1])

    shapes = [jax.ShapeDtypeStruct((len(slots(0)), ny * lanes, 128), f32) for _ in xs]
    shapes += [jax.ShapeDtypeStruct((len(slots(1)), lanes, nx, 128), f32) for _ in ys]
    shapes += [jax.ShapeDtypeStruct((lanes, 4 * FIELDS, 128), f32) for _ in xs for _ in ys]
    msgs = pl.pallas_call(
        functools.partial(pack_faces, dims, sizes),
        out_shape=shapes,
        in_specs=[VM, VM, VM, SM],
        out_specs=[VM] * len(shapes),
        compiler_params=params(),
        name="pack_faces",
    )(e, h, m, permittivity)

    both = ("gx", "gy")
    tables = [("gx", list(enumerate(swap_table(sizes[0], o)))) for o in xs]
    tables += [("gy", list(enumerate(swap_table(sizes[1], o)))) for o in ys]
    for ox in xs:
        for oy in ys:
            tx, ty = swap_table(sizes[0], ox), swap_table(sizes[1], oy)
            pairs = [
                (x * sizes[1] + y, tx[x] * sizes[1] + ty[y])
                for x in range(sizes[0])
                for y in range(sizes[1])
            ]
            tables.append((both, pairs))
    got = [lax.ppermute(msg, axis, pairs) for msg, (axis, pairs) in zip(msgs, tables)]

    ext, up, down = pl.pallas_call(
        functools.partial(gather_block, dims, sizes),
        out_shape=[
            pltpu.VMEM((FIELDS, lanes, total, 128), f32),
            jax.ShapeDtypeStruct((16, padded), f32),
            jax.ShapeDtypeStruct((16, padded), f32),
        ],
        in_specs=[VM, VM, VM, SM] + [VM] * len(got),
        out_specs=[VM] * 3,
        scratch_shapes=[pltpu.VMEM((padded, 128), f32)],
        compiler_params=params(),
        name="gather_block",
    )(e, h, m, permittivity, *got)

    parts = sizes[2]
    low = lax.ppermute(up, "gz", [(i, (i + 1) % parts) for i in range(parts)])
    high = lax.ppermute(down, "gz", [(i, (i - 1) % parts) for i in range(parts)])

    wide = nz + 128
    out = pl.pallas_call(
        functools.partial(march, dims, sizes),
        out_shape=[
            jax.ShapeDtypeStruct(e.shape, f32),
            jax.ShapeDtypeStruct(h.shape, f32),
        ]
        + [jax.ShapeDtypeStruct((nx, ny // parts), f32)] * parts,
        in_specs=[VM, VM, VM, VM, VM, SM, SM],
        out_specs=[VM] * (2 + parts),
        scratch_shapes=[
            pltpu.VMEM((FIELDS, padded, 128), f32),
            pltpu.VMEM((128, padded), f32),
            pltpu.VMEM((3, nx + 4, step, wide), f32),
            pltpu.VMEM((3, nx + 4, step, wide), f32),
            pltpu.VMEM((3, nx + 4, step, wide), f32),
            pltpu.VMEM((step, wide), f32),
            pltpu.VMEM((cells, 128), f32),
        ],
        compiler_params=params(30),
        name="march",
    )(in_vmem(ext), low, high, s, design_mask, ports, amplitudes)
    gradient = out[2]
    for shift in range(1, parts):
        gradient = gradient + lax.ppermute(
            out[2 + shift], "gz", [(i, (i + shift) % parts) for i in range(parts)]
        )
    return untiled(out[0], dims), untiled(out[1], dims), gradient


def solution(mesh):
    placed = (
        P(None, "gx", "gy", "gz"),
        P(None, "gx", "gy", "gz"),
        P(None, None, "gx", "gy", "gz"),
        P("gx", "gy", "gz"),
        P(),
        P("gx", "gy"),
        P(),
        P(),
    )
    sizes = tuple(mesh.shape[axis] for axis in ("gx", "gy", "gz"))
    return jax.shard_map(
        functools.partial(body, sizes),
        mesh=mesh,
        in_specs=placed,
        out_specs=(P(None, "gx", "gy", "gz"), P(None, "gx", "gy", "gz"), P("gx", ("gy", "gz"))),
        check_vma=False,
    )
```

```python
import functools

import jax
import jax.numpy as jnp
from jax import lax
from jax.experimental import pallas as pl
from jax.experimental.pallas import tpu as pltpu
from jax.sharding import PartitionSpec as P

STEPS = 2
FIELDS = 7
HALO = 8
HIGHEST = lax.Precision.HIGHEST

magnetic_step = 0.5
electric_step = 0.5

VM = pl.BlockSpec(memory_space=pltpu.VMEM)
SM = pl.BlockSpec(memory_space=pltpu.SMEM)
ANY = pl.BlockSpec(memory_space=pl.ANY)


HBM = pl.BlockSpec(memory_space=pltpu.HBM)


def in_hbm(array):
    return pltpu.with_memory_space_constraint(array, pltpu.HBM)


def in_vmem(array):
    return pltpu.with_memory_space_constraint(array, pltpu.VMEM)


def swap_table(size, odd):
    table = list(range(size))
    for i in range(odd, size - 1, 2):
        table[i], table[i + 1] = i + 1, i
    return table


def swaps(size):
    return [odd for odd in (0, 1) if odd + 1 < size]


def sends_up(index, odd):
    return lax.rem(index, 2) == odd


def has_partner(index, size, odd):
    up = sends_up(index, odd)
    return (up & (index + 1 < size)) | (jnp.logical_not(up) & (index >= 1))


def slots(axis):
    near = [(f, 0) for f in range(FIELDS)]
    far = [(f, 1) for f in range(3)] + [(3 + f, 1) for f in range(3) if f != axis]
    return near + far


def coef_table(perm_ref):
    return [
        electric_step / jnp.full((1, 1), perm_ref[i], jnp.float32) for i in range(perm_ref.shape[0])
    ]


def coef_of(material, table):
    out = jnp.zeros(material.shape, jnp.float32)
    for i, value in enumerate(table):
        out = jnp.where(material == i, value, out)
    return out


def tiled(array):
    *lead, nx, ny, nz = array.shape
    n = len(lead)
    split = array.reshape(*lead, nx, ny // 8, 8, nz // 128, 128)
    order = tuple(range(n + 2)) + (n + 3, n + 2, n + 4)
    return split.transpose(order).reshape(*lead, nx * ny * nz // 128, 128)


def untiled(array, dims):
    nx, ny, nz = dims
    lead = array.shape[:-2]
    n = len(lead)
    split = array.reshape(*lead, nx, ny // 8, nz // 128, 8, 128)
    order = tuple(range(n + 2)) + (n + 3, n + 2, n + 4)
    return split.transpose(order).reshape(*lead, nx, ny, nz)


def load_faces(dims, sizes, e_ref, h_ref, m_ref, perm_ref, e_v, h_v, m_v, *refs):
    nx, ny, nz = dims
    lanes = nz // 128
    plane = ny * lanes
    outs, sems = refs[:-1], refs[-1]
    gx, gy = lax.axis_index("gx"), lax.axis_index("gy")
    xs, ys = swaps(sizes[0]), swaps(sizes[1])
    copies = [pltpu.make_async_copy(e_ref.at[f], e_v.at[f], sems.at[f]) for f in range(3)]
    copies += [pltpu.make_async_copy(h_ref.at[f], h_v.at[f], sems.at[3 + f]) for f in range(3)]
    copies += [pltpu.make_async_copy(m_ref, m_v, sems.at[6])]
    for copy in copies:
        copy.start()
    table = coef_table(perm_ref)

    def rows(field, index):
        if field < 3:
            return e_v[field, index, :]
        if field < 6:
            return h_v[field - 3, index, :]
        return coef_of(m_v[index, :], table)

    def y_row(y, z):
        return ((y // 8) * lanes + z) * 8 + y % 8

    def x_ends(odd):
        up = sends_up(gx, odd)
        return jnp.where(up, nx - 1, 0) * plane, jnp.where(up, nx - 2, 1) * plane

    def y_ends(odd, z):
        up = sends_up(gy, odd)
        return (
            jnp.where(up, y_row(ny - 1, z), y_row(0, z)),
            jnp.where(up, y_row(ny - 2, z), y_row(1, z)),
        )

    for field in range(FIELDS):
        copies[field].wait()
        at = 0
        for odd in xs:
            place = x_ends(odd)
            for k, (f, far) in enumerate(slots(0)):
                if f == field:
                    outs[at][k] = rows(f, pl.ds(pl.multiple_of(place[far], 8), plane))
            at += 1
        for odd in ys:
            for z in range(lanes):
                place = y_ends(odd, z)
                for k, (f, far) in enumerate(slots(1)):
                    if f == field:
                        outs[at][k, z] = rows(f, pl.ds(place[far], nx, stride=plane))
            at += 1
        for ox in xs:
            for oy in ys:
                px = x_ends(ox)
                for z in range(lanes):
                    py = y_ends(oy, z)
                    for k in range(4):
                        outs[at][z, pl.ds(4 * field + k, 1), :] = rows(
                            field, pl.ds(px[k // 2] + py[k % 2], 1)
                        )
                at += 1


def turn_ends(parts, lane):
    out = None
    for f in range(FIELDS):
        first, last = parts(f)
        turned = pltpu.roll(jnp.where(lane < 64, first, last), 4 * f + 2, 1)
        out = turned if out is None else jnp.where(lane >= 4 * f, turned, out)
    return out


def own_ends(dims, e_v, h_v, m_v, perm_ref, coef_v, packed):
    nx, ny, nz = dims
    lanes = nz // 128
    step = ny + HALO
    table = coef_table(perm_ref)
    lane = lax.broadcasted_iota(jnp.int32, (8, 128), 1)
    tiles = ny // 8

    def one(x, carry):
        for t in range(tiles):
            index = [
                pl.ds(pl.multiple_of(((x * tiles + t) * lanes + z) * 8, 8), 8) for z in range(lanes)
            ]
            for z in range(lanes):
                coef_v[index[z], :] = coef_of(m_v[index[z], :], table)

            def parts(f):
                if f < 3:
                    return e_v[f, index[0], :], e_v[f, index[-1], :]
                if f < 6:
                    return h_v[f - 3, index[0], :], h_v[f - 3, index[-1], :]
                return coef_v[index[0], :], coef_v[index[-1], :]

            packed[pl.ds(pl.multiple_of((x + 2) * step + t * 8, 8), 8), :] = turn_ends(parts, lane)
        return carry

    lax.fori_loop(0, nx, one, 0)


def unpack_faces(dims, sizes, own_packed, *refs):
    nx, ny, nz = dims
    lanes = nz // 128
    tiles = ny // 8
    step = ny + HALO
    gx, gy = lax.axis_index("gx"), lax.axis_index("gy")
    xs, ys = swaps(sizes[0]), swaps(sizes[1])
    n_msgs = len(xs) + len(ys) + len(xs) * len(ys)
    msgs = refs[:n_msgs]
    xh, yh, up_ref, down_ref, packed = refs[n_msgs:]
    if len(xs) < 2:
        xh[...] = jnp.zeros(xh.shape, jnp.float32)
    for f in range(FIELDS):
        for z in range(lanes):
            if len(ys) < 2:
                yh[f, z] = jnp.zeros(yh.shape[2:], jnp.float32)
            else:
                for p in (0, 1, nx + 2, nx + 3):
                    yh[f, z, pl.ds(p * HALO, HALO), :] = jnp.zeros((HALO, 128), jnp.float32)

    def planes(odd):
        high = sends_up(gx, odd)
        return jnp.where(high, 2, 1), jnp.where(high, 3, 0)

    def lines(odd):
        high = sends_up(gy, odd)
        return jnp.where(high, 0, HALO - 1), jnp.where(high, 1, HALO - 2)

    at = 0
    for odd in xs:
        ok = has_partner(gx, sizes[0], odd)
        place = planes(odd)
        for k, (f, far) in enumerate(slots(0)):
            for z in range(lanes):
                for t in range(tiles):
                    xh[f, z, pl.ds(pl.multiple_of(place[far] * ny + t * 8, 8), 8), :] = jnp.where(
                        ok, msgs[at][k, pl.ds((t * lanes + z) * 8, 8), :], 0.0
                    )
        at += 1
    for odd in ys:
        ok = has_partner(gy, sizes[1], odd)
        place = lines(odd)
        for k, (f, far) in enumerate(slots(1)):
            for z in range(lanes):
                yh[f, z, pl.ds(2 * HALO + place[far], nx, stride=HALO), :] = jnp.where(
                    ok, msgs[at][k, z], 0.0
                )
        at += 1
    for ox in xs:
        for oy in ys:
            ok = has_partner(gx, sizes[0], ox) & has_partner(gy, sizes[1], oy)
            px, py = planes(ox), lines(oy)
            px = [jnp.where(q < 2, q, q + nx) for q in px]
            for z in range(lanes):
                for f in range(FIELDS):
                    for k in range(4):
                        yh[f, z, pl.ds(px[k // 2] * HALO + py[k % 2], 1), :] = jnp.where(
                            ok, msgs[at][z, pl.ds(4 * f + k, 1), :], 0.0
                        )
            at += 1

    lane = lax.broadcasted_iota(jnp.int32, (8, 128), 1)

    def one(p, carry):
        index = pl.ds(pl.multiple_of(p * HALO, 8), HALO)
        packed[pl.ds(pl.multiple_of(p * step + ny, 8), HALO), :] = turn_ends(
            lambda f: (yh[f, 0, index, :], yh[f, lanes - 1, index, :]), lane
        )
        return carry

    lax.fori_loop(0, nx + 4, one, 0, unroll=2)
    for q, p in enumerate((0, 1, nx + 2, nx + 3)):
        for t in range(tiles):
            index = pl.ds(q * ny + t * 8, 8)
            packed[pl.ds(p * step + t * 8, 8), :] = turn_ends(
                lambda f: (xh[f, 0, index, :], xh[f, lanes - 1, index, :]), lane
            )
    for x in range(nx):
        index = pl.ds((x + 2) * step, ny)
        packed[index, :] = own_packed[index, :]
    total = (nx + 4) * step
    padded = packed.shape[0]
    if padded > total:
        packed[total:padded, :] = jnp.zeros((padded - total, 128), jnp.float32)
    for b in range(padded // 128):
        here = pl.ds(b * 128, 128)
        block = jnp.transpose(packed[here, :])
        for f in range(FIELDS):
            up_ref[f : f + 1, here] = block[4 * f + 1 : 4 * f + 2, :]
            up_ref[8 + f : 9 + f, here] = block[4 * f : 4 * f + 1, :]
            down_ref[f : f + 1, here] = block[4 * f + 2 : 4 * f + 3, :]
            down_ref[8 + f : 9 + f, here] = block[4 * f + 3 : 4 * f + 4, :]
    for row in (7, 15):
        up_ref[row : row + 1, :] = jnp.zeros((1, padded), jnp.float32)
        down_ref[row : row + 1, :] = jnp.zeros((1, padded), jnp.float32)


def march(
    dims,
    sizes,
    e_v,
    h_v,
    coef_v,
    xh,
    yh,
    low_ref,
    high_ref,
    snap_ref,
    mask_ref,
    ports_ref,
    amps_ref,
    *refs,
):
    nx, ny, nz = dims
    lanes = nz // 128
    tiles = ny // 8
    plane = ny * lanes
    step = ny + HALO
    wide = nz + 128
    parts = sizes[2]
    e_out, h_out = refs[0], refs[1]
    grads = refs[2 : 2 + parts]
    (ends, rows_ref, e1, h1, h2, half_ref, struck, sums, turned, e_s, h_s, sems) = refs[2 + parts :]
    gx, gy, gz = lax.axis_index("gx"), lax.axis_index("gy"), lax.axis_index("gz")
    padded = rows_ref.shape[1]

    low_ok, high_ok = gz > 0, gz < sizes[2] - 1
    for f in range(FIELDS):
        rows_ref[4 * f : 4 * f + 1, :] = jnp.where(low_ok, low_ref[8 + f : 9 + f, :], 0.0)
        rows_ref[4 * f + 1 : 4 * f + 2, :] = jnp.where(low_ok, low_ref[f : f + 1, :], 0.0)
        rows_ref[4 * f + 2 : 4 * f + 3, :] = jnp.where(high_ok, high_ref[f : f + 1, :], 0.0)
        rows_ref[4 * f + 3 : 4 * f + 4, :] = jnp.where(high_ok, high_ref[8 + f : 9 + f, :], 0.0)
    rows_ref[4 * FIELDS :, :] = jnp.zeros((128 - 4 * FIELDS, padded), jnp.float32)
    for b in range(padded // 128):
        block = jnp.transpose(rows_ref[:, b * 128 : (b + 1) * 128])
        for f in range(FIELDS):
            ends[f, b * 128 : (b + 1) * 128, :] = pltpu.roll(block, 128 - (4 * f + 2), 1)

    row = lax.broadcasted_iota(jnp.int32, (step, wide), 0)
    lane = lax.broadcasted_iota(jnp.int32, (step, wide), 1)
    inside = (
        ((row < ny) | ((row < ny + 2) & (gy < sizes[1] - 1)) | ((row >= ny + 4) & (gy > 0)))
        & ((lane < nz) | ((lane < nz + 64) & high_ok) | ((lane >= nz + 64) & low_ok))
    )
    half_ref[...] = jnp.where(inside, magnetic_step, 0.0)

    plane_cells = (ny * sizes[1]) * (nz * sizes[2])
    line_cells = nz * sizes[2]
    planes_struck = []
    for q in range(ports_ref.shape[0]):
        cell = ports_ref[q]
        sx = lax.div(cell, plane_cells) - gx * nx
        sy = lax.rem(lax.div(cell, line_cells), ny * sizes[1]) - gy * ny
        sz = lax.rem(cell, line_cells) - gz * nz
        near = (sy >= -2) & (sy < ny + 2) & (sz >= -2) & (sz < nz + 2)
        sy = jnp.where(sy < 0, sy + step, sy)
        sz = jnp.where(sz < 0, sz + wide, sz)
        struck[q] = jnp.where((row == sy) & (lane == sz) & near, 1.0, 0.0)
        planes_struck.append(sx + 2)

    def sources(p, s, rows, columns):
        total = None
        for q, at in enumerate(planes_struck):
            one = struck[q, 0:rows, 0:columns] * jnp.where(at == p, amps_ref[s, q], 0.0)
            total = one if total is None else total + one
        return total

    def spot(x, t, z):
        index = ((x * tiles + t) * lanes + z) * 8
        return pl.ds(index if isinstance(index, int) else pl.multiple_of(index, 8), 8)

    def own_tile(f, p, t, z):
        if isinstance(p, int) and not 2 <= p < nx + 2:
            return xh[f, z, pl.ds((p if p < 2 else p - nx) * ny + t * 8, 8), :]
        if f < 3:
            return e_v[f, spot(p - 2, t, z), :]
        if f < 6:
            return h_v[f - 3, spot(p - 2, t, z), :]
        return coef_v[spot(p - 2, t, z), :]

    def aligned(index):
        return index if isinstance(index, int) else pl.multiple_of(index, 8)

    def load(f, p):
        columns = []
        for z in range(lanes):
            column = [own_tile(f, p, t, z) for t in range(tiles)]
            column.append(yh[f, z, pl.ds(aligned(p * HALO), HALO), :])
            columns.append(jnp.concatenate(column, axis=0))
        columns.append(ends[f, pl.ds(aligned(p * step), step), :])
        return jnp.concatenate(columns, axis=1)

    def load_own(f, p):
        return jnp.concatenate(
            [
                jnp.concatenate([own_tile(f, p, t, z) for t in range(tiles)], axis=0)
                for z in range(lanes)
            ],
            axis=1,
        )

    def put(ref, f, x, v):
        for t in range(tiles):
            for z in range(lanes):
                ref[f, spot(x, t, z), :] = v[t * 8 : t * 8 + 8, z * 128 : z * 128 + 128]

    def y_up(v):
        return pltpu.roll(v, step - 1, 0)

    def y_down(v):
        return pltpu.roll(v, 1, 0)

    def z_up(v):
        return pltpu.roll(v, wide - 1, 1)

    def z_down(v):
        return pltpu.roll(v, 1, 1)

    def new_h(half, ex, ey, ez, ey_x, ez_x, hx, hy, hz):
        cx = (y_up(ez) - ez) - (z_up(ey) - ey)
        cy = (z_up(ex) - ex) - (ez_x - ez)
        cz = (ey_x - ey) - (y_up(ex) - ex)
        return hx - half * cx, hy - half * cy, hz - half * cz

    def curl_h(hx, hy, hz, hy_x, hz_x):
        cx = (hz - y_down(hz)) - (hy - z_down(hy))
        cy = (hx - z_down(hx)) - (hz - hz_x)
        cz = (hy - hy_x) - (hx - y_down(hx))
        return cx, cy, cz

    def half_of(p):
        if isinstance(p, int) and p < 2:
            return half_ref[...] * jnp.where(gx == 0, 0.0, 1.0)
        if isinstance(p, int) and p >= nx + 2:
            return half_ref[...] * jnp.where(gx == sizes[0] - 1, 0.0, 1.0)
        return half_ref[...]

    def first_h(p):
        e = [load(f, p) for f in range(3)]
        h = [load(3 + f, p) for f in range(3)]
        out = new_h(half_of(p), *e, load(1, p + 1), load(2, p + 1), *h)
        for f in range(3):
            h1[f, p] = out[f]

    def first_e(p):
        e = [load(f, p) for f in range(3)]
        curl = curl_h(*[h1[f, p] for f in range(3)], h1[1, p - 1], h1[2, p - 1])
        coef = load(6, p)
        out = [e[f] + coef * curl[f] for f in range(3)]
        out[2] = out[2] + sources(p, 0, step, wide)
        for f in range(3):
            e1[f, p] = out[f]

    def second_h(p):
        e = [e1[f, p] for f in range(3)]
        h = [h1[f, p] for f in range(3)]
        out = new_h(half_of(p), *e, e1[1, p + 1], e1[2, p + 1], *h)
        for f in range(3):
            h2[f, p] = out[f]

    def second_e(p):
        h = [h2[f, p] for f in range(3)]
        curl = curl_h(*h, h2[1, p - 1], h2[2, p - 1])
        coef = load_own(6, p)
        old = [e1[f, p, 0:ny, 0:nz] for f in range(3)]
        new = [old[f] + coef * curl[f][:ny, :nz] for f in range(3)]
        new[2] = new[2] + sources(p, 1, ny, nz)
        x = p - 2
        index = pl.ds(aligned(x * ny), ny)
        total = None
        for f in range(3):
            put(e_s, f, x, new[f])
            put(h_s, f, x, h[f][:ny, :nz])
            s = [snap_ref[t, f, index, :].astype(jnp.float32) for t in range(STEPS + 1)]
            one = old[f] * (s[0] - s[1]) + new[f] * (s[1] - s[2])
            total = one if total is None else total + one
        folded = total[:, 0:128]
        for at in range(128, nz, 128):
            folded = folded + total[:, at : at + 128]
        sums[index, :] = folded

    def one(p):
        dynamic = not isinstance(p, int)
        if dynamic or 2 <= p - 4 <= nx + 1:
            second_e(p - 4)
        if dynamic or 1 <= p - 3 <= nx + 1:
            second_h(p - 3)
        if dynamic or 1 <= p - 1 <= nx + 2:
            first_e(p - 1)
        if dynamic or 0 <= p <= nx + 2:
            first_h(p)

    def body(p, carry):
        one(p)
        return carry

    for p in range(6):
        one(p)
    chunk = nx // 4
    copies = []
    for c in range(4):
        lax.fori_loop(6 + c * chunk, min(6 + (c + 1) * chunk, nx + 1), body, 0)
        if c == 3:
            for p in range(nx + 1, nx + 6):
                one(p)
        here = pl.ds(c * chunk * plane, chunk * plane)
        for k, (src, dst) in enumerate(((e_s, e_out), (h_s, h_out))):
            copy = pltpu.make_async_copy(src.at[:, here], dst.at[:, here], sems.at[2 * c + k])
            copy.start()
            copies.append(copy)

    cells = nx * ny
    nt = (((1,), (1,)), ((), ()))
    nn = (((1,), (0,)), ((), ()))
    lined = lax.dot_general(jnp.ones((8, 128), jnp.float32), sums[...], nt, precision=HIGHEST)
    spread = jnp.where(
        lax.rem(lax.broadcasted_iota(jnp.int32, (ny, cells), 1), ny)
        == lax.broadcasted_iota(jnp.int32, (ny, cells), 0),
        lined[0:1, :],
        0.0,
    )
    pick = (
        lax.div(lax.broadcasted_iota(jnp.int32, (cells, nx), 0), ny)
        == lax.broadcasted_iota(jnp.int32, (cells, nx), 1)
    ).astype(jnp.float32)
    turned[...] = lax.dot_general(spread, pick, nn, precision=HIGHEST) * mask_ref[...].astype(
        jnp.float32
    )
    width = ny // parts
    for shift in range(parts):
        owner = lax.rem(gz + shift, parts)
        grads[shift][...] = turned[pl.ds(owner * width, width), :]
    for copy in copies:
        copy.wait()


def params(limit=12):
    return pltpu.CompilerParams(vmem_limit_bytes=limit * 1024 * 1024)


def body(sizes, e_adjoint, h_adjoint, snapshots, material, permittivity, design_mask, ports, amplitudes):
    dims = material.shape
    nx, ny, nz = dims
    lanes = nz // 128
    step = ny + HALO
    total = (nx + 4) * step
    padded = -(-total // 128) * 128
    f32 = jnp.float32
    cells = nx * ny
    e = in_hbm(tiled(e_adjoint))
    h = in_hbm(tiled(h_adjoint))
    m = in_hbm(tiled(material))
    s = in_vmem(snapshots.reshape(STEPS + 1, 3, cells, nz))
    xs, ys = swaps(sizes[0]), swaps(sizes[1])

    block, cube = jax.ShapeDtypeStruct, pltpu.VMEM
    shapes = [block((len(slots(0)), ny * lanes, 128), f32) for _ in xs]
    shapes += [block((len(slots(1)), lanes, nx, 128), f32) for _ in ys]
    shapes += [block((lanes, 4 * FIELDS, 128), f32) for _ in xs for _ in ys]
    e_v, h_v, m_v, *msgs = pl.pallas_call(
        functools.partial(load_faces, dims, sizes),
        out_shape=[cube(e.shape, f32), cube(h.shape, f32), cube(m.shape, jnp.int32)] + shapes,
        in_specs=[HBM, HBM, HBM, SM],
        out_specs=[VM] * (3 + len(shapes)),
        scratch_shapes=[pltpu.SemaphoreType.DMA((FIELDS,))],
        compiler_params=params(),
        name="load_faces",
    )(e, h, m, permittivity)
    coef_v, own_packed = pl.pallas_call(
        functools.partial(own_ends, dims),
        out_shape=[cube(m.shape, f32), cube((padded, 128), f32)],
        in_specs=[VM, VM, VM, SM],
        out_specs=[VM] * 2,
        compiler_params=params(),
        cost_estimate=pl.CostEstimate(flops=10**7, bytes_accessed=4 * 10**6, transcendentals=0),
        name="own_ends",
    )(e_v, h_v, m_v, permittivity)

    both = ("gx", "gy")
    tables = [("gx", list(enumerate(swap_table(sizes[0], o)))) for o in xs]
    tables += [("gy", list(enumerate(swap_table(sizes[1], o)))) for o in ys]
    for ox in xs:
        for oy in ys:
            tx, ty = swap_table(sizes[0], ox), swap_table(sizes[1], oy)
            pairs = [
                (x * sizes[1] + y, tx[x] * sizes[1] + ty[y])
                for x in range(sizes[0])
                for y in range(sizes[1])
            ]
            tables.append((both, pairs))
    got = [lax.ppermute(msg, axis, pairs) for msg, (axis, pairs) in zip(msgs, tables)]

    xh, yh, up, down = pl.pallas_call(
        functools.partial(unpack_faces, dims, sizes),
        out_shape=[
            cube((FIELDS, lanes, 4 * ny, 128), f32),
            cube((FIELDS, lanes, (nx + 4) * HALO, 128), f32),
            block((16, padded), f32),
            block((16, padded), f32),
        ],
        in_specs=[VM] * (1 + len(got)),
        out_specs=[VM] * 4,
        scratch_shapes=[pltpu.VMEM((padded, 128), f32)],
        compiler_params=params(),
        name="unpack_faces",
    )(own_packed, *got)

    parts = sizes[2]
    low = lax.ppermute(up, "gz", [(i, (i + 1) % parts) for i in range(parts)])
    high = lax.ppermute(down, "gz", [(i, (i - 1) % parts) for i in range(parts)])

    wide = nz + 128
    ported = ports.shape[0]
    out = pl.pallas_call(
        functools.partial(march, dims, sizes),
        out_shape=[block(e.shape, f32), block(h.shape, f32)]
        + [block((ny // parts, nx), f32)] * parts,
        in_specs=[VM] * 9 + [SM, SM],
        out_specs=[ANY, ANY] + [VM] * parts,
        scratch_shapes=[
            pltpu.VMEM((FIELDS, padded, 128), f32),
            pltpu.VMEM((128, padded), f32),
            pltpu.VMEM((3, nx + 4, step, wide), f32),
            pltpu.VMEM((3, nx + 4, step, wide), f32),
            pltpu.VMEM((3, nx + 4, step, wide), f32),
            pltpu.VMEM((step, wide), f32),
            pltpu.VMEM((ported, step, wide), f32),
            pltpu.VMEM((cells, 128), f32),
            pltpu.VMEM((ny, nx), f32),
            pltpu.VMEM(e.shape, f32),
            pltpu.VMEM(h.shape, f32),
            pltpu.SemaphoreType.DMA((8,)),
        ],
        compiler_params=params(32),
        name="march",
    )(e_v, h_v, coef_v, xh, yh, low, high, s, design_mask.T, ports, amplitudes)
    gradient = out[2]
    for shift in range(1, parts):
        gradient = gradient + lax.ppermute(
            out[2 + shift], "gz", [(i, (i + shift) % parts) for i in range(parts)]
        )
    return untiled(out[0], dims), untiled(out[1], dims), gradient.T


def solution(mesh):
    placed = (
        P(None, "gx", "gy", "gz"),
        P(None, "gx", "gy", "gz"),
        P(None, None, "gx", "gy", "gz"),
        P("gx", "gy", "gz"),
        P(),
        P("gx", "gy"),
        P(),
        P(),
    )
    sizes = tuple(mesh.shape[axis] for axis in ("gx", "gy", "gz"))
    return jax.shard_map(
        functools.partial(body, sizes),
        mesh=mesh,
        in_specs=placed,
        out_specs=(P(None, "gx", "gy", "gz"), P(None, "gx", "gy", "gz"), P("gx", ("gy", "gz"))),
        check_vma=False,
    )
```

```python
import functools

import jax
import jax.numpy as jnp
from jax import lax
from jax.experimental import pallas as pl
from jax.experimental.pallas import tpu as pltpu
from jax.sharding import PartitionSpec as P

STEPS = 2
FIELDS = 7
HALO = 8
HIGHEST = lax.Precision.HIGHEST

magnetic_step = 0.5
electric_step = 0.5

VM = pl.BlockSpec(memory_space=pltpu.VMEM)
SM = pl.BlockSpec(memory_space=pltpu.SMEM)
ANY = pl.BlockSpec(memory_space=pl.ANY)


HBM = pl.BlockSpec(memory_space=pltpu.HBM)


def in_hbm(array):
    return pltpu.with_memory_space_constraint(array, pltpu.HBM)


def in_vmem(array):
    return pltpu.with_memory_space_constraint(array, pltpu.VMEM)


def swap_table(size, odd):
    table = list(range(size))
    for i in range(odd, size - 1, 2):
        table[i], table[i + 1] = i + 1, i
    return table


def swaps(size):
    return [odd for odd in (0, 1) if odd + 1 < size]


def sends_up(index, odd):
    return lax.rem(index, 2) == odd


def has_partner(index, size, odd):
    up = sends_up(index, odd)
    return (up & (index + 1 < size)) | (jnp.logical_not(up) & (index >= 1))


def coef_table(perm_ref):
    return [
        electric_step / jnp.full((1, 1), perm_ref[i], jnp.float32) for i in range(perm_ref.shape[0])
    ]


def coef_of(material, table):
    out = jnp.zeros(material.shape, jnp.float32)
    for i, value in enumerate(table):
        out = jnp.where(material == i, value, out)
    return out


def tiled(array):
    *lead, nx, ny, nz = array.shape
    n = len(lead)
    split = array.reshape(*lead, nx, ny // 8, 8, nz // 128, 128)
    order = tuple(range(n + 2)) + (n + 3, n + 2, n + 4)
    return split.transpose(order).reshape(*lead, nx * ny * nz // 128, 128)


def untiled(array, dims):
    nx, ny, nz = dims
    lead = array.shape[:-2]
    n = len(lead)
    split = array.reshape(*lead, nx, ny // 8, nz // 128, 8, 128)
    order = tuple(range(n + 2)) + (n + 3, n + 2, n + 4)
    return split.transpose(order).reshape(*lead, nx, ny, nz)


def tiles_of(array):
    *lead, nx, ny, nz = array.shape
    return tiled(array).reshape(*lead, nx, ny // 8, nz // 128, 8, 128)


def send_faces(dims, sizes, e_ref, h_ref, m_ref, perm_ref, *refs):
    nx, ny, nz = dims
    lanes = nz // 128
    tiles = ny // 8
    plane = ny * lanes
    gx, gy = lax.axis_index("gx"), lax.axis_index("gy")
    xs, ys = swaps(sizes[0]), swaps(sizes[1])
    n_out = len(xs) + len(ys) + len(xs) * len(ys)
    outs, refs = refs[:n_out], refs[n_out:]
    x_bufs, refs = refs[: 2 * len(xs)], refs[2 * len(xs) :]
    y_bufs, sems = refs[: 2 * len(ys)], refs[2 * len(ys)]

    def source(f):
        return e_ref.at[f] if f < 3 else h_ref.at[f - 3] if f < 6 else m_ref

    copies = []

    def start(src, dst):
        copy = pltpu.make_async_copy(src, dst, sems.at[len(copies)])
        copy.start()
        copies.append(copy)

    for i, odd in enumerate(ys):
        up = sends_up(gy, odd)
        t, r = jnp.where(up, tiles - 1, 0), jnp.where(up, 6, 0)
        for f in range(FIELDS):
            buf = y_bufs[2 * i].at[f] if f < 6 else y_bufs[2 * i + 1]
            for z in range(lanes):
                start(
                    source(f).at[:, t, z, pl.ds(r, 2), :],
                    buf.at[z].reshape(nx, 8, 128).at[:, pl.ds(0, 2), :],
                )
    for i, odd in enumerate(xs):
        first = jnp.where(sends_up(gx, odd), nx - 2, 0)
        for f in range(FIELDS):
            start(source(f).at[pl.ds(first, 2)], x_bufs[2 * i].at[f] if f < 6 else x_bufs[2 * i + 1])

    table = coef_table(perm_ref)
    lane = lax.broadcasted_iota(jnp.int32, (8, 128), 1)
    lane_n = lax.broadcasted_iota(jnp.int32, (nx, 128), 1)

    def z_up(v, lane):
        out = []
        for z in range(lanes):
            after = pltpu.roll(v[z + 1], 127, 1) if z + 1 < lanes else jnp.zeros_like(v[z])
            out.append(jnp.where(lane < 127, pltpu.roll(v[z], 127, 1), after))
        return out

    def row_up(v):
        rows = v.shape[0]
        row = lax.broadcasted_iota(jnp.int32, v.shape, 0)
        return jnp.where(row < rows - 1, pltpu.roll(v, rows - 1, 0), 0.0)

    done = 0
    for i, odd in enumerate(ys):
        for copy in copies[done : done + FIELDS * lanes]:
            copy.wait()
        done += FIELDS * lanes
        up = sends_up(gy, odd)
        near, far = jnp.where(up, 1, 0), jnp.where(up, 0, 1)
        down = jnp.where(up, 0.0, magnetic_step)
        buf, mat, out = y_bufs[2 * i], y_bufs[2 * i + 1], outs[len(xs) + i]

        def at(f, which):
            return [buf[f, z, pl.ds(which, nx, stride=8), :] for z in range(lanes)]

        ex_f, ey_f, ez_f = (at(f, far) for f in range(3))
        hx_f, hz_f = at(3, far), at(5, far)
        hx_n, hz_n = at(3, near), at(5, near)
        ey_z = z_up(ey_f, lane_n)
        for z in range(lanes):
            for f in range(3):
                out[f * lanes + z] = buf[f, z, pl.ds(near, nx, stride=8), :]
            out[3 * lanes + z] = hx_n[z] - down * ez_f[z]
            out[4 * lanes + z] = buf[4, z, pl.ds(near, nx, stride=8), :]
            out[5 * lanes + z] = hz_n[z] + down * ex_f[z]
            out[6 * lanes + z] = coef_of(mat[z, pl.ds(near, nx, stride=8), :], table)
            out[7 * lanes + z] = hx_f[z] + magnetic_step * (ez_f[z] + (ey_z[z] - ey_f[z]))
            out[8 * lanes + z] = hz_f[z] - magnetic_step * ((row_up(ey_f[z]) - ey_f[z]) + ex_f[z])
        out[9 * lanes] = ey_f[0]
    for i, odd in enumerate(xs):
        for copy in copies[done : done + FIELDS]:
            copy.wait()
        done += FIELDS
        up = sends_up(gx, odd)
        near, far = jnp.where(up, 1, 0), jnp.where(up, 0, 1)
        down = jnp.where(up, 0.0, magnetic_step)
        buf, mat, out = x_bufs[2 * i], x_bufs[2 * i + 1], outs[i]

        def put(k, t, z, v):
            out[pl.ds(k * plane + (t * lanes + z) * 8, 8), :] = v

        ex_y = [
            row_up(jnp.concatenate([buf[0, far, t, z] for t in range(tiles)], axis=0))
            for z in range(lanes)
        ]
        for t in range(tiles):
            ex_z = z_up([buf[0, far, t, z] for z in range(lanes)], lane)
            for z in range(lanes):
                ex_f, ey_f, ez_f = (buf[f, far, t, z] for f in range(3))
                for f in range(4):
                    put(f, t, z, buf[f, near, t, z])
                put(4, t, z, buf[4, near, t, z] + down * ez_f)
                put(5, t, z, buf[5, near, t, z] - down * ey_f)
                put(6, t, z, coef_of(mat[near, t, z], table))
                put(7, t, z, buf[4, far, t, z] - magnetic_step * ((ex_z[z] - ex_f) + ez_f))
                ex_up = ex_y[z][t * 8 : t * 8 + 8]
                put(8, t, z, buf[5, far, t, z] + magnetic_step * (ey_f + (ex_up - ex_f)))
            out[pl.ds(9 * plane + t * 8, 8), :] = buf[0, far, t, 0]
        for j, odd_y in enumerate(ys):
            up_y = sends_up(gy, odd_y)
            t = jnp.where(up_y, tiles - 1, 0)
            lines = (jnp.where(up_y, 7, 0), jnp.where(up_y, 6, 1))
            out = outs[len(xs) + len(ys) + i * len(ys) + j]
            for z in range(lanes):
                for f in range(FIELDS):
                    for k in range(4):
                        where = (near, far)[k // 2], t, z, pl.ds(lines[k % 2], 1)
                        if f < 6:
                            line = buf[(f, *where)]
                        else:
                            line = coef_of(mat[where], table)
                        out[z, pl.ds(4 * f + k, 1), :] = line


def turn_ends(parts, lane):
    out = None
    for f in range(FIELDS):
        first, last = parts(f)
        turned = pltpu.roll(jnp.where(lane < 64, first, last), 4 * f + 2, 1)
        out = turned if out is None else jnp.where(lane >= 4 * f, turned, out)
    return out


def turn_rows(packed, blocks, up_ref, down_ref, offset):
    for b in range(blocks):
        block = jnp.transpose(packed[b * 128 : (b + 1) * 128, :])
        here = pl.ds(offset + b * 128, 128)
        for f in range(FIELDS):
            up_ref[f : f + 1, here] = block[4 * f + 1 : 4 * f + 2, :]
            up_ref[8 + f : 9 + f, here] = block[4 * f : 4 * f + 1, :]
            down_ref[f : f + 1, here] = block[4 * f + 2 : 4 * f + 3, :]
            down_ref[8 + f : 9 + f, here] = block[4 * f + 3 : 4 * f + 4, :]
    for row in (7, 15):
        up_ref[row : row + 1, pl.ds(offset, blocks * 128)] = jnp.zeros((1, blocks * 128), jnp.float32)
        down_ref[row : row + 1, pl.ds(offset, blocks * 128)] = jnp.zeros((1, blocks * 128), jnp.float32)


def own_ends(dims, e_v, h_v, m_v, perm_ref, coef_v, up_ref, down_ref, packed):
    nx, ny, nz = dims
    lanes = nz // 128
    table = coef_table(perm_ref)
    lane = lax.broadcasted_iota(jnp.int32, (8, 128), 1)
    tiles = ny // 8

    def one(x, carry):
        for t in range(tiles):
            index = [
                pl.ds(pl.multiple_of(((x * tiles + t) * lanes + z) * 8, 8), 8) for z in range(lanes)
            ]
            for z in range(lanes):
                coef_v[index[z], :] = coef_of(m_v[index[z], :], table)

            def parts(f):
                if f < 3:
                    return e_v[f, index[0], :], e_v[f, index[-1], :]
                if f < 6:
                    return h_v[f - 3, index[0], :], h_v[f - 3, index[-1], :]
                return coef_v[index[0], :], coef_v[index[-1], :]

            packed[pl.ds(pl.multiple_of(x * ny + t * 8, 8), 8), :] = turn_ends(parts, lane)
        return carry

    lax.fori_loop(0, nx, one, 0)
    turn_rows(packed, nx * ny // 128, up_ref, down_ref, 0)


def unpack_faces(dims, sizes, own_up, own_down, *refs):
    nx, ny, nz = dims
    lanes = nz // 128
    tiles = ny // 8
    plane = ny * lanes
    cells = nx * ny
    gx, gy = lax.axis_index("gx"), lax.axis_index("gy")
    xs, ys = swaps(sizes[0]), swaps(sizes[1])
    n_msgs = len(xs) + len(ys) + len(xs) * len(ys)
    msgs = refs[:n_msgs]
    xh, yh, up_ref, down_ref, packed, x_raw, y_raw = refs[n_msgs:]
    xh[...] = jnp.zeros(xh.shape, jnp.float32)
    x_raw[...] = jnp.zeros(x_raw.shape, jnp.float32)
    y_raw[...] = jnp.zeros(y_raw.shape, jnp.float32)
    for f in range(FIELDS):
        for z in range(lanes):
            if len(ys) < 2 or f < 3:
                yh[f, z] = jnp.zeros(yh.shape[2:], jnp.float32)
            else:
                for p in (0, 1, nx + 2, nx + 3):
                    yh[f, z, pl.ds(p * HALO, HALO), :] = jnp.zeros((HALO, 128), jnp.float32)

    def planes(odd):
        high = sends_up(gx, odd)
        return jnp.where(high, 2, 1), jnp.where(high, 3, 0)

    def lines(odd):
        high = sends_up(gy, odd)
        return jnp.where(high, 0, HALO - 1), jnp.where(high, 1, HALO - 2)

    for i, odd in enumerate(xs):
        ok = has_partner(gx, sizes[0], odd)
        near, far = planes(odd)
        msg = msgs[i]
        for t in range(tiles):
            for z in range(lanes):
                for k, f in enumerate((0, 1, 2, 3, 4, 5, 6, 4, 5)):
                    q = near if k < FIELDS else far
                    xh[f, z, pl.ds(pl.multiple_of(q * ny + t * 8, 8), 8), :] = jnp.where(
                        ok, msg[pl.ds(k * plane + (t * lanes + z) * 8, 8), :], 0.0
                    )
            x_raw[pl.ds(pl.multiple_of(far * ny + t * 8, 8), 8), :] = jnp.where(
                ok & (far == 0), msg[pl.ds(9 * plane + t * 8, 8), :], 0.0
            )
    for i, odd in enumerate(ys):
        ok = has_partner(gy, sizes[1], odd)
        near, far = lines(odd)
        msg = msgs[len(xs) + i]
        for z in range(lanes):
            for k, f in enumerate((0, 1, 2, 3, 4, 5, 6, 3, 5)):
                r = near if k < FIELDS else far
                yh[f, z, pl.ds(2 * HALO + r, nx, stride=HALO), :] = jnp.where(
                    ok, msg[k * lanes + z], 0.0
                )
        y_raw[pl.ds(2 * HALO + far, nx, stride=HALO), :] = jnp.where(
            ok & (far == HALO - 2), msg[9 * lanes], 0.0
        )
    for i, ox in enumerate(xs):
        for j, oy in enumerate(ys):
            ok = has_partner(gx, sizes[0], ox) & has_partner(gy, sizes[1], oy)
            px, py = planes(ox), lines(oy)
            px = [jnp.where(q < 2, q, q + nx) for q in px]
            msg = msgs[len(xs) + len(ys) + i * len(ys) + j]
            for z in range(lanes):
                for f in range(FIELDS):
                    for k in range(4):
                        yh[f, z, pl.ds(px[k // 2] * HALO + py[k % 2], 1), :] = jnp.where(
                            ok, msg[z, pl.ds(4 * f + k, 1), :], 0.0
                        )

    lane = lax.broadcasted_iota(jnp.int32, (8, 128), 1)

    def one(p, carry):
        index = pl.ds(pl.multiple_of(p * HALO, 8), HALO)

        def parts(f):
            first = yh[f, 0, index, :]
            return first + y_raw[index, :] if f == 1 else first, yh[f, lanes - 1, index, :]

        packed[index, :] = turn_ends(parts, lane)
        return carry

    lax.fori_loop(0, nx + 4, one, 0, unroll=4)
    after = (nx + 4) * HALO
    for r in range(0, 4 * ny, 8):
        index = pl.ds(r, 8)

        def parts(f):
            first = xh[f, 0, index, :]
            return first + x_raw[index, :] if f == 0 else first, xh[f, lanes - 1, index, :]

        packed[pl.ds(after + r, 8), :] = turn_ends(parts, lane)
    after += 4 * ny
    if packed.shape[0] > after:
        packed[after:, :] = jnp.zeros((packed.shape[0] - after, 128), jnp.float32)
    up_ref[:, 0:cells] = own_up[...]
    down_ref[:, 0:cells] = own_down[...]
    turn_rows(packed, packed.shape[0] // 128, up_ref, down_ref, cells)


def march(
    dims,
    sizes,
    e_v,
    h_v,
    coef_v,
    xh,
    yh,
    low_ref,
    high_ref,
    snap_ref,
    mask_ref,
    ports_ref,
    amps_ref,
    *refs,
):
    nx, ny, nz = dims
    lanes = nz // 128
    tiles = ny // 8
    plane = ny * lanes
    cells = nx * ny
    step = ny + HALO
    wide = nz + 128
    parts = sizes[2]
    e_out, h_out = refs[0], refs[1]
    grads = refs[2 : 2 + parts]
    (ends, rows_ref, ends_t, e1, h1, h2, half_ref, struck, sums, turned, e_s, h_s, sems) = refs[
        2 + parts :
    ]
    gx, gy, gz = lax.axis_index("gx"), lax.axis_index("gy"), lax.axis_index("gz")
    padded = rows_ref.shape[1]

    low_ok, high_ok = gz > 0, gz < sizes[2] - 1
    for f in range(FIELDS):
        rows_ref[4 * f : 4 * f + 1, :] = jnp.where(low_ok, low_ref[8 + f : 9 + f, :], 0.0)
        rows_ref[4 * f + 1 : 4 * f + 2, :] = jnp.where(low_ok, low_ref[f : f + 1, :], 0.0)
        rows_ref[4 * f + 2 : 4 * f + 3, :] = jnp.where(high_ok, high_ref[f : f + 1, :], 0.0)
        rows_ref[4 * f + 3 : 4 * f + 4, :] = jnp.where(high_ok, high_ref[8 + f : 9 + f, :], 0.0)
    rows_ref[4 * FIELDS :, :] = jnp.zeros((128 - 4 * FIELDS, padded), jnp.float32)
    for b in range(padded // 128):
        ends_t[b * 128 : (b + 1) * 128, :] = jnp.transpose(rows_ref[:, b * 128 : (b + 1) * 128])

    row = lax.broadcasted_iota(jnp.int32, (step, wide), 0)
    lane = lax.broadcasted_iota(jnp.int32, (step, wide), 1)
    inside = (
        ((row < ny) | ((row < ny + 2) & (gy < sizes[1] - 1)) | ((row >= ny + 4) & (gy > 0)))
        & ((lane < nz) | ((lane < nz + 64) & high_ok) | ((lane >= nz + 64) & low_ok))
    )
    half_ref[...] = jnp.where(inside, magnetic_step, 0.0)

    plane_cells = (ny * sizes[1]) * (nz * sizes[2])
    line_cells = nz * sizes[2]
    planes_struck = []
    for q in range(ports_ref.shape[0]):
        cell = ports_ref[q]
        sx = lax.div(cell, plane_cells) - gx * nx
        sy = lax.rem(lax.div(cell, line_cells), ny * sizes[1]) - gy * ny
        sz = lax.rem(cell, line_cells) - gz * nz
        near = (sy >= -2) & (sy < ny + 2) & (sz >= -2) & (sz < nz + 2)
        sy = jnp.where(sy < 0, sy + step, sy)
        sz = jnp.where(sz < 0, sz + wide, sz)
        struck[q] = jnp.where((row == sy) & (lane == sz) & near, 1.0, 0.0)
        planes_struck.append(sx + 2)

    def spot(x, t, z):
        index = ((x * tiles + t) * lanes + z) * 8
        return pl.ds(index if isinstance(index, int) else pl.multiple_of(index, 8), 8)

    def own_tile(f, p, t, z):
        if isinstance(p, int) and not 2 <= p < nx + 2:
            return xh[f, z, pl.ds((p if p < 2 else p - nx) * ny + t * 8, 8), :]
        if f < 3:
            return e_v[f, spot(p - 2, t, z), :]
        if f < 6:
            return h_v[f - 3, spot(p - 2, t, z), :]
        return coef_v[spot(p - 2, t, z), :]

    def aligned(index):
        return index if isinstance(index, int) else pl.multiple_of(index, 8)

    def load(f, p):
        columns = []
        for z in range(lanes):
            column = [own_tile(f, p, t, z) for t in range(tiles)]
            column.append(yh[f, z, pl.ds(aligned(p * HALO), HALO), :])
            columns.append(jnp.concatenate(column, axis=0))
        columns.append(ends[f, p])
        return jnp.concatenate(columns, axis=1)

    def spread(p):
        if isinstance(p, int) and not 2 <= p < nx + 2:
            own = cells + (nx + 4) * HALO + (p if p < 2 else p - nx) * ny
        else:
            own = (p - 2) * ny
        rows = [own + t * 8 for t in range(tiles)] + [cells + p * HALO]
        for k, r in enumerate(rows):
            v = ends_t[pl.ds(aligned(r), 8), :]
            for f in range(FIELDS):
                ends[f, p, k * 8 : k * 8 + 8, :] = pltpu.roll(v, 128 - (4 * f + 2), 1)

    def load_own(f, p):
        return jnp.concatenate(
            [
                jnp.concatenate([own_tile(f, p, t, z) for t in range(tiles)], axis=0)
                for z in range(lanes)
            ],
            axis=1,
        )

    def put(ref, f, x, v):
        for t in range(tiles):
            for z in range(lanes):
                ref[f, spot(x, t, z), :] = v[t * 8 : t * 8 + 8, z * 128 : z * 128 + 128]

    def y_up(v):
        return pltpu.roll(v, step - 1, 0)

    def y_down(v):
        return pltpu.roll(v, 1, 0)

    def z_up(v):
        return pltpu.roll(v, wide - 1, 1)

    def z_down(v):
        return pltpu.roll(v, 1, 1)

    def new_h(half, ex, ey, ez, ey_x, ez_x, hx, hy, hz):
        cx = (y_up(ez) - ez) - (z_up(ey) - ey)
        cy = (z_up(ex) - ex) - (ez_x - ez)
        cz = (ey_x - ey) - (y_up(ex) - ex)
        return hx - half * cx, hy - half * cy, hz - half * cz

    def curl_h(hx, hy, hz, hy_x, hz_x):
        cx = (hz - y_down(hz)) - (hy - z_down(hy))
        cy = (hx - z_down(hx)) - (hz - hz_x)
        cz = (hy - hy_x) - (hx - y_down(hx))
        return cx, cy, cz

    def half_of(p):
        if isinstance(p, int) and p < 2:
            return half_ref[...] * jnp.where(gx == 0, 0.0, 1.0)
        if isinstance(p, int) and p >= nx + 2:
            return half_ref[...] * jnp.where(gx == sizes[0] - 1, 0.0, 1.0)
        return half_ref[...]

    def first_h(p):
        e = [load(f, p) for f in range(3)]
        h = [load(3 + f, p) for f in range(3)]
        out = new_h(half_of(p), *e, load(1, p + 1), load(2, p + 1), *h)
        for f in range(3):
            h1[f, p] = out[f]

    def first_e(p):
        e = [load(f, p) for f in range(3)]
        curl = curl_h(*[h1[f, p] for f in range(3)], h1[1, p - 1], h1[2, p - 1])
        coef = load(6, p)
        out = [e[f] + coef * curl[f] for f in range(3)]
        for f in range(3):
            e1[f, p] = out[f]

    def second_h(p):
        e = [e1[f, p] for f in range(3)]
        h = [h1[f, p] for f in range(3)]
        out = new_h(half_of(p), *e, e1[1, p + 1], e1[2, p + 1], *h)
        for f in range(3):
            h2[f, p] = out[f]

    def second_e(p):
        h = [h2[f, p] for f in range(3)]
        curl = curl_h(*h, h2[1, p - 1], h2[2, p - 1])
        coef = load_own(6, p)
        old = [e1[f, p, 0:ny, 0:nz] for f in range(3)]
        new = [old[f] + coef * curl[f][:ny, :nz] for f in range(3)]
        x = p - 2
        index = pl.ds(aligned(x * ny), ny)
        total = None
        for f in range(3):
            put(e_s, f, x, new[f])
            put(h_s, f, x, h[f][:ny, :nz])
            s = [snap_ref[t, f, index, :].astype(jnp.float32) for t in range(STEPS + 1)]
            one = old[f] * (s[0] - s[1]) + new[f] * (s[1] - s[2])
            total = one if total is None else total + one
        folded = total[:, 0:128]
        for at in range(128, nz, 128):
            folded = folded + total[:, at : at + 128]
        sums[index, :] = folded

    def strike(p):
        dynamic = not isinstance(p, int)
        first, second = p - 1, p - 4
        hit = None
        for at in planes_struck:
            here = (at == first) | (at == second)
            hit = here if hit is None else hit | here

        @pl.when(hit)
        def _():
            for q, at in enumerate(planes_struck):
                if dynamic or 1 <= first <= nx + 2:
                    amp = jnp.where(at == first, amps_ref[0, q], 0.0)
                    e1[2, first] = e1[2, first] + struck[q] * amp
                if dynamic or 2 <= second <= nx + 1:
                    x = second - 2
                    amp = jnp.where(at == second, amps_ref[1, q], 0.0)
                    index = pl.ds(aligned(x * ny), ny)
                    s = [snap_ref[t, 2, index, :].astype(jnp.float32) for t in (1, 2)]
                    folded = jnp.zeros((ny, 128), jnp.float32)
                    for z in range(lanes):
                        gain = struck[q, 0:ny, z * 128 : z * 128 + 128] * amp
                        folded = folded + gain * (s[0] - s[1])[:, z * 128 : z * 128 + 128]
                        for t in range(tiles):
                            here = spot(x, t, z)
                            e_s[2, here, :] = e_s[2, here, :] + gain[t * 8 : t * 8 + 8]
                    sums[index, :] = sums[index, :] + folded

    def one(p):
        dynamic = not isinstance(p, int)
        if dynamic or 2 <= p - 4 <= nx + 1:
            second_e(p - 4)
        if dynamic or 1 <= p - 3 <= nx + 1:
            second_h(p - 3)
        if dynamic or 1 <= p - 1 <= nx + 2:
            first_e(p - 1)
        if dynamic or 0 <= p <= nx + 2:
            first_h(p)
        if dynamic or p + 2 <= nx + 3:
            spread(p + 2)
        strike(p)

    def body(p, carry):
        one(p)
        return carry

    spread(0)
    spread(1)
    for p in range(6):
        one(p)
    chunk = nx // 4
    copies = []
    for c in range(4):
        lax.fori_loop(6 + c * chunk, min(6 + (c + 1) * chunk, nx), body, 0)
        if c == 3:
            for p in range(nx, nx + 6):
                one(p)
        here = pl.ds(c * chunk * plane, chunk * plane)
        for k, (src, dst) in enumerate(((e_s, e_out), (h_s, h_out))):
            copy = pltpu.make_async_copy(src.at[:, here], dst.at[:, here], sems.at[2 * c + k])
            copy.start()
            copies.append(copy)

    nt = (((1,), (1,)), ((), ()))
    nn = (((1,), (0,)), ((), ()))
    lined = lax.dot_general(jnp.ones((8, 128), jnp.float32), sums[...], nt, precision=HIGHEST)
    spread = jnp.where(
        lax.rem(lax.broadcasted_iota(jnp.int32, (ny, cells), 1), ny)
        == lax.broadcasted_iota(jnp.int32, (ny, cells), 0),
        lined[0:1, :],
        0.0,
    )
    pick = (
        lax.div(lax.broadcasted_iota(jnp.int32, (cells, nx), 0), ny)
        == lax.broadcasted_iota(jnp.int32, (cells, nx), 1)
    ).astype(jnp.float32)
    turned[...] = lax.dot_general(spread, pick, nn, precision=HIGHEST) * mask_ref[...].astype(
        jnp.float32
    )
    width = ny // parts
    for shift in range(parts):
        owner = lax.rem(gz + shift, parts)
        grads[shift][...] = turned[pl.ds(owner * width, width), :]
    for copy in copies:
        copy.wait()


def params(limit=12):
    return pltpu.CompilerParams(vmem_limit_bytes=limit * 1024 * 1024)


def body(sizes, e_adjoint, h_adjoint, snapshots, material, permittivity, design_mask, ports, amplitudes):
    permittivity = in_hbm(permittivity)
    permittivity = in_hbm(permittivity)
    dims = material.shape
    nx, ny, nz = dims
    lanes = nz // 128
    tiles = ny // 8
    plane = ny * lanes
    cells = nx * ny
    step = ny + HALO
    edge = -(-((nx + 4) * HALO + 4 * ny) // 128) * 128
    padded = cells + edge
    f32, i32 = jnp.float32, jnp.int32
    xs, ys = swaps(sizes[0]), swaps(sizes[1])
    block, cube = jax.ShapeDtypeStruct, pltpu.VMEM

    shapes = [block((9 * plane + ny, 128), f32) for _ in xs]
    shapes += [block((9 * lanes + 1, nx, 128), f32) for _ in ys]
    shapes += [block((lanes, 4 * FIELDS, 128), f32) for _ in xs for _ in ys]
    buffers = []
    for _ in xs:
        buffers += [cube((6, 2, tiles, lanes, 8, 128), f32), cube((2, tiles, lanes, 8, 128), i32)]
    for _ in ys:
        buffers += [cube((6, lanes, nx * 8, 128), f32), cube((lanes, nx * 8, 128), i32)]
    n_copies = FIELDS * (len(xs) + lanes * len(ys))
    msgs = pl.pallas_call(
        functools.partial(send_faces, dims, sizes),
        out_shape=shapes,
        in_specs=[HBM, HBM, HBM, SM],
        out_specs=[VM] * len(shapes),
        scratch_shapes=buffers + [pltpu.SemaphoreType.DMA((n_copies,))],
        compiler_params=params(),
        name="send_faces",
    )(
        in_hbm(tiles_of(e_adjoint)),
        in_hbm(tiles_of(h_adjoint)),
        in_hbm(tiles_of(material)),
        permittivity,
    )
    e_v, h_v, m_v = in_vmem(tiled(e_adjoint)), in_vmem(tiled(h_adjoint)), in_vmem(tiled(material))
    s = in_vmem(snapshots.reshape(STEPS + 1, 3, cells, nz))
    coef_v, own_up, own_down = pl.pallas_call(
        functools.partial(own_ends, dims),
        out_shape=[cube(m_v.shape, f32), cube((16, cells), f32), cube((16, cells), f32)],
        in_specs=[VM, VM, VM, SM],
        out_specs=[VM] * 3,
        scratch_shapes=[pltpu.VMEM((cells, 128), f32)],
        compiler_params=params(),
        cost_estimate=pl.CostEstimate(flops=10**7, bytes_accessed=4 * 10**6, transcendentals=0),
        name="own_ends",
    )(e_v, h_v, m_v, permittivity)

    both = ("gx", "gy")
    tables = [("gx", list(enumerate(swap_table(sizes[0], o)))) for o in xs]
    tables += [("gy", list(enumerate(swap_table(sizes[1], o)))) for o in ys]
    for ox in xs:
        for oy in ys:
            tx, ty = swap_table(sizes[0], ox), swap_table(sizes[1], oy)
            pairs = [
                (x * sizes[1] + y, tx[x] * sizes[1] + ty[y])
                for x in range(sizes[0])
                for y in range(sizes[1])
            ]
            tables.append((both, pairs))
    got = [lax.ppermute(msg, axis, pairs) for msg, (axis, pairs) in zip(msgs, tables)]

    xh, yh, up, down = pl.pallas_call(
        functools.partial(unpack_faces, dims, sizes),
        out_shape=[
            cube((FIELDS, lanes, 4 * ny, 128), f32),
            cube((FIELDS, lanes, (nx + 4) * HALO, 128), f32),
            block((16, padded), f32),
            block((16, padded), f32),
        ],
        in_specs=[VM] * (2 + len(got)),
        out_specs=[VM] * 4,
        scratch_shapes=[
            pltpu.VMEM((edge, 128), f32),
            pltpu.VMEM((4 * ny, 128), f32),
            pltpu.VMEM(((nx + 4) * HALO, 128), f32),
        ],
        compiler_params=params(),
        name="unpack_faces",
    )(own_up, own_down, *got)

    parts = sizes[2]
    low = lax.ppermute(up, "gz", [(i, (i + 1) % parts) for i in range(parts)])
    high = lax.ppermute(down, "gz", [(i, (i - 1) % parts) for i in range(parts)])

    wide = nz + 128
    ported = ports.shape[0]
    out = pl.pallas_call(
        functools.partial(march, dims, sizes),
        out_shape=[block(e_v.shape, f32), block(h_v.shape, f32)]
        + [block((ny // parts, nx), f32)] * parts,
        in_specs=[VM] * 9 + [SM, SM],
        out_specs=[ANY, ANY] + [VM] * parts,
        scratch_shapes=[
            pltpu.VMEM((FIELDS, nx + 4, step, 128), f32),
            pltpu.VMEM((128, padded), f32),
            pltpu.VMEM((padded, 128), f32),
            pltpu.VMEM((3, nx + 4, step, wide), f32),
            pltpu.VMEM((3, nx + 4, step, wide), f32),
            pltpu.VMEM((3, nx + 4, step, wide), f32),
            pltpu.VMEM((step, wide), f32),
            pltpu.VMEM((ported, step, wide), f32),
            pltpu.VMEM((cells, 128), f32),
            pltpu.VMEM((ny, nx), f32),
            pltpu.VMEM(e_v.shape, f32),
            pltpu.VMEM(h_v.shape, f32),
            pltpu.SemaphoreType.DMA((8,)),
        ],
        compiler_params=params(32),
        name="march",
    )(e_v, h_v, coef_v, xh, yh, low, high, s, design_mask.T, ports, amplitudes)
    gradient = out[2]
    for shift in range(1, parts):
        gradient = gradient + lax.ppermute(
            out[2 + shift], "gz", [(i, (i + shift) % parts) for i in range(parts)]
        )
    return untiled(out[0], dims), untiled(out[1], dims), gradient.T


def solution(mesh):
    placed = (
        P(None, "gx", "gy", "gz"),
        P(None, "gx", "gy", "gz"),
        P(None, None, "gx", "gy", "gz"),
        P("gx", "gy", "gz"),
        P(),
        P("gx", "gy"),
        P(),
        P(),
    )
    sizes = tuple(mesh.shape[axis] for axis in ("gx", "gy", "gz"))
    return jax.shard_map(
        functools.partial(body, sizes),
        mesh=mesh,
        in_specs=placed,
        out_specs=(P(None, "gx", "gy", "gz"), P(None, "gx", "gy", "gz"), P("gx", ("gy", "gz"))),
        check_vma=False,
    )
```

```python
import functools

import jax
import jax.numpy as jnp
from jax import lax
from jax.experimental import pallas as pl
from jax.experimental.pallas import tpu as pltpu
from jax.sharding import PartitionSpec as P

STEPS = 2
FIELDS = 7
HALO = 8
HIGHEST = lax.Precision.HIGHEST

magnetic_step = 0.5
electric_step = 0.5

VM = pl.BlockSpec(memory_space=pltpu.VMEM)
SM = pl.BlockSpec(memory_space=pltpu.SMEM)
ANY = pl.BlockSpec(memory_space=pl.ANY)


HBM = pl.BlockSpec(memory_space=pltpu.HBM)


def in_hbm(array):
    return pltpu.with_memory_space_constraint(array, pltpu.HBM)


def in_vmem(array):
    return pltpu.with_memory_space_constraint(array, pltpu.VMEM)


def swap_table(size, odd):
    table = list(range(size))
    for i in range(odd, size - 1, 2):
        table[i], table[i + 1] = i + 1, i
    return table


def swaps(size):
    return [odd for odd in (0, 1) if odd + 1 < size]


def sends_up(index, odd):
    return lax.rem(index, 2) == odd


def has_partner(index, size, odd):
    up = sends_up(index, odd)
    return (up & (index + 1 < size)) | (jnp.logical_not(up) & (index >= 1))


def coef_table(perm_ref):
    return [
        electric_step / jnp.full((1, 1), perm_ref[i], jnp.float32) for i in range(perm_ref.shape[0])
    ]


def coef_of(material, table):
    out = jnp.zeros(material.shape, jnp.float32)
    for i, value in enumerate(table):
        out = jnp.where(material == i, value, out)
    return out


def tiled(array):
    *lead, nx, ny, nz = array.shape
    n = len(lead)
    split = array.reshape(*lead, nx, ny // 8, 8, nz // 128, 128)
    order = tuple(range(n + 2)) + (n + 3, n + 2, n + 4)
    return split.transpose(order).reshape(*lead, nx * ny * nz // 128, 128)


def untiled(array, dims):
    nx, ny, nz = dims
    lead = array.shape[:-2]
    n = len(lead)
    split = array.reshape(*lead, nx, ny // 8, nz // 128, 8, 128)
    order = tuple(range(n + 2)) + (n + 3, n + 2, n + 4)
    return split.transpose(order).reshape(*lead, nx, ny, nz)


def tiles_of(array):
    *lead, nx, ny, nz = array.shape
    return tiled(array).reshape(*lead, nx, ny // 8, nz // 128, 8, 128)


def send_faces(dims, sizes, e_ref, h_ref, m_ref, perm_ref, *refs):
    nx, ny, nz = dims
    lanes = nz // 128
    tiles = ny // 8
    plane = ny * lanes
    gx, gy = lax.axis_index("gx"), lax.axis_index("gy")
    xs, ys = swaps(sizes[0]), swaps(sizes[1])
    n_out = len(xs) + len(ys) + len(xs) * len(ys)
    outs, refs = refs[:n_out], refs[n_out:]
    x_bufs, refs = refs[: 2 * len(xs)], refs[2 * len(xs) :]
    y_bufs, sems = refs[: 2 * len(ys)], refs[2 * len(ys)]

    def source(f):
        return e_ref.at[f] if f < 3 else h_ref.at[f - 3] if f < 6 else m_ref

    copies = []

    def start(src, dst):
        copy = pltpu.make_async_copy(src, dst, sems.at[len(copies)])
        copy.start()
        copies.append(copy)

    for i, odd in enumerate(ys):
        up = sends_up(gy, odd)
        t, r = jnp.where(up, tiles - 1, 0), jnp.where(up, 6, 0)
        for f in range(FIELDS):
            buf = y_bufs[2 * i].at[f] if f < 6 else y_bufs[2 * i + 1]
            for z in range(lanes):
                start(
                    source(f).at[:, t, z, pl.ds(r, 2), :],
                    buf.at[z].reshape(nx, 8, 128).at[:, pl.ds(0, 2), :],
                )
    for i, odd in enumerate(xs):
        first = jnp.where(sends_up(gx, odd), nx - 2, 0)
        for f in range(FIELDS):
            start(source(f).at[pl.ds(first, 2)], x_bufs[2 * i].at[f] if f < 6 else x_bufs[2 * i + 1])

    table = coef_table(perm_ref)
    lane = lax.broadcasted_iota(jnp.int32, (8, 128), 1)
    lane_n = lax.broadcasted_iota(jnp.int32, (nx, 128), 1)

    def z_up(v, lane):
        out = []
        for z in range(lanes):
            after = pltpu.roll(v[z + 1], 127, 1) if z + 1 < lanes else jnp.zeros_like(v[z])
            out.append(jnp.where(lane < 127, pltpu.roll(v[z], 127, 1), after))
        return out

    def row_up(v):
        rows = v.shape[0]
        row = lax.broadcasted_iota(jnp.int32, v.shape, 0)
        return jnp.where(row < rows - 1, pltpu.roll(v, rows - 1, 0), 0.0)

    done = 0
    for i, odd in enumerate(ys):
        for copy in copies[done : done + FIELDS * lanes]:
            copy.wait()
        done += FIELDS * lanes
        up = sends_up(gy, odd)
        near, far = jnp.where(up, 1, 0), jnp.where(up, 0, 1)
        down = jnp.where(up, 0.0, magnetic_step)
        buf, mat, out = y_bufs[2 * i], y_bufs[2 * i + 1], outs[len(xs) + i]

        def at(f, which):
            return [buf[f, z, pl.ds(which, nx, stride=8), :] for z in range(lanes)]

        ex_f, ey_f, ez_f = (at(f, far) for f in range(3))
        hx_f, hz_f = at(3, far), at(5, far)
        hx_n, hz_n = at(3, near), at(5, near)
        ey_z = z_up(ey_f, lane_n)
        for z in range(lanes):
            for f in range(3):
                out[f * lanes + z] = buf[f, z, pl.ds(near, nx, stride=8), :]
            out[3 * lanes + z] = hx_n[z] - down * ez_f[z]
            out[4 * lanes + z] = buf[4, z, pl.ds(near, nx, stride=8), :]
            out[5 * lanes + z] = hz_n[z] + down * ex_f[z]
            out[6 * lanes + z] = coef_of(mat[z, pl.ds(near, nx, stride=8), :], table)
            out[7 * lanes + z] = hx_f[z] + magnetic_step * (ez_f[z] + (ey_z[z] - ey_f[z]))
            out[8 * lanes + z] = hz_f[z] - magnetic_step * ((row_up(ey_f[z]) - ey_f[z]) + ex_f[z])
        out[9 * lanes] = ey_f[0]
    for i, odd in enumerate(xs):
        for copy in copies[done : done + FIELDS]:
            copy.wait()
        done += FIELDS
        up = sends_up(gx, odd)
        near, far = jnp.where(up, 1, 0), jnp.where(up, 0, 1)
        down = jnp.where(up, 0.0, magnetic_step)
        buf, mat, out = x_bufs[2 * i], x_bufs[2 * i + 1], outs[i]

        def put(k, t, z, v):
            out[pl.ds(k * plane + (t * lanes + z) * 8, 8), :] = v

        ex_y = [
            row_up(jnp.concatenate([buf[0, far, t, z] for t in range(tiles)], axis=0))
            for z in range(lanes)
        ]
        for t in range(tiles):
            ex_z = z_up([buf[0, far, t, z] for z in range(lanes)], lane)
            for z in range(lanes):
                ex_f, ey_f, ez_f = (buf[f, far, t, z] for f in range(3))
                for f in range(4):
                    put(f, t, z, buf[f, near, t, z])
                put(4, t, z, buf[4, near, t, z] + down * ez_f)
                put(5, t, z, buf[5, near, t, z] - down * ey_f)
                put(6, t, z, coef_of(mat[near, t, z], table))
                put(7, t, z, buf[4, far, t, z] - magnetic_step * ((ex_z[z] - ex_f) + ez_f))
                ex_up = ex_y[z][t * 8 : t * 8 + 8]
                put(8, t, z, buf[5, far, t, z] + magnetic_step * (ey_f + (ex_up - ex_f)))
            out[pl.ds(9 * plane + t * 8, 8), :] = buf[0, far, t, 0]
        for j, odd_y in enumerate(ys):
            up_y = sends_up(gy, odd_y)
            t = jnp.where(up_y, tiles - 1, 0)
            lines = (jnp.where(up_y, 7, 0), jnp.where(up_y, 6, 1))
            out = outs[len(xs) + len(ys) + i * len(ys) + j]
            for z in range(lanes):
                for f in range(FIELDS):
                    for k in range(4):
                        where = (near, far)[k // 2], t, z, pl.ds(lines[k % 2], 1)
                        if f < 6:
                            line = buf[(f, *where)]
                        else:
                            line = coef_of(mat[where], table)
                        out[z, pl.ds(4 * f + k, 1), :] = line


def turn_ends(parts, lane, count):
    out = None
    for k in range(count):
        first, last = parts(k)
        turned = pltpu.roll(jnp.where(lane < 64, first, last), 8 * k + 4, 1)
        out = turned if out is None else jnp.where(lane >= 8 * k, turned, out)
    return out


def own_ends(dims, e_v, h_v, m_v, snap_ref, perm_ref, coef_v, packed):
    nx, ny, nz = dims
    lanes = nz // 128
    step = ny + HALO
    table = coef_table(perm_ref)
    lane = lax.broadcasted_iota(jnp.int32, (8, 128), 1)
    tiles = ny // 8

    def one(x, carry):
        index = pl.ds(pl.multiple_of(x * ny, ny), ny)
        change = []
        for c in range(3):
            s = [
                [
                    snap_ref[t, c, index, z * 128 : z * 128 + 128].astype(jnp.float32)
                    for z in (0, lanes - 1)
                ]
                for t in range(STEPS + 1)
            ]
            change.append([[s[t][z] - s[t + 1][z] for z in range(2)] for t in range(STEPS)])
        for t in range(tiles):
            here = [
                pl.ds(pl.multiple_of(((x * tiles + t) * lanes + z) * 8, 8), 8) for z in range(lanes)
            ]
            for z in range(lanes):
                coef_v[here[z], :] = coef_of(m_v[here[z], :], table)

            def parts(k):
                if k < 3:
                    return e_v[k, here[0], :], e_v[k, here[-1], :]
                if k < 6:
                    return h_v[k - 3, here[0], :], h_v[k - 3, here[-1], :]
                if k == 6:
                    return coef_v[here[0], :], coef_v[here[-1], :]
                pair = change[(k - FIELDS) % 3][1 - (k - FIELDS) // 3]
                return tuple(v[t * 8 : t * 8 + 8] for v in pair)

            row = pl.multiple_of((x + 2) * step + HALO + t * 8, 8)
            packed[pl.ds(row, 8), :] = turn_ends(parts, lane, FIELDS + 6)
        return carry

    lax.fori_loop(0, nx, one, 0, unroll=2)


def unpack_faces(dims, sizes, own_packed, *refs):
    nx, ny, nz = dims
    lanes = nz // 128
    tiles = ny // 8
    plane = ny * lanes
    step = ny + HALO
    gx, gy = lax.axis_index("gx"), lax.axis_index("gy")
    xs, ys = swaps(sizes[0]), swaps(sizes[1])
    n_msgs = len(xs) + len(ys) + len(xs) * len(ys)
    msgs = refs[:n_msgs]
    xh, yh, own_t, up_ref, down_ref, packed, x_raw, y_raw = refs[n_msgs:]
    xh[...] = jnp.zeros(xh.shape, jnp.float32)
    x_raw[...] = jnp.zeros(x_raw.shape, jnp.float32)
    y_raw[...] = jnp.zeros(y_raw.shape, jnp.float32)
    for f in range(FIELDS):
        for z in range(lanes):
            if len(ys) < 2 or f < 3:
                yh[f, z] = jnp.zeros(yh.shape[2:], jnp.float32)
            else:
                for p in (0, 1, nx + 2, nx + 3):
                    yh[f, z, pl.ds(p * HALO, HALO), :] = jnp.zeros((HALO, 128), jnp.float32)

    def planes(odd):
        high = sends_up(gx, odd)
        return jnp.where(high, 2, 1), jnp.where(high, 3, 0)

    def lines(odd):
        high = sends_up(gy, odd)
        return jnp.where(high, 0, HALO - 1), jnp.where(high, 1, HALO - 2)

    for i, odd in enumerate(xs):
        ok = has_partner(gx, sizes[0], odd)
        near, far = planes(odd)
        msg = msgs[i]
        for t in range(tiles):
            for z in range(lanes):
                for k, f in enumerate((0, 1, 2, 3, 4, 5, 6, 4, 5)):
                    q = near if k < FIELDS else far
                    xh[f, z, pl.ds(pl.multiple_of(q * ny + t * 8, 8), 8), :] = jnp.where(
                        ok, msg[pl.ds(k * plane + (t * lanes + z) * 8, 8), :], 0.0
                    )
            x_raw[pl.ds(pl.multiple_of(far * ny + t * 8, 8), 8), :] = jnp.where(
                ok & (far == 0), msg[pl.ds(9 * plane + t * 8, 8), :], 0.0
            )
    for i, odd in enumerate(ys):
        ok = has_partner(gy, sizes[1], odd)
        near, far = lines(odd)
        msg = msgs[len(xs) + i]
        for z in range(lanes):
            for k, f in enumerate((0, 1, 2, 3, 4, 5, 6, 3, 5)):
                r = near if k < FIELDS else far
                yh[f, z, pl.ds(2 * HALO + r, nx, stride=HALO), :] = jnp.where(
                    ok, msg[k * lanes + z], 0.0
                )
        y_raw[pl.ds(2 * HALO + far, nx, stride=HALO), :] = jnp.where(
            ok & (far == HALO - 2), msg[9 * lanes], 0.0
        )
    for i, ox in enumerate(xs):
        for j, oy in enumerate(ys):
            ok = has_partner(gx, sizes[0], ox) & has_partner(gy, sizes[1], oy)
            px, py = planes(ox), lines(oy)
            px = [jnp.where(q < 2, q, q + nx) for q in px]
            msg = msgs[len(xs) + len(ys) + i * len(ys) + j]
            for z in range(lanes):
                for f in range(FIELDS):
                    for k in range(4):
                        yh[f, z, pl.ds(px[k // 2] * HALO + py[k % 2], 1), :] = jnp.where(
                            ok, msg[z, pl.ds(4 * f + k, 1), :], 0.0
                        )

    lane = lax.broadcasted_iota(jnp.int32, (8, 128), 1)
    upper = lax.broadcasted_iota(jnp.int32, (8, 128), 0) < HALO // 2

    def halo_rows(p, before, here):
        def tile(f, z):
            if f == FIELDS:
                return y_raw[here, :]
            return jnp.where(upper, yh[f, z, before, :], yh[f, z, here, :])

        packed[pl.ds(p * step if isinstance(p, int) else pl.multiple_of(p * step, 8), HALO), :] = (
            turn_ends(lambda f: (tile(f, 0), tile(f, lanes - 1)), lane, FIELDS + 1)
        )

    def one(p, carry):
        halo_rows(
            p,
            pl.ds(pl.multiple_of((p - 1) * HALO, 8), HALO),
            pl.ds(pl.multiple_of(p * HALO, 8), HALO),
        )
        return carry

    halo_rows(0, pl.ds(0, HALO), pl.ds(0, HALO))
    lax.fori_loop(1, nx + 4, one, 0, unroll=5)
    last = pl.ds((nx + 3) * HALO, HALO)
    halo_rows(nx + 4, last, last)
    for q, p in enumerate((0, 1, nx + 2, nx + 3)):
        for t in range(tiles):
            index = pl.ds(q * ny + t * 8, 8)

            def parts(f):
                if f == FIELDS:
                    return x_raw[index, :], x_raw[index, :]
                return xh[f, 0, index, :], xh[f, lanes - 1, index, :]

            packed[pl.ds(p * step + HALO + t * 8, 8), :] = turn_ends(parts, lane, FIELDS + 1)
    for x in range(nx):
        index = pl.ds((x + 2) * step + HALO, ny)
        packed[index, :] = own_packed[index, :]
    after = (nx + 4) * step + HALO
    padded = packed.shape[0]
    if padded > after:
        packed[after:, :] = jnp.zeros((padded - after, 128), jnp.float32)
    for b in range(padded // 128):
        here = pl.ds(b * 128, 128)
        block = jnp.transpose(packed[here, :])
        own_t[:, here] = block
        for f in range(FIELDS):
            up_ref[f : f + 1, here] = block[8 * f + 3 : 8 * f + 4, :]
            up_ref[8 + f : 9 + f, here] = block[8 * f + 2 : 8 * f + 3, :]
            down = [block[8 * f + 4 + k : 8 * f + 5 + k, :] for k in range(2)]
            if f < 2:
                at = lax.broadcasted_iota(jnp.int32, (1, 128), 1) + b * 128
                raw = (at >= HALO) & (at < step) if f == 0 else lax.rem(at, step) < HALO
                tail = [block[8 * FIELDS + 4 + k : 8 * FIELDS + 5 + k, :] for k in range(2)]
                down = [down[k] + jnp.where(raw, tail[k], 0.0) for k in range(2)]
            down_ref[f : f + 1, here] = down[0]
            down_ref[8 + f : 9 + f, here] = down[1]
    for row in (7, 15):
        up_ref[row : row + 1, :] = jnp.zeros((1, padded), jnp.float32)
        down_ref[row : row + 1, :] = jnp.zeros((1, padded), jnp.float32)


def columns_of(line, nx, ny, step, first, skip):
    size = line.shape[1]
    at = lax.broadcasted_iota(jnp.int32, (ny, size), 1) - first
    y = lax.broadcasted_iota(jnp.int32, (ny, size), 0)
    ok = (at >= 0) & (at < nx * step) & (lax.rem(at + skip, step) == y)
    spread = jnp.where(ok, line, 0.0)
    at = lax.broadcasted_iota(jnp.int32, (size, nx), 0) - first
    x = lax.broadcasted_iota(jnp.int32, (size, nx), 1)
    pick = ((at >= x * step) & (at < (x + 1) * step)).astype(jnp.float32)
    return lax.dot_general(spread, pick, (((1,), (0,)), ((), ())), precision=HIGHEST)


def find_ports(dims, sizes, ports_ref):
    nx, ny, nz = dims
    gx, gy, gz = lax.axis_index("gx"), lax.axis_index("gy"), lax.axis_index("gz")
    plane_cells = (ny * sizes[1]) * (nz * sizes[2])
    line_cells = nz * sizes[2]
    found = []
    for q in range(ports_ref.shape[0]):
        cell = ports_ref[q]
        x = lax.div(cell, plane_cells) - gx * nx
        y = lax.rem(lax.div(cell, line_cells), ny * sizes[1]) - gy * ny
        z = lax.rem(cell, line_cells) - gz * nz
        found.append((x, y, z))
    return found


def march(dims, sizes, e_v, h_v, coef_v, xh, yh, snap_ref, ports_ref, amps_ref, *refs):
    nx, ny, nz = dims
    lanes = nz // 128
    tiles = ny // 8
    step = ny + HALO
    e_s, h_s, column_ref, e1, h1, h2, half_ref, struck, clean, sums = refs
    gx, gy = lax.axis_index("gx"), lax.axis_index("gy")
    row = lax.broadcasted_iota(jnp.int32, (step, nz), 0)
    lane = lax.broadcasted_iota(jnp.int32, (step, nz), 1)
    inside = (row < ny) | ((row < ny + 2) & (gy < sizes[1] - 1)) | ((row >= ny + 4) & (gy > 0))
    half_ref[...] = jnp.where(inside, magnetic_step, 0.0)
    for k in range(2):
        clean[k] = jnp.where((lane[:ny] > k) & (lane[:ny] < nz - 1 - k), 1.0, 0.0)

    planes_struck = []
    for q, (x, y, z) in enumerate(find_ports(dims, sizes, ports_ref)):
        near = (y >= -2) & (y < ny + 2) & (z >= 0) & (z < nz)
        at = jnp.where(y < 0, y + step, y)
        struck[q] = jnp.where((row == at) & (lane == z) & near, 1.0, 0.0)
        planes_struck.append(x + 2)

    def spot(x, t, z):
        index = ((x * tiles + t) * lanes + z) * 8
        return pl.ds(index if isinstance(index, int) else pl.multiple_of(index, 8), 8)

    def own_tile(f, p, t, z):
        if isinstance(p, int) and not 2 <= p < nx + 2:
            return xh[f, z, pl.ds((p if p < 2 else p - nx) * ny + t * 8, 8), :]
        if f < 3:
            return e_v[f, spot(p - 2, t, z), :]
        if f < 6:
            return h_v[f - 3, spot(p - 2, t, z), :]
        return coef_v[spot(p - 2, t, z), :]

    def aligned(index):
        return index if isinstance(index, int) else pl.multiple_of(index, 8)

    def load(f, p):
        columns = []
        for z in range(lanes):
            column = [own_tile(f, p, t, z) for t in range(tiles)]
            column.append(yh[f, z, pl.ds(aligned(p * HALO), HALO), :])
            columns.append(jnp.concatenate(column, axis=0))
        return jnp.concatenate(columns, axis=1)

    def load_own(f, p):
        return jnp.concatenate(
            [
                jnp.concatenate([own_tile(f, p, t, z) for t in range(tiles)], axis=0)
                for z in range(lanes)
            ],
            axis=1,
        )

    def put(ref, f, x, v):
        for t in range(tiles):
            for z in range(lanes):
                ref[f, spot(x, t, z), :] = v[t * 8 : t * 8 + 8, z * 128 : z * 128 + 128]

    def y_up(v):
        return pltpu.roll(v, step - 1, 0)

    def y_down(v):
        return pltpu.roll(v, 1, 0)

    def z_up(v):
        return pltpu.roll(v, nz - 1, 1)

    def z_down(v):
        return pltpu.roll(v, 1, 1)

    def new_h(half, ex, ey, ez, ey_x, ez_x, hx, hy, hz):
        cx = (y_up(ez) - ez) - (z_up(ey) - ey)
        cy = (z_up(ex) - ex) - (ez_x - ez)
        cz = (ey_x - ey) - (y_up(ex) - ex)
        return hx - half * cx, hy - half * cy, hz - half * cz

    def curl_h(hx, hy, hz, hy_x, hz_x):
        cx = (hz - y_down(hz)) - (hy - z_down(hy))
        cy = (hx - z_down(hx)) - (hz - hz_x)
        cz = (hy - hy_x) - (hx - y_down(hx))
        return cx, cy, cz

    def half_of(p):
        if isinstance(p, int) and p < 2:
            return half_ref[...] * jnp.where(gx == 0, 0.0, 1.0)
        if isinstance(p, int) and p >= nx + 2:
            return half_ref[...] * jnp.where(gx == sizes[0] - 1, 0.0, 1.0)
        return half_ref[...]

    def first_h(p):
        e = [load(f, p) for f in range(3)]
        h = [load(3 + f, p) for f in range(3)]
        out = new_h(half_of(p), *e, load(1, p + 1), load(2, p + 1), *h)
        for f in range(3):
            h1[f, p] = out[f]

    def first_e(p):
        e = [load(f, p) for f in range(3)]
        curl = curl_h(*[h1[f, p] for f in range(3)], h1[1, p - 1], h1[2, p - 1])
        coef = load(6, p)
        out = [e[f] + coef * curl[f] for f in range(3)]
        for f in range(3):
            e1[f, p] = out[f]

    def second_h(p):
        e = [e1[f, p] for f in range(3)]
        h = [h1[f, p] for f in range(3)]
        out = new_h(half_of(p), *e, e1[1, p + 1], e1[2, p + 1], *h)
        for f in range(3):
            h2[f, p] = out[f]

    def second_e(p):
        h = [h2[f, p] for f in range(3)]
        curl = curl_h(*h, h2[1, p - 1], h2[2, p - 1])
        coef = load_own(6, p)
        old = [e1[f, p, 0:ny, 0:nz] for f in range(3)]
        new = [old[f] + coef * curl[f][:ny, :nz] for f in range(3)]
        x = p - 2
        index = pl.ds(aligned(x * ny), ny)
        total = None
        for f in range(3):
            put(e_s, f, x, new[f])
            put(h_s, f, x, h[f][:ny, :nz])
            s = [snap_ref[t, f, index, :].astype(jnp.float32) for t in range(STEPS + 1)]
            one = [old[f] * (s[0] - s[1]), new[f] * (s[1] - s[2])]
            total = one if total is None else [total[k] + one[k] for k in range(2)]
        total = total[0] * clean[0] + total[1] * clean[1]
        folded = total[:, 0:128]
        for at in range(128, nz, 128):
            folded = folded + total[:, at : at + 128]
        sums[index, :] = folded

    def strike(p):
        dynamic = not isinstance(p, int)
        first, second = p - 1, p - 4
        hit = None
        for at in planes_struck:
            here = (at == first) | (at == second)
            hit = here if hit is None else hit | here

        @pl.when(hit)
        def _():
            for q, at in enumerate(planes_struck):
                if dynamic or 1 <= first <= nx + 2:
                    amp = jnp.where(at == first, amps_ref[0, q], 0.0)
                    e1[2, first] = e1[2, first] + struck[q] * amp
                if dynamic or 2 <= second <= nx + 1:
                    x = second - 2
                    amp = jnp.where(at == second, amps_ref[1, q], 0.0)
                    index = pl.ds(aligned(x * ny), ny)
                    s = [snap_ref[t, 2, index, :].astype(jnp.float32) for t in (1, 2)]
                    folded = jnp.zeros((ny, 128), jnp.float32)
                    for z in range(lanes):
                        here = slice(z * 128, z * 128 + 128)
                        gain = struck[q, 0:ny, here] * amp
                        folded = folded + gain * clean[1, :, here] * (s[0] - s[1])[:, here]
                        for t in range(tiles):
                            here = spot(x, t, z)
                            e_s[2, here, :] = e_s[2, here, :] + gain[t * 8 : t * 8 + 8]
                    sums[index, :] = sums[index, :] + folded

    def one(p):
        dynamic = not isinstance(p, int)
        if dynamic or 2 <= p - 4 <= nx + 1:
            second_e(p - 4)
        if dynamic or 1 <= p - 3 <= nx + 1:
            second_h(p - 3)
        if dynamic or 1 <= p - 1 <= nx + 2:
            first_e(p - 1)
        if dynamic or 0 <= p <= nx + 2:
            first_h(p)
        strike(p)

    def body(p, carry):
        one(p)
        return carry

    for p in range(6):
        one(p)
    lax.fori_loop(6, nx + 1, body, 0)
    for p in range(nx + 1, nx + 6):
        one(p)
    nt = (((1,), (1,)), ((), ()))
    line = lax.dot_general(jnp.ones((8, 128), jnp.float32), sums[...], nt, precision=HIGHEST)
    column_ref[...] = columns_of(line[0:1, :], nx, ny, ny, 0, 0)


def finish_ends(
    dims, sizes, own_t, low_ref, high_ref, column_ref, mask_ref, ports_ref, amps_ref, *refs
):
    nx, ny, nz = dims
    step = ny + HALO
    parts = sizes[2]
    ends_ref = refs[0]
    grads = refs[1 : 1 + parts]
    strips, turned, rows_ref = refs[1 + parts :]
    gx, gy, gz = lax.axis_index("gx"), lax.axis_index("gy"), lax.axis_index("gz")
    padded = own_t.shape[1]
    row = lax.broadcasted_iota(jnp.int32, (8, padded), 0)
    lane = lax.broadcasted_iota(jnp.int32, (8, padded), 1) - HALO
    has_low, has_high = gz > 0, gz < sizes[2] - 1
    for k, (msg, ok, far, near) in enumerate(((low_ref, has_low, 2, 3), (high_ref, has_high, 5, 4))):
        for f in range(FIELDS):
            strips[k, f] = own_t[8 * f : 8 * f + 8, :]
            strips[k, f, far : far + 1, :] = jnp.where(ok, msg[8 + f : 9 + f, :], 0.0)
            strips[k, f, near : near + 1, :] = jnp.where(ok, msg[f : f + 1, :], 0.0)

    at = lane + 2
    p, y = lax.div(at, step), lax.rem(at, step) - 2
    inside = ((p >= 2) | (gx > 0)) & ((p < nx + 2) | (gx < sizes[0] - 1))
    inside = inside & ((y >= 0) | (gy > 0)) & ((y < ny) | (gy < sizes[1] - 1))
    found = find_ports(dims, sizes, ports_ref)

    def x_up(v):
        return pltpu.roll(v, padded - step, 1)

    def x_down(v):
        return pltpu.roll(v, step, 1)

    def y_up(v):
        return pltpu.roll(v, padded - 1, 1)

    def y_down(v):
        return pltpu.roll(v, 1, 1)

    def z_up(v):
        return pltpu.roll(v, 7, 0)

    def z_down(v):
        return pltpu.roll(v, 1, 0)

    total = None
    results = []
    for k in range(2):
        ex, ey, ez, hx, hy, hz, coef = (strips[k, f] for f in range(FIELDS))
        first = -4 if k == 0 else nz - 4
        good = ((row >= 4) | has_low) if k == 0 else ((row < 4) | has_high)
        half = jnp.where(inside & good, magnetic_step, 0.0)
        for s in range(STEPS):
            cx = (y_up(ez) - ez) - (z_up(ey) - ey)
            cy = (z_up(ex) - ex) - (x_up(ez) - ez)
            cz = (x_up(ey) - ey) - (y_up(ex) - ex)
            hx, hy, hz = hx - half * cx, hy - half * cy, hz - half * cz
            cx = (hz - y_down(hz)) - (hy - z_down(hy))
            cy = (hx - z_down(hx)) - (hz - x_down(hz))
            cz = (hy - x_down(hy)) - (hx - y_down(hx))
            ex, ey, ez = ex + coef * cx, ey + coef * cy, ez + coef * cz
            for q, (sx, sy, sz) in enumerate(found):
                near = (sx >= -2) & (sx < nx + 2) & (sy >= -2) & (sy < ny + 2)
                hit = (row == sz - first) & (at == (sx + 2) * step + sy + 2) & near
                ez = ez + jnp.where(hit, amps_ref[s, q], 0.0)
            if k == 0:
                mine = (row == 4) | ((row == 5) & (s == 1))
            else:
                mine = (row == 3) | ((row == 2) & (s == 1))
            for c, e in enumerate((ex, ey, ez)):
                tile = FIELDS + c + 3 * (1 - s)
                one = jnp.where(mine, e * own_t[8 * tile : 8 * tile + 8, :], 0.0)
                total = one if total is None else total + one
        results.append((ex, ey, ez, hx, hy, hz))
    for c in range(6):
        rows_ref[8 * c : 8 * c + 8, :] = jnp.where(row < 4, results[1][c], results[0][c])
    line = jnp.sum(total, axis=0, keepdims=True)
    column = column_ref[...] + columns_of(line, nx, ny, step, 2 * step + HALO, 0)
    turned[...] = column * mask_ref[...].astype(jnp.float32)
    width = ny // parts
    for shift in range(parts):
        owner = lax.rem(gz + shift, parts)
        grads[shift][...] = turned[pl.ds(owner * width, width), :]
    ends_ref[...] = rows_ref[...]


def write_out(dims, e_s, h_s, ends_ref, e_out, h_out, spare, e_v, h_v, ends_t, sems):
    nx, ny, nz = dims
    lanes = nz // 128
    tiles = ny // 8
    plane = ny * lanes
    step = ny + HALO
    lane = lax.broadcasted_iota(jnp.int32, (8, 128), 1)
    spare[...] = jnp.zeros(spare.shape, jnp.float32)
    spare[0 : ends_ref.shape[0], :] = ends_ref[...]
    for b in range(spare.shape[1] // 128):
        ends_t[b * 128 : (b + 1) * 128, :] = jnp.transpose(spare[:, b * 128 : (b + 1) * 128])

    def one(x, carry):
        for t in range(tiles):
            v = ends_t[pl.ds(pl.multiple_of((x + 2) * step + HALO + t * 8, 8), 8), :]
            for c in range(6):
                src, dst = (e_s, e_v) if c < 3 else (h_s, h_v)
                placed = pltpu.roll(v, 124 - 8 * c, 1)
                for z in range(lanes):
                    here = pl.ds(pl.multiple_of(((x * tiles + t) * lanes + z) * 8, 8), 8)
                    out = src[c % 3, here, :]
                    if z == 0:
                        out = jnp.where(lane < 2, placed, out)
                    if z == lanes - 1:
                        out = jnp.where(lane >= 126, placed, out)
                    dst[c % 3, here, :] = out
        return carry

    chunk = nx // 4
    copies = []
    for c in range(4):
        lax.fori_loop(c * chunk, (c + 1) * chunk, one, 0, unroll=2)
        here = pl.ds(c * chunk * plane, chunk * plane)
        for k, (src, dst) in enumerate(((e_v, e_out), (h_v, h_out))):
            copy = pltpu.make_async_copy(src.at[:, here], dst.at[:, here], sems.at[2 * c + k])
            copy.start()
            copies.append(copy)
    for copy in copies:
        copy.wait()


def params(limit=12):
    return pltpu.CompilerParams(vmem_limit_bytes=limit * 1024 * 1024)


def body(sizes, e_adjoint, h_adjoint, snapshots, material, permittivity, design_mask, ports, amplitudes):
    permittivity = in_hbm(permittivity)
    permittivity = in_hbm(permittivity)
    dims = material.shape
    nx, ny, nz = dims
    lanes = nz // 128
    tiles = ny // 8
    plane = ny * lanes
    cells = nx * ny
    step = ny + HALO
    padded = -(-((nx + 4) * step + HALO) // 128) * 128
    f32, i32 = jnp.float32, jnp.int32
    xs, ys = swaps(sizes[0]), swaps(sizes[1])
    block, cube = jax.ShapeDtypeStruct, pltpu.VMEM

    shapes = [block((9 * plane + ny, 128), f32) for _ in xs]
    shapes += [block((9 * lanes + 1, nx, 128), f32) for _ in ys]
    shapes += [block((lanes, 4 * FIELDS, 128), f32) for _ in xs for _ in ys]
    buffers = []
    for _ in xs:
        buffers += [cube((6, 2, tiles, lanes, 8, 128), f32), cube((2, tiles, lanes, 8, 128), i32)]
    for _ in ys:
        buffers += [cube((6, lanes, nx * 8, 128), f32), cube((lanes, nx * 8, 128), i32)]
    n_copies = FIELDS * (len(xs) + lanes * len(ys))
    msgs = pl.pallas_call(
        functools.partial(send_faces, dims, sizes),
        out_shape=shapes,
        in_specs=[HBM, HBM, HBM, SM],
        out_specs=[VM] * len(shapes),
        scratch_shapes=buffers + [pltpu.SemaphoreType.DMA((n_copies,))],
        compiler_params=params(),
        name="send_faces",
    )(
        in_hbm(tiles_of(e_adjoint)),
        in_hbm(tiles_of(h_adjoint)),
        in_hbm(tiles_of(material)),
        permittivity,
    )
    e_v, h_v, m_v = in_vmem(tiled(e_adjoint)), in_vmem(tiled(h_adjoint)), in_vmem(tiled(material))
    s = in_vmem(snapshots.reshape(STEPS + 1, 3, cells, nz))
    coef_v, own_packed = pl.pallas_call(
        functools.partial(own_ends, dims),
        out_shape=[cube(m_v.shape, f32), cube((padded, 128), f32)],
        in_specs=[VM, VM, VM, VM, SM],
        out_specs=[VM] * 2,
        compiler_params=params(),
        cost_estimate=pl.CostEstimate(flops=10**7, bytes_accessed=4 * 10**6, transcendentals=0),
        name="own_ends",
    )(e_v, h_v, m_v, s, permittivity)

    both = ("gx", "gy")
    tables = [("gx", list(enumerate(swap_table(sizes[0], o)))) for o in xs]
    tables += [("gy", list(enumerate(swap_table(sizes[1], o)))) for o in ys]
    for ox in xs:
        for oy in ys:
            tx, ty = swap_table(sizes[0], ox), swap_table(sizes[1], oy)
            pairs = [
                (x * sizes[1] + y, tx[x] * sizes[1] + ty[y])
                for x in range(sizes[0])
                for y in range(sizes[1])
            ]
            tables.append((both, pairs))
    got = [lax.ppermute(msg, axis, pairs) for msg, (axis, pairs) in zip(msgs, tables)]

    xh, yh, own_t, up, down = pl.pallas_call(
        functools.partial(unpack_faces, dims, sizes),
        out_shape=[
            cube((FIELDS, lanes, 4 * ny, 128), f32),
            cube((FIELDS, lanes, (nx + 4) * HALO, 128), f32),
            cube((128, padded), f32),
            block((16, padded), f32),
            block((16, padded), f32),
        ],
        in_specs=[VM] * (1 + len(got)),
        out_specs=[VM] * 5,
        scratch_shapes=[
            pltpu.VMEM((padded, 128), f32),
            pltpu.VMEM((4 * ny, 128), f32),
            pltpu.VMEM(((nx + 4) * HALO, 128), f32),
        ],
        compiler_params=params(),
        name="unpack_faces",
    )(own_packed, *got)

    parts = sizes[2]
    low = lax.ppermute(up, "gz", [(i, (i + 1) % parts) for i in range(parts)])
    high = lax.ppermute(down, "gz", [(i, (i - 1) % parts) for i in range(parts)])

    ported = ports.shape[0]
    e_s, h_s, column = pl.pallas_call(
        functools.partial(march, dims, sizes),
        out_shape=[cube(e_v.shape, f32), cube(h_v.shape, f32), cube((ny, nx), f32)],
        in_specs=[VM] * 6 + [SM, SM],
        out_specs=[VM] * 3,
        scratch_shapes=[
            pltpu.VMEM((3, nx + 4, step, nz), f32),
            pltpu.VMEM((3, nx + 4, step, nz), f32),
            pltpu.VMEM((3, nx + 4, step, nz), f32),
            pltpu.VMEM((step, nz), f32),
            pltpu.VMEM((ported, step, nz), f32),
            pltpu.VMEM((2, ny, nz), f32),
            pltpu.VMEM((cells, 128), f32),
        ],
        compiler_params=params(24),
        cost_estimate=pl.CostEstimate(flops=4 * 10**7, bytes_accessed=10**7, transcendentals=0),
        name="march",
    )(e_v, h_v, coef_v, xh, yh, s, ports, amplitudes)
    ends, *chunks = pl.pallas_call(
        functools.partial(finish_ends, dims, sizes),
        out_shape=[cube((48, padded), f32)] + [block((ny // parts, nx), f32)] * parts,
        in_specs=[VM] * 5 + [SM, SM],
        out_specs=[VM] * (1 + parts),
        scratch_shapes=[
            pltpu.VMEM((2, FIELDS, 8, padded), f32),
            pltpu.VMEM((ny, nx), f32),
            pltpu.VMEM((48, padded), f32),
        ],
        compiler_params=params(),
        name="finish_ends",
    )(own_t, low, high, column, design_mask.T, ports, amplitudes)
    e_out, h_out = pl.pallas_call(
        functools.partial(write_out, dims),
        out_shape=[block(e_v.shape, f32), block(h_v.shape, f32)],
        in_specs=[VM] * 3,
        out_specs=[HBM] * 2,
        scratch_shapes=[
            pltpu.VMEM((128, padded), f32),
            pltpu.VMEM(e_v.shape, f32),
            pltpu.VMEM(h_v.shape, f32),
            pltpu.VMEM((padded, 128), f32),
            pltpu.SemaphoreType.DMA((8,)),
        ],
        compiler_params=params(),
        cost_estimate=pl.CostEstimate(flops=10**7, bytes_accessed=8 * 10**6, transcendentals=0),
        name="write_out",
    )(e_s, h_s, ends)
    gradient = chunks[0]
    for shift in range(1, parts):
        gradient = gradient + lax.ppermute(
            chunks[shift], "gz", [(i, (i + shift) % parts) for i in range(parts)]
        )
    return untiled(e_out, dims), untiled(h_out, dims), gradient.T


def solution(mesh):
    placed = (
        P(None, "gx", "gy", "gz"),
        P(None, "gx", "gy", "gz"),
        P(None, None, "gx", "gy", "gz"),
        P("gx", "gy", "gz"),
        P(),
        P("gx", "gy"),
        P(),
        P(),
    )
    sizes = tuple(mesh.shape[axis] for axis in ("gx", "gy", "gz"))
    return jax.shard_map(
        functools.partial(body, sizes),
        mesh=mesh,
        in_specs=placed,
        out_specs=(P(None, "gx", "gy", "gz"), P(None, "gx", "gy", "gz"), P("gx", ("gy", "gz"))),
        check_vma=False,
    )
```

```python
import functools

import jax
import jax.numpy as jnp
from jax import lax
from jax.experimental import pallas as pl
from jax.experimental.pallas import tpu as pltpu
from jax.sharding import PartitionSpec as P

STEPS = 2
FIELDS = 7
HALO = 8

magnetic_step = 0.5
electric_step = 0.5

VM = pl.BlockSpec(memory_space=pltpu.VMEM)
SM = pl.BlockSpec(memory_space=pltpu.SMEM)
ANY = pl.BlockSpec(memory_space=pl.ANY)


HBM = pl.BlockSpec(memory_space=pltpu.HBM)


def in_hbm(array):
    return pltpu.with_memory_space_constraint(array, pltpu.HBM)


def in_vmem(array):
    return pltpu.with_memory_space_constraint(array, pltpu.VMEM)


def swap_table(size, odd):
    table = list(range(size))
    for i in range(odd, size - 1, 2):
        table[i], table[i + 1] = i + 1, i
    return table


def swaps(size):
    return [odd for odd in (0, 1) if odd + 1 < size]


def partner_of(index, shift, size):
    if size & (size - 1) == 0:
        return index ^ shift
    return (index + shift) % size


def sends_up(index, odd):
    return lax.rem(index, 2) == odd


def has_partner(index, size, odd):
    up = sends_up(index, odd)
    return (up & (index + 1 < size)) | (jnp.logical_not(up) & (index >= 1))


def coef_table(perm_ref):
    return [
        electric_step / jnp.full((1, 1), perm_ref[i], jnp.float32) for i in range(perm_ref.shape[0])
    ]


def coef_of(material, table):
    out = jnp.zeros(material.shape, jnp.float32)
    for i, value in enumerate(table):
        out = jnp.where(material == i, value, out)
    return out


def tiled(array):
    *lead, nx, ny, nz = array.shape
    n = len(lead)
    split = array.reshape(*lead, nx, ny // 8, 8, nz // 128, 128)
    order = tuple(range(n + 2)) + (n + 3, n + 2, n + 4)
    return split.transpose(order).reshape(*lead, nx * ny * nz // 128, 128)


def untiled(array, dims):
    nx, ny, nz = dims
    lead = array.shape[:-2]
    n = len(lead)
    split = array.reshape(*lead, nx, ny // 8, nz // 128, 8, 128)
    order = tuple(range(n + 2)) + (n + 3, n + 2, n + 4)
    return split.transpose(order).reshape(*lead, nx, ny, nz)


def tiles_of(array):
    *lead, nx, ny, nz = array.shape
    return tiled(array).reshape(*lead, nx, ny // 8, nz // 128, 8, 128)


def send_faces(dims, sizes, e_ref, h_ref, m_ref, perm_ref, *refs):
    nx, ny, nz = dims
    lanes = nz // 128
    tiles = ny // 8
    plane = ny * lanes
    gx, gy = lax.axis_index("gx"), lax.axis_index("gy")
    xs, ys = swaps(sizes[0]), swaps(sizes[1])
    n_out = len(xs) + len(ys) + len(xs) * len(ys)
    outs, refs = refs[:n_out], refs[n_out:]
    x_bufs, refs = refs[: 3 * len(xs)], refs[3 * len(xs) :]
    y_bufs, (perm_s, sems) = refs[: 3 * len(ys)], refs[3 * len(ys) :]
    copies = []

    def start(src, dst):
        copy = pltpu.make_async_copy(src, dst, sems.at[len(copies)])
        copy.start()
        copies.append(copy)

    for i, odd in enumerate(ys):
        up = sends_up(gy, odd)
        t, r = jnp.where(up, tiles - 1, 0), jnp.where(up, 6, 0)
        for k, ref in enumerate((e_ref, h_ref, m_ref)):
            src = ref.at[:, t, :, pl.ds(r, 2), :] if k == 2 else ref.at[:, :, t, :, pl.ds(r, 2), :]
            dst = y_bufs[3 * i + k]
            dst = dst.reshape(*dst.shape[:-2], nx, lanes, 8, 128)
            start(src, dst.at[:, :, pl.ds(0, 2), :] if k == 2 else dst.at[:, :, :, pl.ds(0, 2), :])
    for i, odd in enumerate(xs):
        first = pl.ds(jnp.where(sends_up(gx, odd), nx - 2, 0), 2)
        for k, ref in enumerate((e_ref, h_ref, m_ref)):
            start(ref.at[first] if k == 2 else ref.at[:, first], x_bufs[3 * i + k])
    start(perm_ref, perm_s)
    copies.pop().wait()
    table = coef_table(perm_s)
    lane = lax.broadcasted_iota(jnp.int32, (8, 128), 1)
    lane_n = lax.broadcasted_iota(jnp.int32, (nx, 128), 1)

    def z_up(v, lane):
        out = []
        for z in range(lanes):
            after = pltpu.roll(v[z + 1], 127, 1) if z + 1 < lanes else jnp.zeros_like(v[z])
            out.append(jnp.where(lane < 127, pltpu.roll(v[z], 127, 1), after))
        return out

    def row_up(v):
        rows = v.shape[0]
        row = lax.broadcasted_iota(jnp.int32, v.shape, 0)
        return jnp.where(row < rows - 1, pltpu.roll(v, rows - 1, 0), 0.0)

    step = lanes * 8
    for i, odd in enumerate(ys):
        for copy in copies[3 * i : 3 * i + 3]:
            copy.wait()
        up = sends_up(gy, odd)
        near, far = jnp.where(up, 1, 0), jnp.where(up, 0, 1)
        down = jnp.where(up, 0.0, magnetic_step)
        e_b, h_b, m_b = y_bufs[3 * i : 3 * i + 3]
        out = outs[len(xs) + i]

        def at(ref, c, which):
            return [ref[c, pl.ds(z * 8 + which, nx, stride=step), :] for z in range(lanes)]

        e_n = [at(e_b, c, near) for c in range(3)]
        h_n = [at(h_b, c, near) for c in range(3)]
        ex_f, ey_f, ez_f = (at(e_b, c, far) for c in range(3))
        hx_f, hz_f = at(h_b, 0, far), at(h_b, 2, far)
        ey_z = z_up(ey_f, lane_n)
        for z in range(lanes):
            for c in range(3):
                out[c * lanes + z] = e_n[c][z]
            out[3 * lanes + z] = h_n[0][z] - down * ez_f[z]
            out[4 * lanes + z] = h_n[1][z]
            out[5 * lanes + z] = h_n[2][z] + down * ex_f[z]
            out[6 * lanes + z] = coef_of(m_b[pl.ds(z * 8 + near, nx, stride=step), :], table)
            out[7 * lanes + z] = hx_f[z] + magnetic_step * (ez_f[z] + (ey_z[z] - ey_f[z]))
            out[8 * lanes + z] = hz_f[z] - magnetic_step * ((row_up(ey_f[z]) - ey_f[z]) + ex_f[z])
        out[9 * lanes] = ey_f[0]
    for i, odd in enumerate(xs):
        for copy in copies[3 * (len(ys) + i) : 3 * (len(ys) + i) + 3]:
            copy.wait()
        up = sends_up(gx, odd)
        near, far = jnp.where(up, 1, 0), jnp.where(up, 0, 1)
        down = jnp.where(up, 0.0, magnetic_step)
        e_b, h_b, m_b = x_bufs[3 * i : 3 * i + 3]
        out = outs[i]

        def put(k, t, z, v):
            out[pl.ds(k * plane + (t * lanes + z) * 8, 8), :] = v

        ex_y = [
            row_up(jnp.concatenate([e_b[0, far, t, z] for t in range(tiles)], axis=0))
            for z in range(lanes)
        ]
        for t in range(tiles):
            ex_z = z_up([e_b[0, far, t, z] for z in range(lanes)], lane)
            for z in range(lanes):
                ex_f, ey_f, ez_f = (e_b[c, far, t, z] for c in range(3))
                for c in range(3):
                    put(c, t, z, e_b[c, near, t, z])
                put(3, t, z, h_b[0, near, t, z])
                put(4, t, z, h_b[1, near, t, z] + down * ez_f)
                put(5, t, z, h_b[2, near, t, z] - down * ey_f)
                put(6, t, z, coef_of(m_b[near, t, z], table))
                put(7, t, z, h_b[1, far, t, z] - magnetic_step * ((ex_z[z] - ex_f) + ez_f))
                ex_up = ex_y[z][t * 8 : t * 8 + 8]
                put(8, t, z, h_b[2, far, t, z] + magnetic_step * (ey_f + (ex_up - ex_f)))
            out[pl.ds(9 * plane + t * 8, 8), :] = e_b[0, far, t, 0]
        for j, odd_y in enumerate(ys):
            up = sends_up(gy, odd_y)
            t = jnp.where(up, tiles - 1, 0)
            rows = (jnp.where(up, 7, 0), jnp.where(up, 6, 1))
            out = outs[len(xs) + len(ys) + i * len(ys) + j]
            for z in range(lanes):
                for f in range(FIELDS):
                    for k in range(4):
                        where = (near, far)[k // 2], t, z, pl.ds(rows[k % 2], 1)
                        if f < 6:
                            line = (e_b, h_b)[f // 3][(f % 3, *where)]
                        else:
                            line = coef_of(m_b[where], table)
                        out[z, pl.ds(4 * f + k, 1), :] = line


def turn_ends(parts, lane, first_field, after_field):
    out = None
    for k in range(first_field, after_field):
        first, last = parts(k)
        turned = pltpu.roll(jnp.where(lane < 64, first, last), 8 * k + 4, 1)
        out = turned if out is None else jnp.where(lane >= 8 * k, turned, out)
    return out


def own_ends(dims, e_v, h_v, m_v, snap_hbm, perm_ref, coef_v, packed, snap_ref, sems):
    nx, ny, nz = dims
    lanes = nz // 128
    step = ny + HALO
    copies = []
    for t in range(STEPS + 1):
        for c in range(3):
            copy = pltpu.make_async_copy(snap_hbm.at[t, c], snap_ref.at[t, c], sems.at[3 * t + c])
            copy.start()
            copies.append(copy)
    table = coef_table(perm_ref)
    lane = lax.broadcasted_iota(jnp.int32, (8, 128), 1)
    tiles = ny // 8

    def fields(x, carry):
        for t in range(tiles):
            here = [
                pl.ds(pl.multiple_of(((x * tiles + t) * lanes + z) * 8, 8), 8) for z in range(lanes)
            ]
            for z in range(lanes):
                coef_v[here[z], :] = coef_of(m_v[here[z], :], table)

            def parts(k):
                if k < 3:
                    return e_v[k, here[0], :], e_v[k, here[-1], :]
                if k < 6:
                    return h_v[k - 3, here[0], :], h_v[k - 3, here[-1], :]
                return coef_v[here[0], :], coef_v[here[-1], :]

            row = pl.multiple_of((x + 2) * step + HALO + t * 8, 8)
            packed[pl.ds(row, 8), :] = turn_ends(parts, lane, 0, FIELDS)
        return carry

    lax.fori_loop(0, nx, fields, 0, unroll=4)

    for copy in copies:
        copy.wait()

    def changes(x, carry):
        index = pl.ds(pl.multiple_of(x * ny, ny), ny)
        change = []
        for c in range(3):
            s = [
                [
                    snap_ref[t, c, index, z * 128 : z * 128 + 128].astype(jnp.float32)
                    for z in (0, lanes - 1)
                ]
                for t in range(STEPS + 1)
            ]
            change.append([[s[t][z] - s[t + 1][z] for z in range(2)] for t in range(STEPS)])
        for t in range(tiles):

            def parts(k):
                pair = change[(k - FIELDS) % 3][1 - (k - FIELDS) // 3]
                return tuple(v[t * 8 : t * 8 + 8] for v in pair)

            here = pl.ds(pl.multiple_of((x + 2) * step + HALO + t * 8, 8), 8)
            after = turn_ends(parts, lane, FIELDS, FIELDS + 6)
            packed[here, :] = jnp.where(lane < 8 * FIELDS, packed[here, :], after)
        return carry

    lax.fori_loop(0, nx, changes, 0, unroll=4)


def unpack_faces(dims, sizes, own_packed, *refs):
    nx, ny, nz = dims
    lanes = nz // 128
    tiles = ny // 8
    plane = ny * lanes
    step = ny + HALO
    gx, gy = lax.axis_index("gx"), lax.axis_index("gy")
    xs, ys = swaps(sizes[0]), swaps(sizes[1])
    n_msgs = len(xs) + len(ys) + len(xs) * len(ys)
    msgs = refs[:n_msgs]
    xh, yh, own_t, up_ref, down_ref, packed, x_raw, y_raw = refs[n_msgs:]
    xh[...] = jnp.zeros(xh.shape, jnp.float32)
    x_raw[...] = jnp.zeros(x_raw.shape, jnp.float32)
    y_raw[...] = jnp.zeros(y_raw.shape, jnp.float32)
    for f in range(FIELDS):
        for z in range(lanes):
            if len(ys) < 2 or f < 3:
                yh[f, z] = jnp.zeros(yh.shape[2:], jnp.float32)
            else:
                for p in (0, 1, nx + 2, nx + 3):
                    yh[f, z, pl.ds(p * HALO, HALO), :] = jnp.zeros((HALO, 128), jnp.float32)

    def planes(odd):
        high = sends_up(gx, odd)
        return jnp.where(high, 2, 1), jnp.where(high, 3, 0)

    def lines(odd):
        high = sends_up(gy, odd)
        return jnp.where(high, 0, HALO - 1), jnp.where(high, 1, HALO - 2)

    for i, odd in enumerate(xs):
        ok = has_partner(gx, sizes[0], odd)
        near, far = planes(odd)
        msg = msgs[i]
        for t in range(tiles):
            for z in range(lanes):
                for k, f in enumerate((0, 1, 2, 3, 4, 5, 6, 4, 5)):
                    q = near if k < FIELDS else far
                    xh[f, z, pl.ds(pl.multiple_of(q * ny + t * 8, 8), 8), :] = jnp.where(
                        ok, msg[pl.ds(k * plane + (t * lanes + z) * 8, 8), :], 0.0
                    )
            x_raw[pl.ds(pl.multiple_of(far * ny + t * 8, 8), 8), :] = jnp.where(
                ok & (far == 0), msg[pl.ds(9 * plane + t * 8, 8), :], 0.0
            )
    for i, odd in enumerate(ys):
        ok = has_partner(gy, sizes[1], odd)
        near, far = lines(odd)
        msg = msgs[len(xs) + i]
        for z in range(lanes):
            for k, f in enumerate((0, 1, 2, 3, 4, 5, 6, 3, 5)):
                r = near if k < FIELDS else far
                yh[f, z, pl.ds(2 * HALO + r, nx, stride=HALO), :] = jnp.where(
                    ok, msg[k * lanes + z], 0.0
                )
        y_raw[pl.ds(2 * HALO + far, nx, stride=HALO), :] = jnp.where(
            ok & (far == HALO - 2), msg[9 * lanes], 0.0
        )
    for i, ox in enumerate(xs):
        for j, oy in enumerate(ys):
            ok = has_partner(gx, sizes[0], ox) & has_partner(gy, sizes[1], oy)
            px, py = planes(ox), lines(oy)
            px = [jnp.where(q < 2, q, q + nx) for q in px]
            msg = msgs[len(xs) + len(ys) + i * len(ys) + j]
            for z in range(lanes):
                for f in range(FIELDS):
                    for k in range(4):
                        yh[f, z, pl.ds(px[k // 2] * HALO + py[k % 2], 1), :] = jnp.where(
                            ok, msg[z, pl.ds(4 * f + k, 1), :], 0.0
                        )

    lane = lax.broadcasted_iota(jnp.int32, (8, 128), 1)
    upper = lax.broadcasted_iota(jnp.int32, (8, 128), 0) < HALO // 2

    def halo_rows(p, before, here):
        def tile(f, z):
            if f == FIELDS:
                return y_raw[here, :]
            return jnp.where(upper, yh[f, z, before, :], yh[f, z, here, :])

        packed[pl.ds(p * step if isinstance(p, int) else pl.multiple_of(p * step, 8), HALO), :] = (
            turn_ends(lambda f: (tile(f, 0), tile(f, lanes - 1)), lane, 0, FIELDS + 1)
        )

    def one(p, carry):
        halo_rows(
            p,
            pl.ds(pl.multiple_of((p - 1) * HALO, 8), HALO),
            pl.ds(pl.multiple_of(p * HALO, 8), HALO),
        )
        return carry

    halo_rows(0, pl.ds(0, HALO), pl.ds(0, HALO))
    lax.fori_loop(1, nx + 4, one, 0, unroll=5)
    last = pl.ds((nx + 3) * HALO, HALO)
    halo_rows(nx + 4, last, last)
    for q, p in enumerate((0, 1, nx + 2, nx + 3)):
        for t in range(tiles):
            index = pl.ds(q * ny + t * 8, 8)

            def parts(f):
                if f == FIELDS:
                    return x_raw[index, :], x_raw[index, :]
                return xh[f, 0, index, :], xh[f, lanes - 1, index, :]

            packed[pl.ds(p * step + HALO + t * 8, 8), :] = turn_ends(parts, lane, 0, FIELDS + 1)
    for x in range(nx):
        index = pl.ds((x + 2) * step + HALO, ny)
        packed[index, :] = own_packed[index, :]
    after = (nx + 4) * step + HALO
    padded = packed.shape[0]
    if padded > after:
        packed[after:, :] = jnp.zeros((padded - after, 128), jnp.float32)
    for b in range(padded // 128):
        here = pl.ds(b * 128, 128)
        block = jnp.transpose(packed[here, :])
        own_t[:, here] = block
        for f in range(FIELDS):
            up_ref[f : f + 1, here] = block[8 * f + 3 : 8 * f + 4, :]
            up_ref[8 + f : 9 + f, here] = block[8 * f + 2 : 8 * f + 3, :]
            down = [block[8 * f + 4 + k : 8 * f + 5 + k, :] for k in range(2)]
            if f < 2:
                at = lax.broadcasted_iota(jnp.int32, (1, 128), 1) + b * 128
                raw = (at >= HALO) & (at < step) if f == 0 else lax.rem(at, step) < HALO
                tail = [block[8 * FIELDS + 4 + k : 8 * FIELDS + 5 + k, :] for k in range(2)]
                down = [down[k] + jnp.where(raw, tail[k], 0.0) for k in range(2)]
            down_ref[f : f + 1, here] = down[0]
            down_ref[8 + f : 9 + f, here] = down[1]
    for row in (7, 15):
        up_ref[row : row + 1, :] = jnp.zeros((1, padded), jnp.float32)
        down_ref[row : row + 1, :] = jnp.zeros((1, padded), jnp.float32)


def columns_of(lines, nx, ny):
    spread, pick = [], []
    for line, step, first in lines:
        size = line.shape[1]
        at = lax.broadcasted_iota(jnp.int32, (ny, size), 1) - first
        y = lax.broadcasted_iota(jnp.int32, (ny, size), 0)
        ok = (at >= 0) & (at < nx * step) & (lax.rem(at, step) == y)
        spread.append(jnp.where(ok, line, 0.0))
        at = lax.broadcasted_iota(jnp.int32, (nx, size), 1) - first
        x = lax.broadcasted_iota(jnp.int32, (nx, size), 0) * step
        pick.append(jnp.where((at >= x) & (at < x + step), 1.0, 0.0))
    left = jnp.concatenate(spread, axis=1)
    thirds = []
    for _ in range(3):
        part = left.astype(jnp.bfloat16)
        left = left - part.astype(jnp.float32)
        thirds.append(part)
    out = lax.dot_general(
        jnp.concatenate(thirds, axis=0),
        jnp.concatenate(pick, axis=1).astype(jnp.bfloat16),
        (((1,), (1,)), ((), ())),
        preferred_element_type=jnp.float32,
    )
    return out[0:ny] + (out[ny : 2 * ny] + out[2 * ny : 3 * ny])


def find_ports(dims, sizes, ports_ref):
    nx, ny, nz = dims
    gx, gy, gz = lax.axis_index("gx"), lax.axis_index("gy"), lax.axis_index("gz")
    plane_cells = (ny * sizes[1]) * (nz * sizes[2])
    line_cells = nz * sizes[2]
    found = []
    for q in range(ports_ref.shape[0]):
        cell = ports_ref[q]
        x = lax.div(cell, plane_cells) - gx * nx
        y = lax.rem(lax.div(cell, line_cells), ny * sizes[1]) - gy * ny
        z = lax.rem(cell, line_cells) - gz * nz
        found.append((x, y, z))
    return found


def march(dims, sizes, e_v, h_v, coef_v, xh, yh, snap_ref, ports_ref, amps_ref, *refs):
    nx, ny, nz = dims
    lanes = nz // 128
    tiles = ny // 8
    step = ny + HALO
    e_s, h_s, line_ref, e1, h1, h2, half_ref, struck, clean, sums = refs
    gx, gy = lax.axis_index("gx"), lax.axis_index("gy")
    row = lax.broadcasted_iota(jnp.int32, (step, nz), 0)
    lane = lax.broadcasted_iota(jnp.int32, (step, nz), 1)
    inside = (row < ny) | ((row < ny + 2) & (gy < sizes[1] - 1)) | ((row >= ny + 4) & (gy > 0))
    half_ref[...] = jnp.where(inside, magnetic_step, 0.0)
    for k in range(2):
        clean[k] = jnp.where((lane[:ny] > k) & (lane[:ny] < nz - 1 - k), 1.0, 0.0)

    planes_struck = []
    for q, (x, y, z) in enumerate(find_ports(dims, sizes, ports_ref)):
        near = (y >= -2) & (y < ny + 2) & (z >= 0) & (z < nz)
        at = jnp.where(y < 0, y + step, y)
        struck[q] = jnp.where((row == at) & (lane == z) & near, 1.0, 0.0)
        planes_struck.append(x + 2)

    def spot(x, t, z):
        index = ((x * tiles + t) * lanes + z) * 8
        return pl.ds(index if isinstance(index, int) else pl.multiple_of(index, 8), 8)

    def own_tile(f, p, t, z):
        if isinstance(p, int) and not 2 <= p < nx + 2:
            return xh[f, z, pl.ds((p if p < 2 else p - nx) * ny + t * 8, 8), :]
        if f < 3:
            return e_v[f, spot(p - 2, t, z), :]
        if f < 6:
            return h_v[f - 3, spot(p - 2, t, z), :]
        return coef_v[spot(p - 2, t, z), :]

    def aligned(index):
        return index if isinstance(index, int) else pl.multiple_of(index, 8)

    def load(f, p):
        columns = []
        for z in range(lanes):
            column = [own_tile(f, p, t, z) for t in range(tiles)]
            column.append(yh[f, z, pl.ds(aligned(p * HALO), HALO), :])
            columns.append(jnp.concatenate(column, axis=0))
        return jnp.concatenate(columns, axis=1)

    def load_own(f, p):
        return jnp.concatenate(
            [
                jnp.concatenate([own_tile(f, p, t, z) for t in range(tiles)], axis=0)
                for z in range(lanes)
            ],
            axis=1,
        )

    def put(ref, f, x, v):
        for t in range(tiles):
            for z in range(lanes):
                ref[f, spot(x, t, z), :] = v[t * 8 : t * 8 + 8, z * 128 : z * 128 + 128]

    def y_up(v):
        return pltpu.roll(v, step - 1, 0)

    def y_down(v):
        return pltpu.roll(v, 1, 0)

    def z_up(v):
        return pltpu.roll(v, nz - 1, 1)

    def z_down(v):
        return pltpu.roll(v, 1, 1)

    def new_h(half, ex, ey, ez, ey_x, ez_x, hx, hy, hz):
        cx = (y_up(ez) - ez) - (z_up(ey) - ey)
        cy = (z_up(ex) - ex) - (ez_x - ez)
        cz = (ey_x - ey) - (y_up(ex) - ex)
        return hx - half * cx, hy - half * cy, hz - half * cz

    def curl_h(hx, hy, hz, hy_x, hz_x):
        cx = (hz - y_down(hz)) - (hy - z_down(hy))
        cy = (hx - z_down(hx)) - (hz - hz_x)
        cz = (hy - hy_x) - (hx - y_down(hx))
        return cx, cy, cz

    def half_of(p):
        if isinstance(p, int) and p < 2:
            return half_ref[...] * jnp.where(gx == 0, 0.0, 1.0)
        if isinstance(p, int) and p >= nx + 2:
            return half_ref[...] * jnp.where(gx == sizes[0] - 1, 0.0, 1.0)
        return half_ref[...]

    def first_h(p):
        e = [load(f, p) for f in range(3)]
        h = [load(3 + f, p) for f in range(3)]
        out = new_h(half_of(p), *e, load(1, p + 1), load(2, p + 1), *h)
        for f in range(3):
            h1[f, p] = out[f]

    def first_e(p):
        e = [load(f, p) for f in range(3)]
        curl = curl_h(*[h1[f, p] for f in range(3)], h1[1, p - 1], h1[2, p - 1])
        coef = load(6, p)
        out = [e[f] + coef * curl[f] for f in range(3)]
        for f in range(3):
            e1[f, p] = out[f]

    def second_h(p):
        e = [e1[f, p] for f in range(3)]
        h = [h1[f, p] for f in range(3)]
        out = new_h(half_of(p), *e, e1[1, p + 1], e1[2, p + 1], *h)
        for f in range(3):
            h2[f, p] = out[f]

    def second_e(p):
        h = [h2[f, p] for f in range(3)]
        curl = curl_h(*h, h2[1, p - 1], h2[2, p - 1])
        coef = load_own(6, p)
        old = [e1[f, p, 0:ny, 0:nz] for f in range(3)]
        new = [old[f] + coef * curl[f][:ny, :nz] for f in range(3)]
        x = p - 2
        index = pl.ds(aligned(x * ny), ny)
        total = None
        for f in range(3):
            put(e_s, f, x, new[f])
            put(h_s, f, x, h[f][:ny, :nz])
            s = [snap_ref[t, f, index, :].astype(jnp.float32) for t in range(STEPS + 1)]
            one = [old[f] * (s[0] - s[1]), new[f] * (s[1] - s[2])]
            total = one if total is None else [total[k] + one[k] for k in range(2)]
        total = total[0] * clean[0] + total[1] * clean[1]
        folded = total[:, 0:128]
        for at in range(128, nz, 128):
            folded = folded + total[:, at : at + 128]
        sums[index, :] = folded

    def strike(p):
        dynamic = not isinstance(p, int)
        first, second = p - 1, p - 4
        hit = None
        for at in planes_struck:
            here = (at == first) | (at == second)
            hit = here if hit is None else hit | here

        @pl.when(hit)
        def _():
            for q, at in enumerate(planes_struck):
                if dynamic or 1 <= first <= nx + 2:
                    amp = jnp.where(at == first, amps_ref[0, q], 0.0)
                    e1[2, first] = e1[2, first] + struck[q] * amp
                if dynamic or 2 <= second <= nx + 1:
                    x = second - 2
                    amp = jnp.where(at == second, amps_ref[1, q], 0.0)
                    index = pl.ds(aligned(x * ny), ny)
                    s = [snap_ref[t, 2, index, :].astype(jnp.float32) for t in (1, 2)]
                    folded = jnp.zeros((ny, 128), jnp.float32)
                    for z in range(lanes):
                        here = slice(z * 128, z * 128 + 128)
                        gain = struck[q, 0:ny, here] * amp
                        folded = folded + gain * clean[1, :, here] * (s[0] - s[1])[:, here]
                        for t in range(tiles):
                            here = spot(x, t, z)
                            e_s[2, here, :] = e_s[2, here, :] + gain[t * 8 : t * 8 + 8]
                    sums[index, :] = sums[index, :] + folded

    def one(p):
        dynamic = not isinstance(p, int)
        if dynamic or 2 <= p - 4 <= nx + 1:
            second_e(p - 4)
        if dynamic or 1 <= p - 3 <= nx + 1:
            second_h(p - 3)
        if dynamic or 1 <= p - 1 <= nx + 2:
            first_e(p - 1)
        if dynamic or 0 <= p <= nx + 2:
            first_h(p)
        strike(p)

    def body(p, carry):
        one(p)
        return carry

    for p in range(6):
        one(p)
    lax.fori_loop(6, nx + 1, body, 0, unroll=3)
    for p in range(nx + 1, nx + 6):
        one(p)
    for b in range(nx * ny // 128):
        here = pl.ds(b * 128, 128)
        line_ref[:, here] = jnp.sum(jnp.transpose(sums[here, :]), axis=0, keepdims=True)


def finish_ends(
    dims, sizes, own_t, low_ref, high_ref, line_ref, mask_ref, ports_ref, amps_ref, *refs
):
    nx, ny, nz = dims
    step = ny + HALO
    parts = sizes[2]
    ends_ref = refs[0]
    grads = refs[1 : 1 + parts]
    strips, turned, rows_ref = refs[1 + parts :]
    gx, gy, gz = lax.axis_index("gx"), lax.axis_index("gy"), lax.axis_index("gz")
    padded = own_t.shape[1]
    row = lax.broadcasted_iota(jnp.int32, (8, padded), 0)
    lane = lax.broadcasted_iota(jnp.int32, (8, padded), 1) - HALO
    has_low, has_high = gz > 0, gz < sizes[2] - 1
    for k, (msg, ok, far, near) in enumerate(((low_ref, has_low, 2, 3), (high_ref, has_high, 5, 4))):
        for f in range(FIELDS):
            strips[k, f] = own_t[8 * f : 8 * f + 8, :]
            strips[k, f, far : far + 1, :] = jnp.where(ok, msg[8 + f : 9 + f, :], 0.0)
            strips[k, f, near : near + 1, :] = jnp.where(ok, msg[f : f + 1, :], 0.0)

    at = lane + 2
    p, y = lax.div(at, step), lax.rem(at, step) - 2
    inside = ((p >= 2) | (gx > 0)) & ((p < nx + 2) | (gx < sizes[0] - 1))
    inside = inside & ((y >= 0) | (gy > 0)) & ((y < ny) | (gy < sizes[1] - 1))
    found = find_ports(dims, sizes, ports_ref)

    def x_up(v):
        return pltpu.roll(v, padded - step, 1)

    def x_down(v):
        return pltpu.roll(v, step, 1)

    def y_up(v):
        return pltpu.roll(v, padded - 1, 1)

    def y_down(v):
        return pltpu.roll(v, 1, 1)

    def z_up(v):
        return pltpu.roll(v, 7, 0)

    def z_down(v):
        return pltpu.roll(v, 1, 0)

    total = None
    results = []
    for k in range(2):
        ex, ey, ez, hx, hy, hz, coef = (strips[k, f] for f in range(FIELDS))
        first = -4 if k == 0 else nz - 4
        good = ((row >= 4) | has_low) if k == 0 else ((row < 4) | has_high)
        half = jnp.where(inside & good, magnetic_step, 0.0)
        for s in range(STEPS):
            cx = (y_up(ez) - ez) - (z_up(ey) - ey)
            cy = (z_up(ex) - ex) - (x_up(ez) - ez)
            cz = (x_up(ey) - ey) - (y_up(ex) - ex)
            hx, hy, hz = hx - half * cx, hy - half * cy, hz - half * cz
            cx = (hz - y_down(hz)) - (hy - z_down(hy))
            cy = (hx - z_down(hx)) - (hz - x_down(hz))
            cz = (hy - x_down(hy)) - (hx - y_down(hx))
            ex, ey, ez = ex + coef * cx, ey + coef * cy, ez + coef * cz
            for q, (sx, sy, sz) in enumerate(found):
                near = (sx >= -2) & (sx < nx + 2) & (sy >= -2) & (sy < ny + 2)
                hit = (row == sz - first) & (at == (sx + 2) * step + sy + 2) & near
                ez = ez + jnp.where(hit, amps_ref[s, q], 0.0)
            if k == 0:
                mine = (row == 4) | ((row == 5) & (s == 1))
            else:
                mine = (row == 3) | ((row == 2) & (s == 1))
            for c, e in enumerate((ex, ey, ez)):
                tile = FIELDS + c + 3 * (1 - s)
                one = jnp.where(mine, e * own_t[8 * tile : 8 * tile + 8, :], 0.0)
                total = one if total is None else total + one
        results.append((ex, ey, ez, hx, hy, hz))
    for c in range(6):
        rows_ref[8 * c : 8 * c + 8, :] = jnp.where(row < 4, results[1][c], results[0][c])
    line = jnp.sum(total, axis=0, keepdims=True)
    column = columns_of([(line_ref[...], ny, 0), (line, step, 2 * step + HALO)], nx, ny)
    turned[...] = column * mask_ref[...].astype(jnp.float32)
    width = ny // parts
    for shift in range(parts):
        owner = partner_of(gz, shift, parts)
        grads[shift][...] = turned[pl.ds(owner * width, width), :]
    ends_ref[...] = rows_ref[...]


def write_out(dims, e_s, h_s, ends_ref, e_out, h_out, spare, e_v, h_v, ends_t, sems):
    nx, ny, nz = dims
    lanes = nz // 128
    tiles = ny // 8
    plane = ny * lanes
    step = ny + HALO
    lane = lax.broadcasted_iota(jnp.int32, (8, 128), 1)
    spare[...] = jnp.zeros(spare.shape, jnp.float32)
    spare[0 : ends_ref.shape[0], :] = ends_ref[...]
    for b in range(spare.shape[1] // 128):
        ends_t[b * 128 : (b + 1) * 128, :] = jnp.transpose(spare[:, b * 128 : (b + 1) * 128])

    def one(x, carry):
        for t in range(tiles):
            v = ends_t[pl.ds(pl.multiple_of((x + 2) * step + HALO + t * 8, 8), 8), :]
            for c in range(6):
                src, dst = (e_s, e_v) if c < 3 else (h_s, h_v)
                placed = pltpu.roll(v, 124 - 8 * c, 1)
                for z in range(lanes):
                    here = pl.ds(pl.multiple_of(((x * tiles + t) * lanes + z) * 8, 8), 8)
                    out = src[c % 3, here, :]
                    if z == 0:
                        out = jnp.where(lane < 2, placed, out)
                    if z == lanes - 1:
                        out = jnp.where(lane >= 126, placed, out)
                    dst[c % 3, here, :] = out
        return carry

    chunk = nx // 4
    copies = []
    for c in range(4):
        lax.fori_loop(c * chunk, (c + 1) * chunk, one, 0, unroll=4)
        here = pl.ds(c * chunk * plane, chunk * plane)
        for k, (src, dst) in enumerate(((e_v, e_out), (h_v, h_out))):
            copy = pltpu.make_async_copy(src.at[:, here], dst.at[:, here], sems.at[2 * c + k])
            copy.start()
            copies.append(copy)
    for copy in copies:
        copy.wait()


def params(limit=12):
    return pltpu.CompilerParams(vmem_limit_bytes=limit * 1024 * 1024)


def body(sizes, e_adjoint, h_adjoint, snapshots, material, permittivity, design_mask, ports, amplitudes):
    permittivity = in_hbm(permittivity)
    permittivity = in_hbm(permittivity)
    dims = material.shape
    nx, ny, nz = dims
    lanes = nz // 128
    tiles = ny // 8
    plane = ny * lanes
    cells = nx * ny
    step = ny + HALO
    padded = -(-((nx + 4) * step + HALO) // 128) * 128
    f32, i32 = jnp.float32, jnp.int32
    xs, ys = swaps(sizes[0]), swaps(sizes[1])
    block, cube = jax.ShapeDtypeStruct, pltpu.VMEM

    shapes = [block((9 * plane + ny, 128), f32) for _ in xs]
    shapes += [block((9 * lanes + 1, nx, 128), f32) for _ in ys]
    shapes += [block((lanes, 4 * FIELDS, 128), f32) for _ in xs for _ in ys]
    buffers = []
    for _ in xs:
        tile = (2, tiles, lanes, 8, 128)
        buffers += [cube((3, *tile), f32), cube((3, *tile), f32), cube(tile, i32)]
    for _ in ys:
        tile = (nx * lanes * 8, 128)
        buffers += [cube((3, *tile), f32), cube((3, *tile), f32), cube(tile, i32)]
    n_copies = 3 * (len(xs) + len(ys)) + 1
    msgs = pl.pallas_call(
        functools.partial(send_faces, dims, sizes),
        out_shape=shapes,
        in_specs=[HBM, HBM, HBM, HBM],
        out_specs=[VM] * len(shapes),
        scratch_shapes=buffers
        + [pltpu.SMEM(permittivity.shape, f32), pltpu.SemaphoreType.DMA((n_copies,))],
        compiler_params=params(),
        name="send_faces",
    )(
        in_hbm(tiles_of(e_adjoint)),
        in_hbm(tiles_of(h_adjoint)),
        in_hbm(tiles_of(material)),
        permittivity,
    )
    e_v, h_v, m_v = in_vmem(tiled(e_adjoint)), in_vmem(tiled(h_adjoint)), in_vmem(tiled(material))
    snaps = in_hbm(snapshots.reshape(STEPS + 1, 3, cells, nz))
    coef_v, own_packed, s = pl.pallas_call(
        functools.partial(own_ends, dims),
        out_shape=[cube(m_v.shape, f32), cube((padded, 128), f32), cube(snaps.shape, snaps.dtype)],
        in_specs=[VM, VM, VM, HBM, SM],
        out_specs=[VM] * 3,
        scratch_shapes=[pltpu.SemaphoreType.DMA((3 * (STEPS + 1),))],
        compiler_params=params(),
        cost_estimate=pl.CostEstimate(flops=10**7, bytes_accessed=4 * 10**6, transcendentals=0),
        name="own_ends",
    )(e_v, h_v, m_v, snaps, permittivity)

    both = ("gx", "gy")
    tables = [("gx", list(enumerate(swap_table(sizes[0], o)))) for o in xs]
    tables += [("gy", list(enumerate(swap_table(sizes[1], o)))) for o in ys]
    for ox in xs:
        for oy in ys:
            tx, ty = swap_table(sizes[0], ox), swap_table(sizes[1], oy)
            pairs = [
                (x * sizes[1] + y, tx[x] * sizes[1] + ty[y])
                for x in range(sizes[0])
                for y in range(sizes[1])
            ]
            tables.append((both, pairs))
    got = [lax.ppermute(msg, axis, pairs) for msg, (axis, pairs) in zip(msgs, tables)]

    xh, yh, own_t, up, down = pl.pallas_call(
        functools.partial(unpack_faces, dims, sizes),
        out_shape=[
            cube((FIELDS, lanes, 4 * ny, 128), f32),
            cube((FIELDS, lanes, (nx + 4) * HALO, 128), f32),
            cube((128, padded), f32),
            block((16, padded), f32),
            block((16, padded), f32),
        ],
        in_specs=[VM] * (1 + len(got)),
        out_specs=[VM] * 5,
        scratch_shapes=[
            pltpu.VMEM((padded, 128), f32),
            pltpu.VMEM((4 * ny, 128), f32),
            pltpu.VMEM(((nx + 4) * HALO, 128), f32),
        ],
        compiler_params=params(),
        name="unpack_faces",
    )(own_packed, *got)

    parts = sizes[2]
    low = lax.ppermute(up, "gz", [(i, (i + 1) % parts) for i in range(parts)])
    high = lax.ppermute(down, "gz", [(i, (i - 1) % parts) for i in range(parts)])

    ported = ports.shape[0]
    e_s, h_s, line = pl.pallas_call(
        functools.partial(march, dims, sizes),
        out_shape=[cube(e_v.shape, f32), cube(h_v.shape, f32), block((1, cells), f32)],
        in_specs=[VM] * 6 + [SM, SM],
        out_specs=[VM] * 3,
        scratch_shapes=[
            pltpu.VMEM((3, nx + 4, step, nz), f32),
            pltpu.VMEM((3, nx + 4, step, nz), f32),
            pltpu.VMEM((3, nx + 4, step, nz), f32),
            pltpu.VMEM((step, nz), f32),
            pltpu.VMEM((ported, step, nz), f32),
            pltpu.VMEM((2, ny, nz), f32),
            pltpu.VMEM((cells, 128), f32),
        ],
        compiler_params=params(24),
        cost_estimate=pl.CostEstimate(flops=4 * 10**7, bytes_accessed=10**7, transcendentals=0),
        name="march",
    )(e_v, h_v, coef_v, xh, yh, s, ports, amplitudes)
    ends, *chunks = pl.pallas_call(
        functools.partial(finish_ends, dims, sizes),
        out_shape=[cube((48, padded), f32)] + [block((ny // parts, nx), f32)] * parts,
        in_specs=[VM] * 5 + [SM, SM],
        out_specs=[VM] * (1 + parts),
        scratch_shapes=[
            pltpu.VMEM((2, FIELDS, 8, padded), f32),
            pltpu.VMEM((ny, nx), f32),
            pltpu.VMEM((48, padded), f32),
        ],
        compiler_params=params(),
        name="finish_ends",
    )(own_t, low, high, line, design_mask.T, ports, amplitudes)
    e_out, h_out = pl.pallas_call(
        functools.partial(write_out, dims),
        out_shape=[block(e_v.shape, f32), block(h_v.shape, f32)],
        in_specs=[VM] * 3,
        out_specs=[HBM] * 2,
        scratch_shapes=[
            pltpu.VMEM((128, padded), f32),
            pltpu.VMEM(e_v.shape, f32),
            pltpu.VMEM(h_v.shape, f32),
            pltpu.VMEM((padded, 128), f32),
            pltpu.SemaphoreType.DMA((8,)),
        ],
        compiler_params=params(),
        cost_estimate=pl.CostEstimate(flops=10**7, bytes_accessed=8 * 10**6, transcendentals=0),
        name="write_out",
    )(e_s, h_s, ends)
    gradient = chunks[0]
    for shift in range(1, parts):
        gradient = gradient + lax.ppermute(
            chunks[shift], "gz", [(i, partner_of(i, shift, parts)) for i in range(parts)]
        )
    return untiled(e_out, dims), untiled(h_out, dims), gradient.T


def solution(mesh):
    placed = (
        P(None, "gx", "gy", "gz"),
        P(None, "gx", "gy", "gz"),
        P(None, None, "gx", "gy", "gz"),
        P("gx", "gy", "gz"),
        P(),
        P("gx", "gy"),
        P(),
        P(),
    )
    sizes = tuple(mesh.shape[axis] for axis in ("gx", "gy", "gz"))
    return jax.shard_map(
        functools.partial(body, sizes),
        mesh=mesh,
        in_specs=placed,
        out_specs=(P(None, "gx", "gy", "gz"), P(None, "gx", "gy", "gz"), P("gx", ("gy", "gz"))),
        check_vma=False,
    )
```

```python
import functools

import jax
import jax.numpy as jnp
from jax import lax
from jax.experimental import pallas as pl
from jax.experimental.pallas import tpu as pltpu
from jax.sharding import PartitionSpec as P

STEPS = 2
FIELDS = 7
HALO = 8

magnetic_step = 0.5
electric_step = 0.5

VM = pl.BlockSpec(memory_space=pltpu.VMEM)
SM = pl.BlockSpec(memory_space=pltpu.SMEM)
ANY = pl.BlockSpec(memory_space=pl.ANY)


HBM = pl.BlockSpec(memory_space=pltpu.HBM)


def in_hbm(array):
    return pltpu.with_memory_space_constraint(array, pltpu.HBM)


def in_vmem(array):
    return pltpu.with_memory_space_constraint(array, pltpu.VMEM)


def swap_table(size, odd):
    table = list(range(size))
    for i in range(odd, size - 1, 2):
        table[i], table[i + 1] = i + 1, i
    return table


def swaps(size):
    return [odd for odd in (0, 1) if odd + 1 < size]


def partner_of(index, shift, size):
    if size & (size - 1) == 0:
        return index ^ shift
    return (index + shift) % size


def sends_up(index, odd):
    return lax.rem(index, 2) == odd


def has_partner(index, size, odd):
    up = sends_up(index, odd)
    return (up & (index + 1 < size)) | (jnp.logical_not(up) & (index >= 1))


def coef_table(perm_ref):
    return [
        electric_step / jnp.full((1, 1), perm_ref[i], jnp.float32) for i in range(perm_ref.shape[0])
    ]


def coef_of(material, table):
    out = jnp.zeros(material.shape, jnp.float32)
    for i, value in enumerate(table):
        out = jnp.where(material == i, value, out)
    return out


def tiled(array):
    *lead, nx, ny, nz = array.shape
    n = len(lead)
    split = array.reshape(*lead, nx, ny // 8, 8, nz // 128, 128)
    order = tuple(range(n + 2)) + (n + 3, n + 2, n + 4)
    return split.transpose(order).reshape(*lead, nx * ny * nz // 128, 128)


def untiled(array, dims):
    nx, ny, nz = dims
    lead = array.shape[:-2]
    n = len(lead)
    split = array.reshape(*lead, nx, ny // 8, nz // 128, 8, 128)
    order = tuple(range(n + 2)) + (n + 3, n + 2, n + 4)
    return split.transpose(order).reshape(*lead, nx, ny, nz)


def tiles_of(array):
    *lead, nx, ny, nz = array.shape
    return tiled(array).reshape(*lead, nx, ny // 8, nz // 128, 8, 128)


def send_faces(dims, sizes, e_ref, h_ref, m_ref, perm_ref, *refs):
    nx, ny, nz = dims
    lanes = nz // 128
    tiles = ny // 8
    plane = ny * lanes
    gx, gy = lax.axis_index("gx"), lax.axis_index("gy")
    xs, ys = swaps(sizes[0]), swaps(sizes[1])
    n_out = len(xs) + len(ys) + len(xs) * len(ys)
    outs, refs = refs[:n_out], refs[n_out:]
    x_bufs, refs = refs[: 3 * len(xs)], refs[3 * len(xs) :]
    y_bufs, (perm_s, sems) = refs[: 3 * len(ys)], refs[3 * len(ys) :]
    copies = []

    def start(src, dst):
        copy = pltpu.make_async_copy(src, dst, sems.at[len(copies)])
        copy.start()
        copies.append(copy)

    for i, odd in enumerate(ys):
        up = sends_up(gy, odd)
        t, r = jnp.where(up, tiles - 1, 0), jnp.where(up, 6, 0)
        for k, ref in enumerate((e_ref, h_ref, m_ref)):
            src = ref.at[:, t, :, pl.ds(r, 2), :] if k == 2 else ref.at[:, :, t, :, pl.ds(r, 2), :]
            dst = y_bufs[3 * i + k]
            dst = dst.reshape(*dst.shape[:-2], nx, lanes, 8, 128)
            start(src, dst.at[:, :, pl.ds(0, 2), :] if k == 2 else dst.at[:, :, :, pl.ds(0, 2), :])
    for i, odd in enumerate(xs):
        first = pl.ds(jnp.where(sends_up(gx, odd), nx - 2, 0), 2)
        for k, ref in enumerate((e_ref, h_ref, m_ref)):
            start(ref.at[first] if k == 2 else ref.at[:, first], x_bufs[3 * i + k])
    start(perm_ref, perm_s)
    copies.pop().wait()
    table = coef_table(perm_s)
    lane = lax.broadcasted_iota(jnp.int32, (8, 128), 1)
    lane_n = lax.broadcasted_iota(jnp.int32, (nx, 128), 1)

    def z_up(v, lane):
        out = []
        for z in range(lanes):
            after = pltpu.roll(v[z + 1], 127, 1) if z + 1 < lanes else jnp.zeros_like(v[z])
            out.append(jnp.where(lane < 127, pltpu.roll(v[z], 127, 1), after))
        return out

    def row_up(v):
        rows = v.shape[0]
        row = lax.broadcasted_iota(jnp.int32, v.shape, 0)
        return jnp.where(row < rows - 1, pltpu.roll(v, rows - 1, 0), 0.0)

    step = lanes * 8
    for i, odd in enumerate(ys):
        for copy in copies[3 * i : 3 * i + 3]:
            copy.wait()
        up = sends_up(gy, odd)
        near, far = jnp.where(up, 1, 0), jnp.where(up, 0, 1)
        down = jnp.where(up, 0.0, magnetic_step)
        e_b, h_b, m_b = y_bufs[3 * i : 3 * i + 3]
        out = outs[len(xs) + i]

        def at(ref, c, which):
            return [ref[c, pl.ds(z * 8 + which, nx, stride=step), :] for z in range(lanes)]

        e_n = [at(e_b, c, near) for c in range(3)]
        h_n = [at(h_b, c, near) for c in range(3)]
        ex_f, ey_f, ez_f = (at(e_b, c, far) for c in range(3))
        hx_f, hz_f = at(h_b, 0, far), at(h_b, 2, far)
        ey_z = z_up(ey_f, lane_n)
        for z in range(lanes):
            for c in range(3):
                out[c * lanes + z] = e_n[c][z]
            out[3 * lanes + z] = h_n[0][z] - down * ez_f[z]
            out[4 * lanes + z] = h_n[1][z]
            out[5 * lanes + z] = h_n[2][z] + down * ex_f[z]
            out[6 * lanes + z] = coef_of(m_b[pl.ds(z * 8 + near, nx, stride=step), :], table)
            out[7 * lanes + z] = hx_f[z] + magnetic_step * (ez_f[z] + (ey_z[z] - ey_f[z]))
            out[8 * lanes + z] = hz_f[z] - magnetic_step * ((row_up(ey_f[z]) - ey_f[z]) + ex_f[z])
        out[9 * lanes] = ey_f[0]
    for i, odd in enumerate(xs):
        for copy in copies[3 * (len(ys) + i) : 3 * (len(ys) + i) + 3]:
            copy.wait()
        up = sends_up(gx, odd)
        near, far = jnp.where(up, 1, 0), jnp.where(up, 0, 1)
        down = jnp.where(up, 0.0, magnetic_step)
        e_b, h_b, m_b = x_bufs[3 * i : 3 * i + 3]
        out = outs[i]

        def put(k, t, z, v):
            out[pl.ds(k * plane + (t * lanes + z) * 8, 8), :] = v

        ex_y = [
            row_up(jnp.concatenate([e_b[0, far, t, z] for t in range(tiles)], axis=0))
            for z in range(lanes)
        ]
        for t in range(tiles):
            ex_z = z_up([e_b[0, far, t, z] for z in range(lanes)], lane)
            for z in range(lanes):
                ex_f, ey_f, ez_f = (e_b[c, far, t, z] for c in range(3))
                for c in range(3):
                    put(c, t, z, e_b[c, near, t, z])
                put(3, t, z, h_b[0, near, t, z])
                put(4, t, z, h_b[1, near, t, z] + down * ez_f)
                put(5, t, z, h_b[2, near, t, z] - down * ey_f)
                put(6, t, z, coef_of(m_b[near, t, z], table))
                put(7, t, z, h_b[1, far, t, z] - magnetic_step * ((ex_z[z] - ex_f) + ez_f))
                ex_up = ex_y[z][t * 8 : t * 8 + 8]
                put(8, t, z, h_b[2, far, t, z] + magnetic_step * (ey_f + (ex_up - ex_f)))
            out[pl.ds(9 * plane + t * 8, 8), :] = e_b[0, far, t, 0]
        for j, odd_y in enumerate(ys):
            up = sends_up(gy, odd_y)
            t = jnp.where(up, tiles - 1, 0)
            rows = (jnp.where(up, 7, 0), jnp.where(up, 6, 1))
            out = outs[len(xs) + len(ys) + i * len(ys) + j]
            for z in range(lanes):
                for f in range(FIELDS):
                    for k in range(4):
                        where = (near, far)[k // 2], t, z, pl.ds(rows[k % 2], 1)
                        if f < 6:
                            line = (e_b, h_b)[f // 3][(f % 3, *where)]
                        else:
                            line = coef_of(m_b[where], table)
                        out[z, pl.ds(4 * f + k, 1), :] = line


def turn_ends(parts, lane, first_field, after_field):
    out = None
    for k in range(first_field, after_field):
        first, last = parts(k)
        turned = pltpu.roll(jnp.where(lane < 64, first, last), 8 * k + 4, 1)
        out = turned if out is None else jnp.where(lane >= 8 * k, turned, out)
    return out


def own_ends(dims, e_v, h_v, m_v, snap_hbm, perm_ref, coef_v, packed, snap_ref, sems):
    nx, ny, nz = dims
    lanes = nz // 128
    step = ny + HALO
    copies = []
    for t in range(STEPS + 1):
        for c in range(3):
            copy = pltpu.make_async_copy(snap_hbm.at[t, c], snap_ref.at[t, c], sems.at[3 * t + c])
            copy.start()
            copies.append(copy)
    table = coef_table(perm_ref)
    lane = lax.broadcasted_iota(jnp.int32, (8, 128), 1)
    tiles = ny // 8

    def fields(x, carry):
        for t in range(tiles):
            here = [
                pl.ds(pl.multiple_of(((x * tiles + t) * lanes + z) * 8, 8), 8) for z in range(lanes)
            ]
            for z in range(lanes):
                coef_v[here[z], :] = coef_of(m_v[here[z], :], table)

            def parts(k):
                if k < 3:
                    return e_v[k, here[0], :], e_v[k, here[-1], :]
                if k < 6:
                    return h_v[k - 3, here[0], :], h_v[k - 3, here[-1], :]
                return coef_v[here[0], :], coef_v[here[-1], :]

            row = pl.multiple_of((x + 2) * step + HALO + t * 8, 8)
            packed[pl.ds(row, 8), :] = turn_ends(parts, lane, 0, FIELDS)
        return carry

    lax.fori_loop(0, nx, fields, 0, unroll=4)

    for copy in copies:
        copy.wait()

    def changes(x, carry):
        index = pl.ds(pl.multiple_of(x * ny, ny), ny)
        change = []
        for c in range(3):
            s = [
                [
                    snap_ref[t, c, index, z * 128 : z * 128 + 128].astype(jnp.float32)
                    for z in (0, lanes - 1)
                ]
                for t in range(STEPS + 1)
            ]
            change.append([[s[t][z] - s[t + 1][z] for z in range(2)] for t in range(STEPS)])
        for t in range(tiles):

            def parts(k):
                pair = change[(k - FIELDS) % 3][1 - (k - FIELDS) // 3]
                return tuple(v[t * 8 : t * 8 + 8] for v in pair)

            here = pl.ds(pl.multiple_of((x + 2) * step + HALO + t * 8, 8), 8)
            after = turn_ends(parts, lane, FIELDS, FIELDS + 6)
            packed[here, :] = jnp.where(lane < 8 * FIELDS, packed[here, :], after)
        return carry

    lax.fori_loop(0, nx, changes, 0, unroll=4)


def unpack_faces(dims, sizes, own_packed, *refs):
    nx, ny, nz = dims
    lanes = nz // 128
    tiles = ny // 8
    plane = ny * lanes
    step = ny + HALO
    gx, gy = lax.axis_index("gx"), lax.axis_index("gy")
    xs, ys = swaps(sizes[0]), swaps(sizes[1])
    n_msgs = len(xs) + len(ys) + len(xs) * len(ys)
    msgs = refs[:n_msgs]
    xh, yh, own_t, up_ref, down_ref, packed, x_raw, y_raw = refs[n_msgs:]
    xh[...] = jnp.zeros(xh.shape, jnp.float32)
    x_raw[...] = jnp.zeros(x_raw.shape, jnp.float32)
    y_raw[...] = jnp.zeros(y_raw.shape, jnp.float32)
    for f in range(FIELDS):
        for z in range(lanes):
            if len(ys) < 2 or f < 3:
                yh[f, z] = jnp.zeros(yh.shape[2:], jnp.float32)
            else:
                for p in (0, 1, nx + 2, nx + 3):
                    yh[f, z, pl.ds(p * HALO, HALO), :] = jnp.zeros((HALO, 128), jnp.float32)

    def planes(odd):
        high = sends_up(gx, odd)
        return jnp.where(high, 2, 1), jnp.where(high, 3, 0)

    def lines(odd):
        high = sends_up(gy, odd)
        return jnp.where(high, 0, HALO - 1), jnp.where(high, 1, HALO - 2)

    for i, odd in enumerate(xs):
        ok = has_partner(gx, sizes[0], odd)
        near, far = planes(odd)
        msg = msgs[i]
        for t in range(tiles):
            for z in range(lanes):
                for k, f in enumerate((0, 1, 2, 3, 4, 5, 6, 4, 5)):
                    q = near if k < FIELDS else far
                    xh[f, z, pl.ds(pl.multiple_of(q * ny + t * 8, 8), 8), :] = jnp.where(
                        ok, msg[pl.ds(k * plane + (t * lanes + z) * 8, 8), :], 0.0
                    )
            x_raw[pl.ds(pl.multiple_of(far * ny + t * 8, 8), 8), :] = jnp.where(
                ok & (far == 0), msg[pl.ds(9 * plane + t * 8, 8), :], 0.0
            )
    for i, odd in enumerate(ys):
        ok = has_partner(gy, sizes[1], odd)
        near, far = lines(odd)
        msg = msgs[len(xs) + i]
        for z in range(lanes):
            for k, f in enumerate((0, 1, 2, 3, 4, 5, 6, 3, 5)):
                r = near if k < FIELDS else far
                yh[f, z, pl.ds(2 * HALO + r, nx, stride=HALO), :] = jnp.where(
                    ok, msg[k * lanes + z], 0.0
                )
        y_raw[pl.ds(2 * HALO + far, nx, stride=HALO), :] = jnp.where(
            ok & (far == HALO - 2), msg[9 * lanes], 0.0
        )
    for i, ox in enumerate(xs):
        for j, oy in enumerate(ys):
            ok = has_partner(gx, sizes[0], ox) & has_partner(gy, sizes[1], oy)
            px, py = planes(ox), lines(oy)
            px = [jnp.where(q < 2, q, q + nx) for q in px]
            msg = msgs[len(xs) + len(ys) + i * len(ys) + j]
            for z in range(lanes):
                for f in range(FIELDS):
                    for k in range(4):
                        yh[f, z, pl.ds(px[k // 2] * HALO + py[k % 2], 1), :] = jnp.where(
                            ok, msg[z, pl.ds(4 * f + k, 1), :], 0.0
                        )

    lane = lax.broadcasted_iota(jnp.int32, (8, 128), 1)
    upper = lax.broadcasted_iota(jnp.int32, (8, 128), 0) < HALO // 2

    def halo_rows(p, before, here):
        def tile(f, z):
            if f == FIELDS:
                return y_raw[here, :]
            return jnp.where(upper, yh[f, z, before, :], yh[f, z, here, :])

        packed[pl.ds(p * step if isinstance(p, int) else pl.multiple_of(p * step, 8), HALO), :] = (
            turn_ends(lambda f: (tile(f, 0), tile(f, lanes - 1)), lane, 0, FIELDS + 1)
        )

    def one(p, carry):
        halo_rows(
            p,
            pl.ds(pl.multiple_of((p - 1) * HALO, 8), HALO),
            pl.ds(pl.multiple_of(p * HALO, 8), HALO),
        )
        return carry

    halo_rows(0, pl.ds(0, HALO), pl.ds(0, HALO))
    lax.fori_loop(1, nx + 4, one, 0, unroll=5)
    last = pl.ds((nx + 3) * HALO, HALO)
    halo_rows(nx + 4, last, last)
    for q, p in enumerate((0, 1, nx + 2, nx + 3)):
        for t in range(tiles):
            index = pl.ds(q * ny + t * 8, 8)

            def parts(f):
                if f == FIELDS:
                    return x_raw[index, :], x_raw[index, :]
                return xh[f, 0, index, :], xh[f, lanes - 1, index, :]

            packed[pl.ds(p * step + HALO + t * 8, 8), :] = turn_ends(parts, lane, 0, FIELDS + 1)
    for x in range(nx):
        index = pl.ds((x + 2) * step + HALO, ny)
        packed[index, :] = own_packed[index, :]
    after = (nx + 4) * step + HALO
    padded = packed.shape[0]
    if padded > after:
        packed[after:, :] = jnp.zeros((padded - after, 128), jnp.float32)
    for b in range(padded // 128):
        here = pl.ds(b * 128, 128)
        block = jnp.transpose(packed[here, :])
        own_t[:, here] = block
        for f in range(FIELDS):
            up_ref[f : f + 1, here] = block[8 * f + 3 : 8 * f + 4, :]
            up_ref[8 + f : 9 + f, here] = block[8 * f + 2 : 8 * f + 3, :]
            down = [block[8 * f + 4 + k : 8 * f + 5 + k, :] for k in range(2)]
            if f < 2:
                at = lax.broadcasted_iota(jnp.int32, (1, 128), 1) + b * 128
                raw = (at >= HALO) & (at < step) if f == 0 else lax.rem(at, step) < HALO
                tail = [block[8 * FIELDS + 4 + k : 8 * FIELDS + 5 + k, :] for k in range(2)]
                down = [down[k] + jnp.where(raw, tail[k], 0.0) for k in range(2)]
            down_ref[f : f + 1, here] = down[0]
            down_ref[8 + f : 9 + f, here] = down[1]
    for row in (7, 15):
        up_ref[row : row + 1, :] = jnp.zeros((1, padded), jnp.float32)
        down_ref[row : row + 1, :] = jnp.zeros((1, padded), jnp.float32)


def columns_of(lines, nx, ny):
    spread, pick = [], []
    for line, step, first in lines:
        size = line.shape[1]
        at = lax.broadcasted_iota(jnp.int32, (ny, size), 1) - first
        y = lax.broadcasted_iota(jnp.int32, (ny, size), 0)
        ok = (at >= 0) & (at < nx * step) & (lax.rem(at, step) == y)
        spread.append(jnp.where(ok, line, 0.0))
        at = lax.broadcasted_iota(jnp.int32, (nx, size), 1) - first
        x = lax.broadcasted_iota(jnp.int32, (nx, size), 0) * step
        pick.append(jnp.where((at >= x) & (at < x + step), 1.0, 0.0))
    left = jnp.concatenate(spread, axis=1)
    thirds = []
    for _ in range(3):
        part = left.astype(jnp.bfloat16)
        left = left - part.astype(jnp.float32)
        thirds.append(part)
    out = lax.dot_general(
        jnp.concatenate(thirds, axis=0),
        jnp.concatenate(pick, axis=1).astype(jnp.bfloat16),
        (((1,), (1,)), ((), ())),
        preferred_element_type=jnp.float32,
    )
    return out[0:ny] + (out[ny : 2 * ny] + out[2 * ny : 3 * ny])


def find_ports(dims, sizes, ports_ref):
    nx, ny, nz = dims
    gx, gy, gz = lax.axis_index("gx"), lax.axis_index("gy"), lax.axis_index("gz")
    plane_cells = (ny * sizes[1]) * (nz * sizes[2])
    line_cells = nz * sizes[2]
    found = []
    for q in range(ports_ref.shape[0]):
        cell = ports_ref[q]
        x = lax.div(cell, plane_cells) - gx * nx
        y = lax.rem(lax.div(cell, line_cells), ny * sizes[1]) - gy * ny
        z = lax.rem(cell, line_cells) - gz * nz
        found.append((x, y, z))
    return found


def march(dims, sizes, e_v, h_v, coef_v, xh, yh, snap_ref, ports_ref, amps_ref, *refs):
    nx, ny, nz = dims
    lanes = nz // 128
    tiles = ny // 8
    step = ny + HALO
    e_s, h_s, line_ref, e1, h1, h2, half_ref, struck, clean, sums = refs
    gx, gy = lax.axis_index("gx"), lax.axis_index("gy")
    row = lax.broadcasted_iota(jnp.int32, (step, nz), 0)
    lane = lax.broadcasted_iota(jnp.int32, (step, nz), 1)
    inside = (row < ny) | ((row < ny + 2) & (gy < sizes[1] - 1)) | ((row >= ny + 4) & (gy > 0))
    half_ref[...] = jnp.where(inside, magnetic_step, 0.0)
    for k in range(2):
        clean[k] = jnp.where((lane[:ny] > k) & (lane[:ny] < nz - 1 - k), 1.0, 0.0)

    planes_struck = []
    for q, (x, y, z) in enumerate(find_ports(dims, sizes, ports_ref)):
        near = (y >= -2) & (y < ny + 2) & (z >= 0) & (z < nz)
        at = jnp.where(y < 0, y + step, y)
        struck[q] = jnp.where((row == at) & (lane == z) & near, 1.0, 0.0)
        planes_struck.append(x + 2)

    def spot(x, t, z):
        index = ((x * tiles + t) * lanes + z) * 8
        return pl.ds(index if isinstance(index, int) else pl.multiple_of(index, 8), 8)

    def own_tile(f, p, t, z):
        if isinstance(p, int) and not 2 <= p < nx + 2:
            return xh[f, z, pl.ds((p if p < 2 else p - nx) * ny + t * 8, 8), :]
        if f < 3:
            return e_v[f, spot(p - 2, t, z), :]
        if f < 6:
            return h_v[f - 3, spot(p - 2, t, z), :]
        return coef_v[spot(p - 2, t, z), :]

    def aligned(index):
        return index if isinstance(index, int) else pl.multiple_of(index, 8)

    def load(f, p):
        columns = []
        for z in range(lanes):
            column = [own_tile(f, p, t, z) for t in range(tiles)]
            column.append(yh[f, z, pl.ds(aligned(p * HALO), HALO), :])
            columns.append(jnp.concatenate(column, axis=0))
        return jnp.concatenate(columns, axis=1)

    def load_own(f, p):
        return jnp.concatenate(
            [
                jnp.concatenate([own_tile(f, p, t, z) for t in range(tiles)], axis=0)
                for z in range(lanes)
            ],
            axis=1,
        )

    def put(ref, f, x, v):
        for t in range(tiles):
            for z in range(lanes):
                ref[f, spot(x, t, z), :] = v[t * 8 : t * 8 + 8, z * 128 : z * 128 + 128]

    def y_up(v):
        return pltpu.roll(v, step - 1, 0)

    def y_down(v):
        return pltpu.roll(v, 1, 0)

    def z_up(v):
        return pltpu.roll(v, nz - 1, 1)

    def z_down(v):
        return pltpu.roll(v, 1, 1)

    def new_h(half, ex, ey, ez, ey_x, ez_x, hx, hy, hz):
        cx = (y_up(ez) - ez) - (z_up(ey) - ey)
        cy = (z_up(ex) - ex) - (ez_x - ez)
        cz = (ey_x - ey) - (y_up(ex) - ex)
        return hx - half * cx, hy - half * cy, hz - half * cz

    def curl_h(hx, hy, hz, hy_x, hz_x):
        cx = (hz - y_down(hz)) - (hy - z_down(hy))
        cy = (hx - z_down(hx)) - (hz - hz_x)
        cz = (hy - hy_x) - (hx - y_down(hx))
        return cx, cy, cz

    def half_of(p):
        if isinstance(p, int) and p < 2:
            return half_ref[...] * jnp.where(gx == 0, 0.0, 1.0)
        if isinstance(p, int) and p >= nx + 2:
            return half_ref[...] * jnp.where(gx == sizes[0] - 1, 0.0, 1.0)
        return half_ref[...]

    def first_h(p):
        e = [load(f, p) for f in range(3)]
        h = [load(3 + f, p) for f in range(3)]
        out = new_h(half_of(p), *e, load(1, p + 1), load(2, p + 1), *h)
        for f in range(3):
            h1[f, p] = out[f]

    def first_e(p):
        e = [load(f, p) for f in range(3)]
        curl = curl_h(*[h1[f, p] for f in range(3)], h1[1, p - 1], h1[2, p - 1])
        coef = load(6, p)
        out = [e[f] + coef * curl[f] for f in range(3)]
        for f in range(3):
            e1[f, p] = out[f]

    def second_h(p):
        e = [e1[f, p] for f in range(3)]
        h = [h1[f, p] for f in range(3)]
        out = new_h(half_of(p), *e, e1[1, p + 1], e1[2, p + 1], *h)
        h2[0, p] = out[0]
        h2[1, p, 0:ny] = out[1][:ny]
        h2[2, p] = out[2]

    def second_e(p):
        h = [h2[f, p] for f in range(3)]
        curl = curl_h(*h, h2[1, p - 1], h2[2, p - 1])
        coef = load_own(6, p)
        old = [e1[f, p, 0:ny, 0:nz] for f in range(3)]
        new = [old[f] + coef * curl[f][:ny, :nz] for f in range(3)]
        x = p - 2
        index = pl.ds(aligned(x * ny), ny)
        total = None
        for f in range(3):
            put(e_s, f, x, new[f])
            put(h_s, f, x, h[f][:ny, :nz])
            s = [snap_ref[t, f, index, :].astype(jnp.float32) for t in range(STEPS + 1)]
            one = [old[f] * (s[0] - s[1]), new[f] * (s[1] - s[2])]
            total = one if total is None else [total[k] + one[k] for k in range(2)]
        total = total[0] * clean[0] + total[1] * clean[1]
        folded = total[:, 0:128]
        for at in range(128, nz, 128):
            folded = folded + total[:, at : at + 128]
        sums[index, :] = folded

    group = 4
    behind_e, behind_h, behind_last = group, 2 * group + 1, 3 * group + 1

    def some(p, behind, least, most):
        planes = [p - behind + i for i in range(group)]
        return [q for q in planes if not isinstance(q, int) or least <= q <= most]

    def strike(first, second):
        hit = None
        for at in planes_struck:
            for q in first + second:
                hit = at == q if hit is None else hit | (at == q)

        @pl.when(hit)
        def _():
            for k, at in enumerate(planes_struck):
                for p in first:
                    amp = jnp.where(at == p, amps_ref[0, k], 0.0)
                    e1[2, p] = e1[2, p] + struck[k] * amp
                for p in second:
                    x = p - 2
                    amp = jnp.where(at == p, amps_ref[1, k], 0.0)
                    index = pl.ds(aligned(x * ny), ny)
                    s = [snap_ref[t, 2, index, :].astype(jnp.float32) for t in (1, 2)]
                    folded = jnp.zeros((ny, 128), jnp.float32)
                    for z in range(lanes):
                        here = slice(z * 128, z * 128 + 128)
                        gain = struck[k, 0:ny, here] * amp
                        folded = folded + gain * clean[1, :, here] * (s[0] - s[1])[:, here]
                        for t in range(tiles):
                            here = spot(x, t, z)
                            e_s[2, here, :] = e_s[2, here, :] + gain[t * 8 : t * 8 + 8]
                    sums[index, :] = sums[index, :] + folded

    def one(p):
        last = some(p, behind_last, 2, nx + 1)
        first = some(p, behind_e, 1, nx + 2)
        for q in last:
            second_e(q)
        for q in some(p, behind_h, 1, nx + 1):
            second_h(q)
        for q in first:
            first_e(q)
        for q in some(p, 0, 0, nx + 2):
            first_h(q)
        if first + last:
            strike(first, last)

    def body(k, carry):
        one(start + k * group)
        return carry

    start = -(-(2 + behind_last) // group) * group
    passes = (nx + 1 - group - start) // group + 1
    for p in range(0, start, group):
        one(p)
    lax.fori_loop(0, passes, body, 0)
    for p in range(start + passes * group, nx + 2 + behind_last, group):
        one(p)
    for b in range(nx * ny // 128):
        here = pl.ds(b * 128, 128)
        line_ref[:, here] = jnp.sum(jnp.transpose(sums[here, :]), axis=0, keepdims=True)


def finish_ends(
    dims, sizes, own_t, low_ref, high_ref, line_ref, mask_ref, ports_ref, amps_ref, *refs
):
    nx, ny, nz = dims
    step = ny + HALO
    parts = sizes[2]
    ends_ref = refs[0]
    grads = refs[1 : 1 + parts]
    strips, turned, rows_ref = refs[1 + parts :]
    gx, gy, gz = lax.axis_index("gx"), lax.axis_index("gy"), lax.axis_index("gz")
    padded = own_t.shape[1]
    row = lax.broadcasted_iota(jnp.int32, (8, padded), 0)
    lane = lax.broadcasted_iota(jnp.int32, (8, padded), 1) - HALO
    has_low, has_high = gz > 0, gz < sizes[2] - 1
    for k, (msg, ok, far, near) in enumerate(((low_ref, has_low, 2, 3), (high_ref, has_high, 5, 4))):
        for f in range(FIELDS):
            strips[k, f] = own_t[8 * f : 8 * f + 8, :]
            strips[k, f, far : far + 1, :] = jnp.where(ok, msg[8 + f : 9 + f, :], 0.0)
            strips[k, f, near : near + 1, :] = jnp.where(ok, msg[f : f + 1, :], 0.0)

    at = lane + 2
    p, y = lax.div(at, step), lax.rem(at, step) - 2
    inside = ((p >= 2) | (gx > 0)) & ((p < nx + 2) | (gx < sizes[0] - 1))
    inside = inside & ((y >= 0) | (gy > 0)) & ((y < ny) | (gy < sizes[1] - 1))
    found = find_ports(dims, sizes, ports_ref)

    def x_up(v):
        return pltpu.roll(v, padded - step, 1)

    def x_down(v):
        return pltpu.roll(v, step, 1)

    def y_up(v):
        return pltpu.roll(v, padded - 1, 1)

    def y_down(v):
        return pltpu.roll(v, 1, 1)

    def z_up(v):
        return pltpu.roll(v, 7, 0)

    def z_down(v):
        return pltpu.roll(v, 1, 0)

    total = None
    results = []
    for k in range(2):
        ex, ey, ez, hx, hy, hz, coef = (strips[k, f] for f in range(FIELDS))
        first = -4 if k == 0 else nz - 4
        good = ((row >= 4) | has_low) if k == 0 else ((row < 4) | has_high)
        half = jnp.where(inside & good, magnetic_step, 0.0)
        for s in range(STEPS):
            cx = (y_up(ez) - ez) - (z_up(ey) - ey)
            cy = (z_up(ex) - ex) - (x_up(ez) - ez)
            cz = (x_up(ey) - ey) - (y_up(ex) - ex)
            hx, hy, hz = hx - half * cx, hy - half * cy, hz - half * cz
            cx = (hz - y_down(hz)) - (hy - z_down(hy))
            cy = (hx - z_down(hx)) - (hz - x_down(hz))
            cz = (hy - x_down(hy)) - (hx - y_down(hx))
            ex, ey, ez = ex + coef * cx, ey + coef * cy, ez + coef * cz
            for q, (sx, sy, sz) in enumerate(found):
                near = (sx >= -2) & (sx < nx + 2) & (sy >= -2) & (sy < ny + 2)
                hit = (row == sz - first) & (at == (sx + 2) * step + sy + 2) & near
                ez = ez + jnp.where(hit, amps_ref[s, q], 0.0)
            if k == 0:
                mine = (row == 4) | ((row == 5) & (s == 1))
            else:
                mine = (row == 3) | ((row == 2) & (s == 1))
            for c, e in enumerate((ex, ey, ez)):
                tile = FIELDS + c + 3 * (1 - s)
                one = jnp.where(mine, e * own_t[8 * tile : 8 * tile + 8, :], 0.0)
                total = one if total is None else total + one
        results.append((ex, ey, ez, hx, hy, hz))
    for c in range(6):
        rows_ref[8 * c : 8 * c + 8, :] = jnp.where(row < 4, results[1][c], results[0][c])
    line = jnp.sum(total, axis=0, keepdims=True)
    column = columns_of([(line_ref[...], ny, 0), (line, step, 2 * step + HALO)], nx, ny)
    turned[...] = column * mask_ref[...].astype(jnp.float32)
    width = ny // parts
    for shift in range(parts):
        owner = partner_of(gz, shift, parts)
        grads[shift][...] = turned[pl.ds(owner * width, width), :]
    ends_ref[...] = rows_ref[...]


def write_out(dims, e_s, h_s, ends_ref, e_out, h_out, spare, e_v, h_v, ends_t, sems):
    nx, ny, nz = dims
    lanes = nz // 128
    tiles = ny // 8
    plane = ny * lanes
    step = ny + HALO
    lane = lax.broadcasted_iota(jnp.int32, (8, 128), 1)
    spare[...] = jnp.zeros(spare.shape, jnp.float32)
    spare[0 : ends_ref.shape[0], :] = ends_ref[...]
    for b in range(spare.shape[1] // 128):
        ends_t[b * 128 : (b + 1) * 128, :] = jnp.transpose(spare[:, b * 128 : (b + 1) * 128])

    def one(x, carry):
        for t in range(tiles):
            v = ends_t[pl.ds(pl.multiple_of((x + 2) * step + HALO + t * 8, 8), 8), :]
            for c in range(6):
                src, dst = (e_s, e_v) if c < 3 else (h_s, h_v)
                placed = pltpu.roll(v, 124 - 8 * c, 1)
                for z in range(lanes):
                    here = pl.ds(pl.multiple_of(((x * tiles + t) * lanes + z) * 8, 8), 8)
                    out = src[c % 3, here, :]
                    if z == 0:
                        out = jnp.where(lane < 2, placed, out)
                    if z == lanes - 1:
                        out = jnp.where(lane >= 126, placed, out)
                    dst[c % 3, here, :] = out
        return carry

    chunk = nx // 4
    copies = []
    for c in range(4):
        lax.fori_loop(c * chunk, (c + 1) * chunk, one, 0, unroll=4)
        here = pl.ds(c * chunk * plane, chunk * plane)
        for k, (src, dst) in enumerate(((e_v, e_out), (h_v, h_out))):
            copy = pltpu.make_async_copy(src.at[:, here], dst.at[:, here], sems.at[2 * c + k])
            copy.start()
            copies.append(copy)
    for copy in copies:
        copy.wait()


def params(limit=12):
    return pltpu.CompilerParams(vmem_limit_bytes=limit * 1024 * 1024)


def body(sizes, e_adjoint, h_adjoint, snapshots, material, permittivity, design_mask, ports, amplitudes):
    permittivity = in_hbm(permittivity)
    permittivity = in_hbm(permittivity)
    dims = material.shape
    nx, ny, nz = dims
    lanes = nz // 128
    tiles = ny // 8
    plane = ny * lanes
    cells = nx * ny
    step = ny + HALO
    padded = -(-((nx + 4) * step + HALO) // 128) * 128
    f32, i32 = jnp.float32, jnp.int32
    xs, ys = swaps(sizes[0]), swaps(sizes[1])
    block, cube = jax.ShapeDtypeStruct, pltpu.VMEM

    shapes = [block((9 * plane + ny, 128), f32) for _ in xs]
    shapes += [block((9 * lanes + 1, nx, 128), f32) for _ in ys]
    shapes += [block((lanes, 4 * FIELDS, 128), f32) for _ in xs for _ in ys]
    buffers = []
    for _ in xs:
        tile = (2, tiles, lanes, 8, 128)
        buffers += [cube((3, *tile), f32), cube((3, *tile), f32), cube(tile, i32)]
    for _ in ys:
        tile = (nx * lanes * 8, 128)
        buffers += [cube((3, *tile), f32), cube((3, *tile), f32), cube(tile, i32)]
    n_copies = 3 * (len(xs) + len(ys)) + 1
    msgs = pl.pallas_call(
        functools.partial(send_faces, dims, sizes),
        out_shape=shapes,
        in_specs=[HBM, HBM, HBM, HBM],
        out_specs=[VM] * len(shapes),
        scratch_shapes=buffers
        + [pltpu.SMEM(permittivity.shape, f32), pltpu.SemaphoreType.DMA((n_copies,))],
        compiler_params=params(),
        name="send_faces",
    )(
        in_hbm(tiles_of(e_adjoint)),
        in_hbm(tiles_of(h_adjoint)),
        in_hbm(tiles_of(material)),
        permittivity,
    )
    e_v, h_v, m_v = in_vmem(tiled(e_adjoint)), in_vmem(tiled(h_adjoint)), in_vmem(tiled(material))
    snaps = in_hbm(snapshots.reshape(STEPS + 1, 3, cells, nz))
    coef_v, own_packed, s = pl.pallas_call(
        functools.partial(own_ends, dims),
        out_shape=[cube(m_v.shape, f32), cube((padded, 128), f32), cube(snaps.shape, snaps.dtype)],
        in_specs=[VM, VM, VM, HBM, SM],
        out_specs=[VM] * 3,
        scratch_shapes=[pltpu.SemaphoreType.DMA((3 * (STEPS + 1),))],
        compiler_params=params(),
        cost_estimate=pl.CostEstimate(flops=10**7, bytes_accessed=4 * 10**6, transcendentals=0),
        name="own_ends",
    )(e_v, h_v, m_v, snaps, permittivity)

    both = ("gx", "gy")

    def meet(x, y, tx, ty):
        if tx[x] == x or ty[y] == y:
            return x * sizes[1] + y
        return tx[x] * sizes[1] + ty[y]

    tables = [("gx", list(enumerate(swap_table(sizes[0], o)))) for o in xs]
    tables += [("gy", list(enumerate(swap_table(sizes[1], o)))) for o in ys]
    for ox in xs:
        for oy in ys:
            tx, ty = swap_table(sizes[0], ox), swap_table(sizes[1], oy)
            pairs = [
                (x * sizes[1] + y, meet(x, y, tx, ty))
                for x in range(sizes[0])
                for y in range(sizes[1])
            ]
            tables.append((both, pairs))
    got = [lax.ppermute(msg, axis, pairs) for msg, (axis, pairs) in zip(msgs, tables)]

    xh, yh, own_t, up, down = pl.pallas_call(
        functools.partial(unpack_faces, dims, sizes),
        out_shape=[
            cube((FIELDS, lanes, 4 * ny, 128), f32),
            cube((FIELDS, lanes, (nx + 4) * HALO, 128), f32),
            cube((128, padded), f32),
            block((16, padded), f32),
            block((16, padded), f32),
        ],
        in_specs=[VM] * (1 + len(got)),
        out_specs=[VM] * 5,
        scratch_shapes=[
            pltpu.VMEM((padded, 128), f32),
            pltpu.VMEM((4 * ny, 128), f32),
            pltpu.VMEM(((nx + 4) * HALO, 128), f32),
        ],
        compiler_params=params(),
        name="unpack_faces",
    )(own_packed, *got)

    parts = sizes[2]
    low = lax.ppermute(up, "gz", [(i, (i + 1) % parts) for i in range(parts)])
    high = lax.ppermute(down, "gz", [(i, (i - 1) % parts) for i in range(parts)])

    ported = ports.shape[0]
    e_s, h_s, line = pl.pallas_call(
        functools.partial(march, dims, sizes),
        out_shape=[cube(e_v.shape, f32), cube(h_v.shape, f32), block((1, cells), f32)],
        in_specs=[VM] * 6 + [SM, SM],
        out_specs=[VM] * 3,
        scratch_shapes=[
            pltpu.VMEM((3, nx + 4, step, nz), f32),
            pltpu.VMEM((3, nx + 4, step, nz), f32),
            pltpu.VMEM((3, nx + 4, step, nz), f32),
            pltpu.VMEM((step, nz), f32),
            pltpu.VMEM((ported, step, nz), f32),
            pltpu.VMEM((2, ny, nz), f32),
            pltpu.VMEM((cells, 128), f32),
        ],
        compiler_params=params(24),
        cost_estimate=pl.CostEstimate(flops=4 * 10**7, bytes_accessed=10**7, transcendentals=0),
        name="march",
    )(e_v, h_v, coef_v, xh, yh, s, ports, amplitudes)
    ends, *chunks = pl.pallas_call(
        functools.partial(finish_ends, dims, sizes),
        out_shape=[cube((48, padded), f32)] + [block((ny // parts, nx), f32)] * parts,
        in_specs=[VM] * 5 + [SM, SM],
        out_specs=[VM] * (1 + parts),
        scratch_shapes=[
            pltpu.VMEM((2, FIELDS, 8, padded), f32),
            pltpu.VMEM((ny, nx), f32),
            pltpu.VMEM((48, padded), f32),
        ],
        compiler_params=params(),
        name="finish_ends",
    )(own_t, low, high, line, design_mask.T, ports, amplitudes)
    e_out, h_out = pl.pallas_call(
        functools.partial(write_out, dims),
        out_shape=[block(e_v.shape, f32), block(h_v.shape, f32)],
        in_specs=[VM] * 3,
        out_specs=[HBM] * 2,
        scratch_shapes=[
            pltpu.VMEM((128, padded), f32),
            pltpu.VMEM(e_v.shape, f32),
            pltpu.VMEM(h_v.shape, f32),
            pltpu.VMEM((padded, 128), f32),
            pltpu.SemaphoreType.DMA((8,)),
        ],
        compiler_params=params(),
        cost_estimate=pl.CostEstimate(flops=10**7, bytes_accessed=8 * 10**6, transcendentals=0),
        name="write_out",
    )(e_s, h_s, ends)
    gradient = chunks[0]
    for shift in range(1, parts):
        gradient = gradient + lax.ppermute(
            chunks[shift], "gz", [(i, partner_of(i, shift, parts)) for i in range(parts)]
        )
    return untiled(e_out, dims), untiled(h_out, dims), gradient.T


def solution(mesh):
    placed = (
        P(None, "gx", "gy", "gz"),
        P(None, "gx", "gy", "gz"),
        P(None, None, "gx", "gy", "gz"),
        P("gx", "gy", "gz"),
        P(),
        P("gx", "gy"),
        P(),
        P(),
    )
    sizes = tuple(mesh.shape[axis] for axis in ("gx", "gy", "gz"))
    return jax.shard_map(
        functools.partial(body, sizes),
        mesh=mesh,
        in_specs=placed,
        out_specs=(P(None, "gx", "gy", "gz"), P(None, "gx", "gy", "gz"), P("gx", ("gy", "gz"))),
        check_vma=False,
    )
```

```python
import functools

import jax
import jax.numpy as jnp
from jax import lax
from jax.experimental import pallas as pl
from jax.experimental.pallas import tpu as pltpu
from jax.sharding import PartitionSpec as P

STEPS = 2
FIELDS = 7
HALO = 8

magnetic_step = 0.5
electric_step = 0.5

VM = pl.BlockSpec(memory_space=pltpu.VMEM)
SM = pl.BlockSpec(memory_space=pltpu.SMEM)
ANY = pl.BlockSpec(memory_space=pl.ANY)


HBM = pl.BlockSpec(memory_space=pltpu.HBM)


def in_hbm(array):
    return pltpu.with_memory_space_constraint(array, pltpu.HBM)


def in_vmem(array):
    return pltpu.with_memory_space_constraint(array, pltpu.VMEM)


def swap_table(size, odd):
    table = list(range(size))
    for i in range(odd, size - 1, 2):
        table[i], table[i + 1] = i + 1, i
    return table


def swaps(size):
    return [odd for odd in (0, 1) if odd + 1 < size]


def partner_of(index, shift, size):
    if size & (size - 1) == 0:
        return index ^ shift
    return (index + shift) % size


def sends_up(index, odd):
    return lax.rem(index, 2) == odd


def has_partner(index, size, odd):
    up = sends_up(index, odd)
    return (up & (index + 1 < size)) | (jnp.logical_not(up) & (index >= 1))


def coef_table(perm_ref):
    return [
        electric_step / jnp.full((1, 1), perm_ref[i], jnp.float32) for i in range(perm_ref.shape[0])
    ]


def coef_of(material, table):
    out = jnp.zeros(material.shape, jnp.float32)
    for i, value in enumerate(table):
        out = jnp.where(material == i, value, out)
    return out


def tiled(array):
    *lead, nx, ny, nz = array.shape
    n = len(lead)
    split = array.reshape(*lead, nx, ny // 8, 8, nz // 128, 128)
    order = tuple(range(n + 2)) + (n + 3, n + 2, n + 4)
    return split.transpose(order).reshape(*lead, nx * ny * nz // 128, 128)


def untiled(array, dims):
    nx, ny, nz = dims
    lead = array.shape[:-2]
    n = len(lead)
    split = array.reshape(*lead, nx, ny // 8, nz // 128, 8, 128)
    order = tuple(range(n + 2)) + (n + 3, n + 2, n + 4)
    return split.transpose(order).reshape(*lead, nx, ny, nz)


def tiles_of(array):
    *lead, nx, ny, nz = array.shape
    return tiled(array).reshape(*lead, nx, ny // 8, nz // 128, 8, 128)


def send_faces(dims, sizes, e_ref, h_ref, m_ref, perm_ref, *refs):
    nx, ny, nz = dims
    lanes = nz // 128
    tiles = ny // 8
    plane = ny * lanes
    gx, gy = lax.axis_index("gx"), lax.axis_index("gy")
    xs, ys = swaps(sizes[0]), swaps(sizes[1])
    n_out = len(xs) + len(ys) + len(xs) * len(ys)
    outs, refs = refs[:n_out], refs[n_out:]
    x_bufs, refs = refs[: 3 * len(xs)], refs[3 * len(xs) :]
    y_bufs, (perm_s, sems) = refs[: 3 * len(ys)], refs[3 * len(ys) :]
    copies = []

    def start(src, dst):
        copy = pltpu.make_async_copy(src, dst, sems.at[len(copies)])
        copy.start()
        copies.append(copy)

    for i, odd in enumerate(ys):
        up = sends_up(gy, odd)
        t, r = jnp.where(up, tiles - 1, 0), jnp.where(up, 6, 0)
        for k, ref in enumerate((e_ref, h_ref, m_ref)):
            src = ref.at[:, t, :, pl.ds(r, 2), :] if k == 2 else ref.at[:, :, t, :, pl.ds(r, 2), :]
            dst = y_bufs[3 * i + k]
            dst = dst.reshape(*dst.shape[:-2], nx, lanes, 8, 128)
            start(src, dst.at[:, :, pl.ds(0, 2), :] if k == 2 else dst.at[:, :, :, pl.ds(0, 2), :])
    for i, odd in enumerate(xs):
        first = pl.ds(jnp.where(sends_up(gx, odd), nx - 2, 0), 2)
        for k, ref in enumerate((e_ref, h_ref, m_ref)):
            start(ref.at[first] if k == 2 else ref.at[:, first], x_bufs[3 * i + k])
    start(perm_ref, perm_s)
    copies.pop().wait()
    table = coef_table(perm_s)
    lane = lax.broadcasted_iota(jnp.int32, (8, 128), 1)
    lane_n = lax.broadcasted_iota(jnp.int32, (nx, 128), 1)

    def z_up(v, lane):
        out = []
        for z in range(lanes):
            after = pltpu.roll(v[z + 1], 127, 1) if z + 1 < lanes else jnp.zeros_like(v[z])
            out.append(jnp.where(lane < 127, pltpu.roll(v[z], 127, 1), after))
        return out

    def row_up(v):
        rows = v.shape[0]
        row = lax.broadcasted_iota(jnp.int32, v.shape, 0)
        return jnp.where(row < rows - 1, pltpu.roll(v, rows - 1, 0), 0.0)

    step = lanes * 8
    for i, odd in enumerate(ys):
        for copy in copies[3 * i : 3 * i + 3]:
            copy.wait()
        up = sends_up(gy, odd)
        near, far = jnp.where(up, 1, 0), jnp.where(up, 0, 1)
        down = jnp.where(up, 0.0, magnetic_step)
        e_b, h_b, m_b = y_bufs[3 * i : 3 * i + 3]
        out = outs[len(xs) + i]

        def at(ref, c, which):
            return [ref[c, pl.ds(z * 8 + which, nx, stride=step), :] for z in range(lanes)]

        e_n = [at(e_b, c, near) for c in range(3)]
        h_n = [at(h_b, c, near) for c in range(3)]
        ex_f, ey_f, ez_f = (at(e_b, c, far) for c in range(3))
        hx_f, hz_f = at(h_b, 0, far), at(h_b, 2, far)
        ey_z = z_up(ey_f, lane_n)
        for z in range(lanes):
            for c in range(3):
                out[c * lanes + z] = e_n[c][z]
            out[3 * lanes + z] = h_n[0][z] - down * ez_f[z]
            out[4 * lanes + z] = h_n[1][z]
            out[5 * lanes + z] = h_n[2][z] + down * ex_f[z]
            out[6 * lanes + z] = coef_of(m_b[pl.ds(z * 8 + near, nx, stride=step), :], table)
            out[7 * lanes + z] = hx_f[z] + magnetic_step * (ez_f[z] + (ey_z[z] - ey_f[z]))
            out[8 * lanes + z] = hz_f[z] - magnetic_step * ((row_up(ey_f[z]) - ey_f[z]) + ex_f[z])
        out[9 * lanes] = ey_f[0]
    for i, odd in enumerate(xs):
        for copy in copies[3 * (len(ys) + i) : 3 * (len(ys) + i) + 3]:
            copy.wait()
        up = sends_up(gx, odd)
        near, far = jnp.where(up, 1, 0), jnp.where(up, 0, 1)
        down = jnp.where(up, 0.0, magnetic_step)
        e_b, h_b, m_b = x_bufs[3 * i : 3 * i + 3]
        out = outs[i]

        def put(k, t, z, v):
            out[pl.ds(k * plane + (t * lanes + z) * 8, 8), :] = v

        ex_y = [
            row_up(jnp.concatenate([e_b[0, far, t, z] for t in range(tiles)], axis=0))
            for z in range(lanes)
        ]
        for t in range(tiles):
            ex_z = z_up([e_b[0, far, t, z] for z in range(lanes)], lane)
            for z in range(lanes):
                ex_f, ey_f, ez_f = (e_b[c, far, t, z] for c in range(3))
                for c in range(3):
                    put(c, t, z, e_b[c, near, t, z])
                put(3, t, z, h_b[0, near, t, z])
                put(4, t, z, h_b[1, near, t, z] + down * ez_f)
                put(5, t, z, h_b[2, near, t, z] - down * ey_f)
                put(6, t, z, coef_of(m_b[near, t, z], table))
                put(7, t, z, h_b[1, far, t, z] - magnetic_step * ((ex_z[z] - ex_f) + ez_f))
                ex_up = ex_y[z][t * 8 : t * 8 + 8]
                put(8, t, z, h_b[2, far, t, z] + magnetic_step * (ey_f + (ex_up - ex_f)))
            out[pl.ds(9 * plane + t * 8, 8), :] = e_b[0, far, t, 0]
        for j, odd_y in enumerate(ys):
            up = sends_up(gy, odd_y)
            t = jnp.where(up, tiles - 1, 0)
            rows = (jnp.where(up, 7, 0), jnp.where(up, 6, 1))
            out = outs[len(xs) + len(ys) + i * len(ys) + j]
            for z in range(lanes):
                for f in range(FIELDS):
                    for k in range(4):
                        where = (near, far)[k // 2], t, z, pl.ds(rows[k % 2], 1)
                        if f < 6:
                            line = (e_b, h_b)[f // 3][(f % 3, *where)]
                        else:
                            line = coef_of(m_b[where], table)
                        out[z, pl.ds(4 * f + k, 1), :] = line


def turn_ends(parts, lane, first_field, after_field):
    out = None
    for k in range(first_field, after_field):
        first, last = parts(k)
        turned = pltpu.roll(jnp.where(lane < 64, first, last), 8 * k + 4, 1)
        out = turned if out is None else jnp.where(lane >= 8 * k, turned, out)
    return out


def own_ends(dims, e_v, h_v, m_v, snap_hbm, perm_ref, coef_v, packed, snap_ref, sems):
    nx, ny, nz = dims
    lanes = nz // 128
    step = ny + HALO
    copies = []
    for t in range(STEPS + 1):
        for c in range(3):
            copy = pltpu.make_async_copy(snap_hbm.at[t, c], snap_ref.at[t, c], sems.at[3 * t + c])
            copy.start()
            copies.append(copy)
    table = coef_table(perm_ref)
    lane = lax.broadcasted_iota(jnp.int32, (8, 128), 1)
    tiles = ny // 8

    def fields(x, carry):
        for t in range(tiles):
            here = [
                pl.ds(pl.multiple_of(((x * tiles + t) * lanes + z) * 8, 8), 8) for z in range(lanes)
            ]
            for z in range(lanes):
                coef_v[here[z], :] = coef_of(m_v[here[z], :], table)

            def parts(k):
                if k < 3:
                    return e_v[k, here[0], :], e_v[k, here[-1], :]
                if k < 6:
                    return h_v[k - 3, here[0], :], h_v[k - 3, here[-1], :]
                return coef_v[here[0], :], coef_v[here[-1], :]

            row = pl.multiple_of((x + 2) * step + HALO + t * 8, 8)
            packed[pl.ds(row, 8), :] = turn_ends(parts, lane, 0, FIELDS)
        return carry

    lax.fori_loop(0, nx, fields, 0, unroll=16)

    for copy in copies:
        copy.wait()

    def changes(x, carry):
        index = pl.ds(pl.multiple_of(x * ny, ny), ny)
        change = []
        for c in range(3):
            s = [
                [
                    snap_ref[t, c, index, z * 128 : z * 128 + 128].astype(jnp.float32)
                    for z in (0, lanes - 1)
                ]
                for t in range(STEPS + 1)
            ]
            change.append([[s[t][z] - s[t + 1][z] for z in range(2)] for t in range(STEPS)])
        for t in range(tiles):

            def parts(k):
                pair = change[(k - FIELDS) % 3][1 - (k - FIELDS) // 3]
                return tuple(v[t * 8 : t * 8 + 8] for v in pair)

            here = pl.ds(pl.multiple_of((x + 2) * step + HALO + t * 8, 8), 8)
            after = turn_ends(parts, lane, FIELDS, FIELDS + 6)
            packed[here, :] = jnp.where(lane < 8 * FIELDS, packed[here, :], after)
        return carry

    lax.fori_loop(0, nx, changes, 0, unroll=16)


def unpack_faces(dims, sizes, own_packed, *refs):
    nx, ny, nz = dims
    lanes = nz // 128
    tiles = ny // 8
    plane = ny * lanes
    step = ny + HALO
    gx, gy = lax.axis_index("gx"), lax.axis_index("gy")
    xs, ys = swaps(sizes[0]), swaps(sizes[1])
    n_msgs = len(xs) + len(ys) + len(xs) * len(ys)
    msgs = refs[:n_msgs]
    xh, yh, own_t, up_ref, down_ref, packed, x_raw, y_raw = refs[n_msgs:]
    xh[...] = jnp.zeros(xh.shape, jnp.float32)
    x_raw[...] = jnp.zeros(x_raw.shape, jnp.float32)
    y_raw[...] = jnp.zeros(y_raw.shape, jnp.float32)
    for f in range(FIELDS):
        for z in range(lanes):
            if len(ys) < 2 or f < 3:
                yh[f, z] = jnp.zeros(yh.shape[2:], jnp.float32)
            else:
                for p in (0, 1, nx + 2, nx + 3):
                    yh[f, z, pl.ds(p * HALO, HALO), :] = jnp.zeros((HALO, 128), jnp.float32)

    def planes(odd):
        high = sends_up(gx, odd)
        return jnp.where(high, 2, 1), jnp.where(high, 3, 0)

    def lines(odd):
        high = sends_up(gy, odd)
        return jnp.where(high, 0, HALO - 1), jnp.where(high, 1, HALO - 2)

    for i, odd in enumerate(xs):
        ok = has_partner(gx, sizes[0], odd)
        near, far = planes(odd)
        msg = msgs[i]
        for t in range(tiles):
            for z in range(lanes):
                for k, f in enumerate((0, 1, 2, 3, 4, 5, 6, 4, 5)):
                    q = near if k < FIELDS else far
                    xh[f, z, pl.ds(pl.multiple_of(q * ny + t * 8, 8), 8), :] = jnp.where(
                        ok, msg[pl.ds(k * plane + (t * lanes + z) * 8, 8), :], 0.0
                    )
            x_raw[pl.ds(pl.multiple_of(far * ny + t * 8, 8), 8), :] = jnp.where(
                ok & (far == 0), msg[pl.ds(9 * plane + t * 8, 8), :], 0.0
            )
    for i, odd in enumerate(ys):
        ok = has_partner(gy, sizes[1], odd)
        near, far = lines(odd)
        msg = msgs[len(xs) + i]
        for z in range(lanes):
            for k, f in enumerate((0, 1, 2, 3, 4, 5, 6, 3, 5)):
                r = near if k < FIELDS else far
                yh[f, z, pl.ds(2 * HALO + r, nx, stride=HALO), :] = jnp.where(
                    ok, msg[k * lanes + z], 0.0
                )
        y_raw[pl.ds(2 * HALO + far, nx, stride=HALO), :] = jnp.where(
            ok & (far == HALO - 2), msg[9 * lanes], 0.0
        )
    for i, ox in enumerate(xs):
        for j, oy in enumerate(ys):
            ok = has_partner(gx, sizes[0], ox) & has_partner(gy, sizes[1], oy)
            px, py = planes(ox), lines(oy)
            px = [jnp.where(q < 2, q, q + nx) for q in px]
            msg = msgs[len(xs) + len(ys) + i * len(ys) + j]
            for z in range(lanes):
                for f in range(FIELDS):
                    for k in range(4):
                        yh[f, z, pl.ds(px[k // 2] * HALO + py[k % 2], 1), :] = jnp.where(
                            ok, msg[z, pl.ds(4 * f + k, 1), :], 0.0
                        )

    lane = lax.broadcasted_iota(jnp.int32, (8, 128), 1)
    upper = lax.broadcasted_iota(jnp.int32, (8, 128), 0) < HALO // 2

    def halo_rows(p, before, here):
        def tile(f, z):
            if f == FIELDS:
                return y_raw[here, :]
            return jnp.where(upper, yh[f, z, before, :], yh[f, z, here, :])

        packed[pl.ds(p * step if isinstance(p, int) else pl.multiple_of(p * step, 8), HALO), :] = (
            turn_ends(lambda f: (tile(f, 0), tile(f, lanes - 1)), lane, 0, FIELDS + 1)
        )

    def one(p, carry):
        halo_rows(
            p,
            pl.ds(pl.multiple_of((p - 1) * HALO, 8), HALO),
            pl.ds(pl.multiple_of(p * HALO, 8), HALO),
        )
        return carry

    halo_rows(0, pl.ds(0, HALO), pl.ds(0, HALO))
    lax.fori_loop(1, nx + 4, one, 0, unroll=True)
    last = pl.ds((nx + 3) * HALO, HALO)
    halo_rows(nx + 4, last, last)
    for q, p in enumerate((0, 1, nx + 2, nx + 3)):
        for t in range(tiles):
            index = pl.ds(q * ny + t * 8, 8)

            def parts(f):
                if f == FIELDS:
                    return x_raw[index, :], x_raw[index, :]
                return xh[f, 0, index, :], xh[f, lanes - 1, index, :]

            packed[pl.ds(p * step + HALO + t * 8, 8), :] = turn_ends(parts, lane, 0, FIELDS + 1)
    for x in range(nx):
        index = pl.ds((x + 2) * step + HALO, ny)
        packed[index, :] = own_packed[index, :]
    after = (nx + 4) * step + HALO
    padded = packed.shape[0]
    if padded > after:
        packed[after:, :] = jnp.zeros((padded - after, 128), jnp.float32)
    for b in range(padded // 128):
        here = pl.ds(b * 128, 128)
        block = jnp.transpose(packed[here, :])
        own_t[:, here] = block
        for f in range(FIELDS):
            up_ref[f : f + 1, here] = block[8 * f + 3 : 8 * f + 4, :]
            up_ref[8 + f : 9 + f, here] = block[8 * f + 2 : 8 * f + 3, :]
            down = [block[8 * f + 4 + k : 8 * f + 5 + k, :] for k in range(2)]
            if f < 2:
                at = lax.broadcasted_iota(jnp.int32, (1, 128), 1) + b * 128
                raw = (at >= HALO) & (at < step) if f == 0 else lax.rem(at, step) < HALO
                tail = [block[8 * FIELDS + 4 + k : 8 * FIELDS + 5 + k, :] for k in range(2)]
                down = [down[k] + jnp.where(raw, tail[k], 0.0) for k in range(2)]
            down_ref[f : f + 1, here] = down[0]
            down_ref[8 + f : 9 + f, here] = down[1]
    for row in (7, 15):
        up_ref[row : row + 1, :] = jnp.zeros((1, padded), jnp.float32)
        down_ref[row : row + 1, :] = jnp.zeros((1, padded), jnp.float32)


def columns_of(lines, nx, ny):
    spread, pick = [], []
    for line, step, first in lines:
        size = line.shape[1]
        at = lax.broadcasted_iota(jnp.int32, (ny, size), 1) - first
        y = lax.broadcasted_iota(jnp.int32, (ny, size), 0)
        ok = (at >= 0) & (at < nx * step) & (lax.rem(at, step) == y)
        spread.append(jnp.where(ok, line, 0.0))
        at = lax.broadcasted_iota(jnp.int32, (nx, size), 1) - first
        x = lax.broadcasted_iota(jnp.int32, (nx, size), 0) * step
        pick.append(jnp.where((at >= x) & (at < x + step), 1.0, 0.0))
    left = jnp.concatenate(spread, axis=1)
    thirds = []
    for _ in range(3):
        part = left.astype(jnp.bfloat16)
        left = left - part.astype(jnp.float32)
        thirds.append(part)
    out = lax.dot_general(
        jnp.concatenate(thirds, axis=0),
        jnp.concatenate(pick, axis=1).astype(jnp.bfloat16),
        (((1,), (1,)), ((), ())),
        preferred_element_type=jnp.float32,
    )
    return out[0:ny] + (out[ny : 2 * ny] + out[2 * ny : 3 * ny])


def find_ports(dims, sizes, ports_ref):
    nx, ny, nz = dims
    gx, gy, gz = lax.axis_index("gx"), lax.axis_index("gy"), lax.axis_index("gz")
    plane_cells = (ny * sizes[1]) * (nz * sizes[2])
    line_cells = nz * sizes[2]
    found = []
    for q in range(ports_ref.shape[0]):
        cell = ports_ref[q]
        x = lax.div(cell, plane_cells) - gx * nx
        y = lax.rem(lax.div(cell, line_cells), ny * sizes[1]) - gy * ny
        z = lax.rem(cell, line_cells) - gz * nz
        found.append((x, y, z))
    return found


def march(dims, sizes, e_v, h_v, coef_v, xh, yh, snap_ref, ports_ref, amps_ref, *refs):
    nx, ny, nz = dims
    lanes = nz // 128
    tiles = ny // 8
    step = ny + HALO
    e_s, h_s, line_ref, e1, h1, h2, half_ref, struck, clean, sums = refs
    gx, gy = lax.axis_index("gx"), lax.axis_index("gy")
    row = lax.broadcasted_iota(jnp.int32, (step, nz), 0)
    lane = lax.broadcasted_iota(jnp.int32, (step, nz), 1)
    inside = (row < ny) | ((row < ny + 2) & (gy < sizes[1] - 1)) | ((row >= ny + 4) & (gy > 0))
    half_ref[...] = jnp.where(inside, magnetic_step, 0.0)
    for k in range(2):
        clean[k] = jnp.where((lane[:ny] > k) & (lane[:ny] < nz - 1 - k), 1.0, 0.0)

    planes_struck = []
    for q, (x, y, z) in enumerate(find_ports(dims, sizes, ports_ref)):
        near = (y >= -2) & (y < ny + 2) & (z >= 0) & (z < nz)
        at = jnp.where(y < 0, y + step, y)
        struck[q] = jnp.where((row == at) & (lane == z) & near, 1.0, 0.0)
        planes_struck.append(x + 2)

    def spot(x, t, z):
        index = ((x * tiles + t) * lanes + z) * 8
        return pl.ds(index if isinstance(index, int) else pl.multiple_of(index, 8), 8)

    def own_tile(f, p, t, z):
        if isinstance(p, int) and not 2 <= p < nx + 2:
            return xh[f, z, pl.ds((p if p < 2 else p - nx) * ny + t * 8, 8), :]
        if f < 3:
            return e_v[f, spot(p - 2, t, z), :]
        if f < 6:
            return h_v[f - 3, spot(p - 2, t, z), :]
        return coef_v[spot(p - 2, t, z), :]

    def aligned(index):
        return index if isinstance(index, int) else pl.multiple_of(index, 8)

    def load(f, p):
        columns = []
        for z in range(lanes):
            column = [own_tile(f, p, t, z) for t in range(tiles)]
            column.append(yh[f, z, pl.ds(aligned(p * HALO), HALO), :])
            columns.append(jnp.concatenate(column, axis=0))
        return jnp.concatenate(columns, axis=1)

    def load_own(f, p):
        return jnp.concatenate(
            [
                jnp.concatenate([own_tile(f, p, t, z) for t in range(tiles)], axis=0)
                for z in range(lanes)
            ],
            axis=1,
        )

    def put(ref, f, x, v):
        for t in range(tiles):
            for z in range(lanes):
                ref[f, spot(x, t, z), :] = v[t * 8 : t * 8 + 8, z * 128 : z * 128 + 128]

    def y_up(v):
        return pltpu.roll(v, step - 1, 0)

    def y_down(v):
        return pltpu.roll(v, 1, 0)

    def z_up(v):
        return pltpu.roll(v, nz - 1, 1)

    def z_down(v):
        return pltpu.roll(v, 1, 1)

    def new_h(half, ex, ey, ez, ey_x, ez_x, hx, hy, hz):
        cx = (y_up(ez) - ez) - (z_up(ey) - ey)
        cy = (z_up(ex) - ex) - (ez_x - ez)
        cz = (ey_x - ey) - (y_up(ex) - ex)
        return hx - half * cx, hy - half * cy, hz - half * cz

    def curl_h(hx, hy, hz, hy_x, hz_x):
        cx = (hz - y_down(hz)) - (hy - z_down(hy))
        cy = (hx - z_down(hx)) - (hz - hz_x)
        cz = (hy - hy_x) - (hx - y_down(hx))
        return cx, cy, cz

    def half_of(p):
        if isinstance(p, int) and p < 2:
            return half_ref[...] * jnp.where(gx == 0, 0.0, 1.0)
        if isinstance(p, int) and p >= nx + 2:
            return half_ref[...] * jnp.where(gx == sizes[0] - 1, 0.0, 1.0)
        return half_ref[...]

    def first_h(p):
        e = [load(f, p) for f in range(3)]
        h = [load(3 + f, p) for f in range(3)]
        out = new_h(half_of(p), *e, load(1, p + 1), load(2, p + 1), *h)
        for f in range(3):
            h1[f, p] = out[f]

    def first_e(p):
        e = [load(f, p) for f in range(3)]
        curl = curl_h(*[h1[f, p] for f in range(3)], h1[1, p - 1], h1[2, p - 1])
        coef = load(6, p)
        out = [e[f] + coef * curl[f] for f in range(3)]
        for f in range(3):
            e1[f, p] = out[f]

    def second_h(p):
        e = [e1[f, p] for f in range(3)]
        h = [h1[f, p] for f in range(3)]
        out = new_h(half_of(p), *e, e1[1, p + 1], e1[2, p + 1], *h)
        h2[0, p] = out[0]
        h2[1, p, 0:ny] = out[1][:ny]
        h2[2, p] = out[2]

    def second_e(p):
        h = [h2[f, p] for f in range(3)]
        curl = curl_h(*h, h2[1, p - 1], h2[2, p - 1])
        coef = load_own(6, p)
        old = [e1[f, p, 0:ny, 0:nz] for f in range(3)]
        new = [old[f] + coef * curl[f][:ny, :nz] for f in range(3)]
        x = p - 2
        index = pl.ds(aligned(x * ny), ny)
        total = None
        for f in range(3):
            put(e_s, f, x, new[f])
            put(h_s, f, x, h[f][:ny, :nz])
            s = [snap_ref[t, f, index, :].astype(jnp.float32) for t in range(STEPS + 1)]
            one = [old[f] * (s[0] - s[1]), new[f] * (s[1] - s[2])]
            total = one if total is None else [total[k] + one[k] for k in range(2)]
        total = total[0] * clean[0] + total[1] * clean[1]
        folded = total[:, 0:128]
        for at in range(128, nz, 128):
            folded = folded + total[:, at : at + 128]
        sums[index, :] = folded

    group = 4
    behind_e, behind_h, behind_last = group, 2 * group + 1, 3 * group + 1

    def some(p, behind, least, most):
        planes = [p - behind + i for i in range(group)]
        return [q for q in planes if not isinstance(q, int) or least <= q <= most]

    def strike(first, second):
        hit = None
        for at in planes_struck:
            for q in first + second:
                hit = at == q if hit is None else hit | (at == q)

        @pl.when(hit)
        def _():
            for k, at in enumerate(planes_struck):
                for p in first:
                    amp = jnp.where(at == p, amps_ref[0, k], 0.0)
                    e1[2, p] = e1[2, p] + struck[k] * amp
                for p in second:
                    x = p - 2
                    amp = jnp.where(at == p, amps_ref[1, k], 0.0)
                    index = pl.ds(aligned(x * ny), ny)
                    s = [snap_ref[t, 2, index, :].astype(jnp.float32) for t in (1, 2)]
                    folded = jnp.zeros((ny, 128), jnp.float32)
                    for z in range(lanes):
                        here = slice(z * 128, z * 128 + 128)
                        gain = struck[k, 0:ny, here] * amp
                        folded = folded + gain * clean[1, :, here] * (s[0] - s[1])[:, here]
                        for t in range(tiles):
                            here = spot(x, t, z)
                            e_s[2, here, :] = e_s[2, here, :] + gain[t * 8 : t * 8 + 8]
                    sums[index, :] = sums[index, :] + folded

    def one(p):
        last = some(p, behind_last, 2, nx + 1)
        first = some(p, behind_e, 1, nx + 2)
        for q in last:
            second_e(q)
        for q in some(p, behind_h, 1, nx + 1):
            second_h(q)
        for q in first:
            first_e(q)
        for q in some(p, 0, 0, nx + 2):
            first_h(q)
        if first + last:
            strike(first, last)

    def body(k, carry):
        one(start + k * group)
        return carry

    start = -(-(2 + behind_last) // group) * group
    passes = (nx + 1 - group - start) // group + 1
    for p in range(0, start, group):
        one(p)
    lax.fori_loop(0, passes, body, 0)
    for p in range(start + passes * group, nx + 2 + behind_last, group):
        one(p)
    for b in range(nx * ny // 128):
        here = pl.ds(b * 128, 128)
        line_ref[:, here] = jnp.sum(jnp.transpose(sums[here, :]), axis=0, keepdims=True)


def finish_ends(
    dims, sizes, own_t, low_ref, high_ref, line_ref, mask_ref, ports_ref, amps_ref, *refs
):
    nx, ny, nz = dims
    step = ny + HALO
    parts = sizes[2]
    ends_ref = refs[0]
    grads = refs[1 : 1 + parts]
    strips, turned, rows_ref = refs[1 + parts :]
    gx, gy, gz = lax.axis_index("gx"), lax.axis_index("gy"), lax.axis_index("gz")
    padded = own_t.shape[1]
    row = lax.broadcasted_iota(jnp.int32, (8, padded), 0)
    lane = lax.broadcasted_iota(jnp.int32, (8, padded), 1) - HALO
    has_low, has_high = gz > 0, gz < sizes[2] - 1
    for k, (msg, ok, far, near) in enumerate(((low_ref, has_low, 2, 3), (high_ref, has_high, 5, 4))):
        for f in range(FIELDS):
            strips[k, f] = own_t[8 * f : 8 * f + 8, :]
            strips[k, f, far : far + 1, :] = jnp.where(ok, msg[8 + f : 9 + f, :], 0.0)
            strips[k, f, near : near + 1, :] = jnp.where(ok, msg[f : f + 1, :], 0.0)

    at = lane + 2
    p, y = lax.div(at, step), lax.rem(at, step) - 2
    inside = ((p >= 2) | (gx > 0)) & ((p < nx + 2) | (gx < sizes[0] - 1))
    inside = inside & ((y >= 0) | (gy > 0)) & ((y < ny) | (gy < sizes[1] - 1))
    found = find_ports(dims, sizes, ports_ref)

    def x_up(v):
        return pltpu.roll(v, padded - step, 1)

    def x_down(v):
        return pltpu.roll(v, step, 1)

    def y_up(v):
        return pltpu.roll(v, padded - 1, 1)

    def y_down(v):
        return pltpu.roll(v, 1, 1)

    def z_up(v):
        return pltpu.roll(v, 7, 0)

    def z_down(v):
        return pltpu.roll(v, 1, 0)

    total = None
    results = []
    for k in range(2):
        ex, ey, ez, hx, hy, hz, coef = (strips[k, f] for f in range(FIELDS))
        first = -4 if k == 0 else nz - 4
        good = ((row >= 4) | has_low) if k == 0 else ((row < 4) | has_high)
        half = jnp.where(inside & good, magnetic_step, 0.0)
        for s in range(STEPS):
            cx = (y_up(ez) - ez) - (z_up(ey) - ey)
            cy = (z_up(ex) - ex) - (x_up(ez) - ez)
            cz = (x_up(ey) - ey) - (y_up(ex) - ex)
            hx, hy, hz = hx - half * cx, hy - half * cy, hz - half * cz
            cx = (hz - y_down(hz)) - (hy - z_down(hy))
            cy = (hx - z_down(hx)) - (hz - x_down(hz))
            cz = (hy - x_down(hy)) - (hx - y_down(hx))
            ex, ey, ez = ex + coef * cx, ey + coef * cy, ez + coef * cz
            for q, (sx, sy, sz) in enumerate(found):
                near = (sx >= -2) & (sx < nx + 2) & (sy >= -2) & (sy < ny + 2)
                hit = (row == sz - first) & (at == (sx + 2) * step + sy + 2) & near
                ez = ez + jnp.where(hit, amps_ref[s, q], 0.0)
            if k == 0:
                mine = (row == 4) | ((row == 5) & (s == 1))
            else:
                mine = (row == 3) | ((row == 2) & (s == 1))
            for c, e in enumerate((ex, ey, ez)):
                tile = FIELDS + c + 3 * (1 - s)
                one = jnp.where(mine, e * own_t[8 * tile : 8 * tile + 8, :], 0.0)
                total = one if total is None else total + one
        results.append((ex, ey, ez, hx, hy, hz))
    for c in range(6):
        rows_ref[8 * c : 8 * c + 8, :] = jnp.where(row < 4, results[1][c], results[0][c])
    line = jnp.sum(total, axis=0, keepdims=True)
    column = columns_of([(line_ref[...], ny, 0), (line, step, 2 * step + HALO)], nx, ny)
    turned[...] = column * mask_ref[...].astype(jnp.float32)
    width = ny // parts
    for shift in range(parts):
        owner = partner_of(gz, shift, parts)
        grads[shift][...] = turned[pl.ds(owner * width, width), :]
    ends_ref[...] = rows_ref[...]


def write_out(dims, e_s, h_s, ends_ref, e_out, h_out, spare, e_v, h_v, ends_t, sems):
    nx, ny, nz = dims
    lanes = nz // 128
    tiles = ny // 8
    plane = ny * lanes
    step = ny + HALO
    lane = lax.broadcasted_iota(jnp.int32, (8, 128), 1)
    spare[...] = jnp.zeros(spare.shape, jnp.float32)
    spare[0 : ends_ref.shape[0], :] = ends_ref[...]
    for b in range(spare.shape[1] // 128):
        ends_t[b * 128 : (b + 1) * 128, :] = jnp.transpose(spare[:, b * 128 : (b + 1) * 128])

    def one(x, carry):
        for t in range(tiles):
            v = ends_t[pl.ds(pl.multiple_of((x + 2) * step + HALO + t * 8, 8), 8), :]
            for c in range(6):
                src, dst = (e_s, e_v) if c < 3 else (h_s, h_v)
                placed = pltpu.roll(v, 124 - 8 * c, 1)
                for z in range(lanes):
                    here = pl.ds(pl.multiple_of(((x * tiles + t) * lanes + z) * 8, 8), 8)
                    out = src[c % 3, here, :]
                    if z == 0:
                        out = jnp.where(lane < 2, placed, out)
                    if z == lanes - 1:
                        out = jnp.where(lane >= 126, placed, out)
                    dst[c % 3, here, :] = out
        return carry

    chunk = nx // 4
    copies = []
    for c in range(4):
        lax.fori_loop(c * chunk, (c + 1) * chunk, one, 0, unroll=True)
        here = pl.ds(c * chunk * plane, chunk * plane)
        for k, (src, dst) in enumerate(((e_v, e_out), (h_v, h_out))):
            copy = pltpu.make_async_copy(src.at[:, here], dst.at[:, here], sems.at[2 * c + k])
            copy.start()
            copies.append(copy)
    for copy in copies:
        copy.wait()


def params(limit=12):
    return pltpu.CompilerParams(vmem_limit_bytes=limit * 1024 * 1024)


def body(sizes, e_adjoint, h_adjoint, snapshots, material, permittivity, design_mask, ports, amplitudes):
    permittivity = in_hbm(permittivity)
    permittivity = in_hbm(permittivity)
    dims = material.shape
    nx, ny, nz = dims
    lanes = nz // 128
    tiles = ny // 8
    plane = ny * lanes
    cells = nx * ny
    step = ny + HALO
    padded = -(-((nx + 4) * step + HALO) // 128) * 128
    f32, i32 = jnp.float32, jnp.int32
    xs, ys = swaps(sizes[0]), swaps(sizes[1])
    block, cube = jax.ShapeDtypeStruct, pltpu.VMEM

    shapes = [block((9 * plane + ny, 128), f32) for _ in xs]
    shapes += [block((9 * lanes + 1, nx, 128), f32) for _ in ys]
    shapes += [block((lanes, 4 * FIELDS, 128), f32) for _ in xs for _ in ys]
    buffers = []
    for _ in xs:
        tile = (2, tiles, lanes, 8, 128)
        buffers += [cube((3, *tile), f32), cube((3, *tile), f32), cube(tile, i32)]
    for _ in ys:
        tile = (nx * lanes * 8, 128)
        buffers += [cube((3, *tile), f32), cube((3, *tile), f32), cube(tile, i32)]
    n_copies = 3 * (len(xs) + len(ys)) + 1
    msgs = pl.pallas_call(
        functools.partial(send_faces, dims, sizes),
        out_shape=shapes,
        in_specs=[HBM, HBM, HBM, HBM],
        out_specs=[VM] * len(shapes),
        scratch_shapes=buffers
        + [pltpu.SMEM(permittivity.shape, f32), pltpu.SemaphoreType.DMA((n_copies,))],
        compiler_params=params(),
        name="send_faces",
    )(
        in_hbm(tiles_of(e_adjoint)),
        in_hbm(tiles_of(h_adjoint)),
        in_hbm(tiles_of(material)),
        permittivity,
    )
    e_v, h_v, m_v = in_vmem(tiled(e_adjoint)), in_vmem(tiled(h_adjoint)), in_vmem(tiled(material))
    snaps = in_hbm(snapshots.reshape(STEPS + 1, 3, cells, nz))
    coef_v, own_packed, s = pl.pallas_call(
        functools.partial(own_ends, dims),
        out_shape=[cube(m_v.shape, f32), cube((padded, 128), f32), cube(snaps.shape, snaps.dtype)],
        in_specs=[VM, VM, VM, HBM, SM],
        out_specs=[VM] * 3,
        scratch_shapes=[pltpu.SemaphoreType.DMA((3 * (STEPS + 1),))],
        compiler_params=params(),
        cost_estimate=pl.CostEstimate(flops=10**7, bytes_accessed=4 * 10**6, transcendentals=0),
        name="own_ends",
    )(e_v, h_v, m_v, snaps, permittivity)

    both = ("gx", "gy")

    def meet(x, y, tx, ty):
        if tx[x] == x or ty[y] == y:
            return x * sizes[1] + y
        return tx[x] * sizes[1] + ty[y]

    tables = [("gx", list(enumerate(swap_table(sizes[0], o)))) for o in xs]
    tables += [("gy", list(enumerate(swap_table(sizes[1], o)))) for o in ys]
    for ox in xs:
        for oy in ys:
            tx, ty = swap_table(sizes[0], ox), swap_table(sizes[1], oy)
            pairs = [
                (x * sizes[1] + y, meet(x, y, tx, ty))
                for x in range(sizes[0])
                for y in range(sizes[1])
            ]
            tables.append((both, pairs))
    got = [lax.ppermute(msg, axis, pairs) for msg, (axis, pairs) in zip(msgs, tables)]

    xh, yh, own_t, up, down = pl.pallas_call(
        functools.partial(unpack_faces, dims, sizes),
        out_shape=[
            cube((FIELDS, lanes, 4 * ny, 128), f32),
            cube((FIELDS, lanes, (nx + 4) * HALO, 128), f32),
            cube((128, padded), f32),
            block((16, padded), f32),
            block((16, padded), f32),
        ],
        in_specs=[VM] * (1 + len(got)),
        out_specs=[VM] * 5,
        scratch_shapes=[
            pltpu.VMEM((padded, 128), f32),
            pltpu.VMEM((4 * ny, 128), f32),
            pltpu.VMEM(((nx + 4) * HALO, 128), f32),
        ],
        compiler_params=params(),
        name="unpack_faces",
    )(own_packed, *got)

    parts = sizes[2]
    low = lax.ppermute(up, "gz", [(i, (i + 1) % parts) for i in range(parts)])
    high = lax.ppermute(down, "gz", [(i, (i - 1) % parts) for i in range(parts)])

    ported = ports.shape[0]
    e_s, h_s, line = pl.pallas_call(
        functools.partial(march, dims, sizes),
        out_shape=[cube(e_v.shape, f32), cube(h_v.shape, f32), block((1, cells), f32)],
        in_specs=[VM] * 6 + [SM, SM],
        out_specs=[VM] * 3,
        scratch_shapes=[
            pltpu.VMEM((3, nx + 4, step, nz), f32),
            pltpu.VMEM((3, nx + 4, step, nz), f32),
            pltpu.VMEM((3, nx + 4, step, nz), f32),
            pltpu.VMEM((step, nz), f32),
            pltpu.VMEM((ported, step, nz), f32),
            pltpu.VMEM((2, ny, nz), f32),
            pltpu.VMEM((cells, 128), f32),
        ],
        compiler_params=params(24),
        cost_estimate=pl.CostEstimate(flops=4 * 10**7, bytes_accessed=10**7, transcendentals=0),
        name="march",
    )(e_v, h_v, coef_v, xh, yh, s, ports, amplitudes)
    ends, *chunks = pl.pallas_call(
        functools.partial(finish_ends, dims, sizes),
        out_shape=[cube((48, padded), f32)] + [block((ny // parts, nx), f32)] * parts,
        in_specs=[VM] * 5 + [SM, SM],
        out_specs=[VM] * (1 + parts),
        scratch_shapes=[
            pltpu.VMEM((2, FIELDS, 8, padded), f32),
            pltpu.VMEM((ny, nx), f32),
            pltpu.VMEM((48, padded), f32),
        ],
        compiler_params=params(),
        name="finish_ends",
    )(own_t, low, high, line, design_mask.T, ports, amplitudes)
    e_out, h_out = pl.pallas_call(
        functools.partial(write_out, dims),
        out_shape=[block(e_v.shape, f32), block(h_v.shape, f32)],
        in_specs=[VM] * 3,
        out_specs=[HBM] * 2,
        scratch_shapes=[
            pltpu.VMEM((128, padded), f32),
            pltpu.VMEM(e_v.shape, f32),
            pltpu.VMEM(h_v.shape, f32),
            pltpu.VMEM((padded, 128), f32),
            pltpu.SemaphoreType.DMA((8,)),
        ],
        compiler_params=params(),
        cost_estimate=pl.CostEstimate(flops=10**7, bytes_accessed=8 * 10**6, transcendentals=0),
        name="write_out",
    )(e_s, h_s, ends)
    gradient = chunks[0]
    for shift in range(1, parts):
        gradient = gradient + lax.ppermute(
            chunks[shift], "gz", [(i, partner_of(i, shift, parts)) for i in range(parts)]
        )
    return untiled(e_out, dims), untiled(h_out, dims), gradient.T


def solution(mesh):
    placed = (
        P(None, "gx", "gy", "gz"),
        P(None, "gx", "gy", "gz"),
        P(None, None, "gx", "gy", "gz"),
        P("gx", "gy", "gz"),
        P(),
        P("gx", "gy"),
        P(),
        P(),
    )
    sizes = tuple(mesh.shape[axis] for axis in ("gx", "gy", "gz"))
    return jax.shard_map(
        functools.partial(body, sizes),
        mesh=mesh,
        in_specs=placed,
        out_specs=(P(None, "gx", "gy", "gz"), P(None, "gx", "gy", "gz"), P("gx", ("gy", "gz"))),
        check_vma=False,
    )
```

```python
import functools

import jax
import jax.numpy as jnp
from jax import lax
from jax.experimental import pallas as pl
from jax.experimental.pallas import tpu as pltpu
from jax.sharding import PartitionSpec as P

STEPS = 2
FIELDS = 7
HALO = 8

magnetic_step = 0.5
electric_step = 0.5

VM = pl.BlockSpec(memory_space=pltpu.VMEM)


HBM = pl.BlockSpec(memory_space=pltpu.HBM)


def in_hbm(array):
    return pltpu.with_memory_space_constraint(array, pltpu.HBM)


def in_vmem(array):
    return pltpu.with_memory_space_constraint(array, pltpu.VMEM)


def swap_table(size, odd):
    table = list(range(size))
    for i in range(odd, size - 1, 2):
        table[i], table[i + 1] = i + 1, i
    return table


def swaps(size):
    return [odd for odd in (0, 1) if odd + 1 < size]


def partner_of(index, shift, size):
    if size & (size - 1) == 0:
        return index ^ shift
    return (index + shift) % size


def sends_up(index, odd):
    return lax.rem(index, 2) == odd


def has_partner(index, size, odd):
    up = sends_up(index, odd)
    return (up & (index + 1 < size)) | (jnp.logical_not(up) & (index >= 1))


def coef_table(perm_ref):
    return [
        electric_step / jnp.full((1, 1), perm_ref[i], jnp.float32) for i in range(perm_ref.shape[0])
    ]


def coef_of(material, table):
    out = jnp.zeros(material.shape, jnp.float32)
    for i, value in enumerate(table):
        out = jnp.where(material == i, value, out)
    return out


def tiled(array):
    *lead, nx, ny, nz = array.shape
    n = len(lead)
    split = array.reshape(*lead, nx, ny // 8, 8, nz // 128, 128)
    order = tuple(range(n + 2)) + (n + 3, n + 2, n + 4)
    return split.transpose(order).reshape(*lead, nx * ny * nz // 128, 128)


def untiled(array, dims):
    nx, ny, nz = dims
    lead = array.shape[:-2]
    n = len(lead)
    split = array.reshape(*lead, nx, ny // 8, nz // 128, 8, 128)
    order = tuple(range(n + 2)) + (n + 3, n + 2, n + 4)
    return split.transpose(order).reshape(*lead, nx, ny, nz)


def tiles_of(array):
    *lead, nx, ny, nz = array.shape
    return tiled(array).reshape(*lead, nx, ny // 8, nz // 128, 8, 128)


def send_faces(dims, sizes, e_ref, h_ref, m_ref, perm_ref, *refs):
    nx, ny, nz = dims
    lanes = nz // 128
    tiles = ny // 8
    plane = ny * lanes
    gx, gy = lax.axis_index("gx"), lax.axis_index("gy")
    xs, ys = swaps(sizes[0]), swaps(sizes[1])
    n_out = len(xs) + len(ys) + len(xs) * len(ys)
    outs, table_ref, refs = refs[:n_out], refs[n_out], refs[n_out + 1 :]
    x_bufs, refs = refs[: 3 * len(xs)], refs[3 * len(xs) :]
    y_bufs, (perm_s, sems) = refs[: 3 * len(ys)], refs[3 * len(ys) :]
    copies = []

    def start(src, dst):
        copy = pltpu.make_async_copy(src, dst, sems.at[len(copies)])
        copy.start()
        copies.append(copy)

    for i, odd in enumerate(ys):
        up = sends_up(gy, odd)
        t, r = jnp.where(up, tiles - 1, 0), jnp.where(up, 6, 0)
        for k, ref in enumerate((e_ref, h_ref, m_ref)):
            src = ref.at[:, t, :, pl.ds(r, 2), :] if k == 2 else ref.at[:, :, t, :, pl.ds(r, 2), :]
            dst = y_bufs[3 * i + k]
            dst = dst.reshape(*dst.shape[:-2], nx, lanes, 8, 128)
            start(src, dst.at[:, :, pl.ds(0, 2), :] if k == 2 else dst.at[:, :, :, pl.ds(0, 2), :])
    for i, odd in enumerate(xs):
        first = pl.ds(jnp.where(sends_up(gx, odd), nx - 2, 0), 2)
        for k, ref in enumerate((e_ref, h_ref, m_ref)):
            start(ref.at[first] if k == 2 else ref.at[:, first], x_bufs[3 * i + k])
    start(perm_ref, perm_s)
    copies.pop().wait()
    table = coef_table(perm_s)
    for k, value in enumerate(table):
        table_ref[k : k + 1, :] = jnp.broadcast_to(value, (1, 128))
    lane = lax.broadcasted_iota(jnp.int32, (8, 128), 1)
    lane_n = lax.broadcasted_iota(jnp.int32, (nx, 128), 1)

    def z_up(v, lane):
        out = []
        for z in range(lanes):
            after = pltpu.roll(v[z + 1], 127, 1) if z + 1 < lanes else jnp.zeros_like(v[z])
            out.append(jnp.where(lane < 127, pltpu.roll(v[z], 127, 1), after))
        return out

    def row_up(v):
        rows = v.shape[0]
        row = lax.broadcasted_iota(jnp.int32, v.shape, 0)
        return jnp.where(row < rows - 1, pltpu.roll(v, rows - 1, 0), 0.0)

    step = lanes * 8
    for i, odd in enumerate(ys):
        for copy in copies[3 * i : 3 * i + 3]:
            copy.wait()
        up = sends_up(gy, odd)
        near, far = jnp.where(up, 1, 0), jnp.where(up, 0, 1)
        down = jnp.where(up, 0.0, magnetic_step)
        e_b, h_b, m_b = y_bufs[3 * i : 3 * i + 3]
        out = outs[len(xs) + i]

        def at(ref, c, which):
            return [ref[c, pl.ds(z * 8 + which, nx, stride=step), :] for z in range(lanes)]

        e_n = [at(e_b, c, near) for c in range(3)]
        h_n = [at(h_b, c, near) for c in range(3)]
        ex_f, ey_f, ez_f = (at(e_b, c, far) for c in range(3))
        hx_f, hz_f = at(h_b, 0, far), at(h_b, 2, far)
        ey_z = z_up(ey_f, lane_n)
        for z in range(lanes):
            for c in range(3):
                out[c * lanes + z] = e_n[c][z]
            out[3 * lanes + z] = h_n[0][z] - down * ez_f[z]
            out[4 * lanes + z] = h_n[1][z]
            out[5 * lanes + z] = h_n[2][z] + down * ex_f[z]
            out[6 * lanes + z] = coef_of(m_b[pl.ds(z * 8 + near, nx, stride=step), :], table)
            out[7 * lanes + z] = hx_f[z] + magnetic_step * (ez_f[z] + (ey_z[z] - ey_f[z]))
            out[8 * lanes + z] = hz_f[z] - magnetic_step * ((row_up(ey_f[z]) - ey_f[z]) + ex_f[z])
        out[9 * lanes] = ey_f[0]
    for i, odd in enumerate(xs):
        for copy in copies[3 * (len(ys) + i) : 3 * (len(ys) + i) + 3]:
            copy.wait()
        up = sends_up(gx, odd)
        near, far = jnp.where(up, 1, 0), jnp.where(up, 0, 1)
        down = jnp.where(up, 0.0, magnetic_step)
        e_b, h_b, m_b = x_bufs[3 * i : 3 * i + 3]
        out = outs[i]

        def put(k, t, z, v):
            out[pl.ds(k * plane + (t * lanes + z) * 8, 8), :] = v

        ex_y = [
            row_up(jnp.concatenate([e_b[0, far, t, z] for t in range(tiles)], axis=0))
            for z in range(lanes)
        ]
        for t in range(tiles):
            ex_z = z_up([e_b[0, far, t, z] for z in range(lanes)], lane)
            for z in range(lanes):
                ex_f, ey_f, ez_f = (e_b[c, far, t, z] for c in range(3))
                for c in range(3):
                    put(c, t, z, e_b[c, near, t, z])
                put(3, t, z, h_b[0, near, t, z])
                put(4, t, z, h_b[1, near, t, z] + down * ez_f)
                put(5, t, z, h_b[2, near, t, z] - down * ey_f)
                put(6, t, z, coef_of(m_b[near, t, z], table))
                put(7, t, z, h_b[1, far, t, z] - magnetic_step * ((ex_z[z] - ex_f) + ez_f))
                ex_up = ex_y[z][t * 8 : t * 8 + 8]
                put(8, t, z, h_b[2, far, t, z] + magnetic_step * (ey_f + (ex_up - ex_f)))
            out[pl.ds(9 * plane + t * 8, 8), :] = e_b[0, far, t, 0]
        for j, odd_y in enumerate(ys):
            up = sends_up(gy, odd_y)
            t = jnp.where(up, tiles - 1, 0)
            rows = (jnp.where(up, 7, 0), jnp.where(up, 6, 1))
            out = outs[len(xs) + len(ys) + i * len(ys) + j]
            for z in range(lanes):
                for f in range(FIELDS):
                    for k in range(4):
                        where = (near, far)[k // 2], t, z, pl.ds(rows[k % 2], 1)
                        if f < 6:
                            line = (e_b, h_b)[f // 3][(f % 3, *where)]
                        else:
                            line = coef_of(m_b[where], table)
                        out[z, pl.ds(4 * f + k, 1), :] = line


def turn_ends(parts, lane, first_field, after_field):
    out = None
    for k in range(first_field, after_field):
        first, last = parts(k)
        turned = pltpu.roll(jnp.where(lane < 64, first, last), 8 * k + 4, 1)
        out = turned if out is None else jnp.where(lane >= 8 * k, turned, out)
    return out


def own_ends(dims, e_v, h_v, m_v, snap_hbm, table_ref, coef_v, packed, snap_ref, sems):
    nx, ny, nz = dims
    lanes = nz // 128
    step = ny + HALO
    copies = []
    for t in range(STEPS + 1):
        for c in range(3):
            copy = pltpu.make_async_copy(snap_hbm.at[t, c], snap_ref.at[t, c], sems.at[3 * t + c])
            copy.start()
            copies.append(copy)
    table = [table_ref[k : k + 1, :] for k in range(table_ref.shape[0])]
    lane = lax.broadcasted_iota(jnp.int32, (8, 128), 1)
    tiles = ny // 8

    def fields(x, carry):
        for t in range(tiles):
            here = [
                pl.ds(pl.multiple_of(((x * tiles + t) * lanes + z) * 8, 8), 8) for z in range(lanes)
            ]
            for z in range(lanes):
                coef_v[here[z], :] = coef_of(m_v[here[z], :], table)

            def parts(k):
                if k < 3:
                    return e_v[k, here[0], :], e_v[k, here[-1], :]
                if k < 6:
                    return h_v[k - 3, here[0], :], h_v[k - 3, here[-1], :]
                return coef_v[here[0], :], coef_v[here[-1], :]

            row = pl.multiple_of((x + 2) * step + HALO + t * 8, 8)
            packed[pl.ds(row, 8), :] = turn_ends(parts, lane, 0, FIELDS)
        return carry

    lax.fori_loop(0, nx, fields, 0, unroll=16)

    for copy in copies:
        copy.wait()

    def changes(x, carry):
        index = pl.ds(pl.multiple_of(x * ny, ny), ny)
        change = []
        for c in range(3):
            s = [
                [
                    snap_ref[t, c, index, z * 128 : z * 128 + 128].astype(jnp.float32)
                    for z in (0, lanes - 1)
                ]
                for t in range(STEPS + 1)
            ]
            change.append([[s[t][z] - s[t + 1][z] for z in range(2)] for t in range(STEPS)])
        for t in range(tiles):

            def parts(k):
                pair = change[(k - FIELDS) % 3][1 - (k - FIELDS) // 3]
                return tuple(v[t * 8 : t * 8 + 8] for v in pair)

            here = pl.ds(pl.multiple_of((x + 2) * step + HALO + t * 8, 8), 8)
            after = turn_ends(parts, lane, FIELDS, FIELDS + 6)
            packed[here, :] = jnp.where(lane < 8 * FIELDS, packed[here, :], after)
        return carry

    lax.fori_loop(0, nx, changes, 0, unroll=16)


def unpack_faces(dims, sizes, own_packed, *refs):
    nx, ny, nz = dims
    lanes = nz // 128
    tiles = ny // 8
    plane = ny * lanes
    step = ny + HALO
    gx, gy = lax.axis_index("gx"), lax.axis_index("gy")
    xs, ys = swaps(sizes[0]), swaps(sizes[1])
    n_msgs = len(xs) + len(ys) + len(xs) * len(ys)
    msgs = refs[:n_msgs]
    xh, yh, own_t, up_ref, down_ref, packed, x_raw, y_raw = refs[n_msgs:]
    xh[...] = jnp.zeros(xh.shape, jnp.float32)
    x_raw[...] = jnp.zeros(x_raw.shape, jnp.float32)
    y_raw[...] = jnp.zeros(y_raw.shape, jnp.float32)
    for f in range(FIELDS):
        for z in range(lanes):
            if len(ys) < 2 or f < 3:
                yh[f, z] = jnp.zeros(yh.shape[2:], jnp.float32)
            else:
                for p in (0, 1, nx + 2, nx + 3):
                    yh[f, z, pl.ds(p * HALO, HALO), :] = jnp.zeros((HALO, 128), jnp.float32)

    def planes(odd):
        high = sends_up(gx, odd)
        return jnp.where(high, 2, 1), jnp.where(high, 3, 0)

    def lines(odd):
        high = sends_up(gy, odd)
        return jnp.where(high, 0, HALO - 1), jnp.where(high, 1, HALO - 2)

    for i, odd in enumerate(xs):
        ok = has_partner(gx, sizes[0], odd)
        near, far = planes(odd)
        msg = msgs[i]
        for t in range(tiles):
            for z in range(lanes):
                for k, f in enumerate((0, 1, 2, 3, 4, 5, 6, 4, 5)):
                    q = near if k < FIELDS else far
                    xh[f, z, pl.ds(pl.multiple_of(q * ny + t * 8, 8), 8), :] = jnp.where(
                        ok, msg[pl.ds(k * plane + (t * lanes + z) * 8, 8), :], 0.0
                    )
            x_raw[pl.ds(pl.multiple_of(far * ny + t * 8, 8), 8), :] = jnp.where(
                ok & (far == 0), msg[pl.ds(9 * plane + t * 8, 8), :], 0.0
            )
    for i, odd in enumerate(ys):
        ok = has_partner(gy, sizes[1], odd)
        near, far = lines(odd)
        msg = msgs[len(xs) + i]
        for z in range(lanes):
            for k, f in enumerate((0, 1, 2, 3, 4, 5, 6, 3, 5)):
                r = near if k < FIELDS else far
                yh[f, z, pl.ds(2 * HALO + r, nx, stride=HALO), :] = jnp.where(
                    ok, msg[k * lanes + z], 0.0
                )
        y_raw[pl.ds(2 * HALO + far, nx, stride=HALO), :] = jnp.where(
            ok & (far == HALO - 2), msg[9 * lanes], 0.0
        )
    for i, ox in enumerate(xs):
        for j, oy in enumerate(ys):
            ok = has_partner(gx, sizes[0], ox) & has_partner(gy, sizes[1], oy)
            px, py = planes(ox), lines(oy)
            px = [jnp.where(q < 2, q, q + nx) for q in px]
            msg = msgs[len(xs) + len(ys) + i * len(ys) + j]
            for z in range(lanes):
                for f in range(FIELDS):
                    for k in range(4):
                        yh[f, z, pl.ds(px[k // 2] * HALO + py[k % 2], 1), :] = jnp.where(
                            ok, msg[z, pl.ds(4 * f + k, 1), :], 0.0
                        )

    lane = lax.broadcasted_iota(jnp.int32, (8, 128), 1)
    upper = lax.broadcasted_iota(jnp.int32, (8, 128), 0) < HALO // 2

    def halo_rows(p, before, here):
        def tile(f, z):
            if f == FIELDS:
                return y_raw[here, :]
            return jnp.where(upper, yh[f, z, before, :], yh[f, z, here, :])

        packed[pl.ds(p * step if isinstance(p, int) else pl.multiple_of(p * step, 8), HALO), :] = (
            turn_ends(lambda f: (tile(f, 0), tile(f, lanes - 1)), lane, 0, FIELDS + 1)
        )

    def one(p, carry):
        halo_rows(
            p,
            pl.ds(pl.multiple_of((p - 1) * HALO, 8), HALO),
            pl.ds(pl.multiple_of(p * HALO, 8), HALO),
        )
        return carry

    halo_rows(0, pl.ds(0, HALO), pl.ds(0, HALO))
    lax.fori_loop(1, nx + 4, one, 0, unroll=True)
    last = pl.ds((nx + 3) * HALO, HALO)
    halo_rows(nx + 4, last, last)
    for q, p in enumerate((0, 1, nx + 2, nx + 3)):
        for t in range(tiles):
            index = pl.ds(q * ny + t * 8, 8)

            def parts(f):
                if f == FIELDS:
                    return x_raw[index, :], x_raw[index, :]
                return xh[f, 0, index, :], xh[f, lanes - 1, index, :]

            packed[pl.ds(p * step + HALO + t * 8, 8), :] = turn_ends(parts, lane, 0, FIELDS + 1)
    for x in range(nx):
        index = pl.ds((x + 2) * step + HALO, ny)
        packed[index, :] = own_packed[index, :]
    after = (nx + 4) * step + HALO
    padded = packed.shape[0]
    if padded > after:
        packed[after:, :] = jnp.zeros((padded - after, 128), jnp.float32)
    for b in range(padded // 128):
        here = pl.ds(b * 128, 128)
        block = jnp.transpose(packed[here, :])
        own_t[:, here] = block
        for f in range(FIELDS):
            up_ref[f : f + 1, here] = block[8 * f + 3 : 8 * f + 4, :]
            up_ref[8 + f : 9 + f, here] = block[8 * f + 2 : 8 * f + 3, :]
            down = [block[8 * f + 4 + k : 8 * f + 5 + k, :] for k in range(2)]
            if f < 2:
                at = lax.broadcasted_iota(jnp.int32, (1, 128), 1) + b * 128
                raw = (at >= HALO) & (at < step) if f == 0 else lax.rem(at, step) < HALO
                tail = [block[8 * FIELDS + 4 + k : 8 * FIELDS + 5 + k, :] for k in range(2)]
                down = [down[k] + jnp.where(raw, tail[k], 0.0) for k in range(2)]
            down_ref[f : f + 1, here] = down[0]
            down_ref[8 + f : 9 + f, here] = down[1]
    for row in (7, 15):
        up_ref[row : row + 1, :] = jnp.zeros((1, padded), jnp.float32)
        down_ref[row : row + 1, :] = jnp.zeros((1, padded), jnp.float32)


def split_index(index, size):
    if size & (size - 1) == 0:
        return lax.shift_right_logical(index, size.bit_length() - 1), index & (size - 1)
    return lax.div(index, size), lax.rem(index, size)


def steps_in(index, step):
    return ((index.astype(jnp.float32) + 0.5) * (1.0 / step)).astype(jnp.int32)


def columns_of(lines, nx, ny):
    spread, pick = [], []
    for line, step, first in lines:
        size = line.shape[1]
        at = lax.broadcasted_iota(jnp.int32, (ny, size), 1) - first
        y = lax.broadcasted_iota(jnp.int32, (ny, size), 0)
        ok = (at >= 0) & (at < nx * step) & (at - steps_in(at, step) * step == y)
        spread.append(jnp.where(ok, line, 0.0))
        at = lax.broadcasted_iota(jnp.int32, (nx, size), 1) - first
        x = lax.broadcasted_iota(jnp.int32, (nx, size), 0) * step
        pick.append(jnp.where((at >= x) & (at < x + step), 1.0, 0.0))
    left = jnp.concatenate(spread, axis=1)
    thirds = []
    for _ in range(3):
        part = left.astype(jnp.bfloat16)
        left = left - part.astype(jnp.float32)
        thirds.append(part)
    out = lax.dot_general(
        jnp.concatenate(thirds, axis=0),
        jnp.concatenate(pick, axis=1).astype(jnp.bfloat16),
        (((1,), (1,)), ((), ())),
        preferred_element_type=jnp.float32,
    )
    return out[0:ny] + (out[ny : 2 * ny] + out[2 * ny : 3 * ny])


def find_ports(dims, sizes, ports_ref):
    nx, ny, nz = dims
    gx, gy, gz = lax.axis_index("gx"), lax.axis_index("gy"), lax.axis_index("gz")
    found = []
    for q in range(ports_ref.shape[0]):
        line, z = split_index(ports_ref[q], nz * sizes[2])
        x, y = split_index(line, ny * sizes[1])
        found.append((x - gx * nx, y - gy * ny, z - gz * nz))
    return found


def march(dims, sizes, e_v, h_v, coef_v, xh, yh, snap_ref, ports_ref, amps_ref, *refs):
    nx, ny, nz = dims
    lanes = nz // 128
    tiles = ny // 8
    step = ny + HALO
    e_s, h_s, line_ref, spots_ref, gains_ref, e1, h1, h2, half_ref, struck, clean, sums = refs[:12]
    ports_s, amps_s, sems = refs[12:]
    copies = [
        pltpu.make_async_copy(ports_ref, ports_s, sems.at[0]),
        pltpu.make_async_copy(amps_ref, amps_s, sems.at[1]),
    ]
    for copy in copies:
        copy.start()
    gx, gy = lax.axis_index("gx"), lax.axis_index("gy")
    row = lax.broadcasted_iota(jnp.int32, (step, nz), 0)
    lane = lax.broadcasted_iota(jnp.int32, (step, nz), 1)
    inside = (row < ny) | ((row < ny + 2) & (gy < sizes[1] - 1)) | ((row >= ny + 4) & (gy > 0))
    half_ref[...] = jnp.where(inside, magnetic_step, 0.0)
    for k in range(2):
        clean[k] = jnp.where((lane[:ny] > k) & (lane[:ny] < nz - 1 - k), 1.0, 0.0)

    planes_struck = []

    def place_ports():
        for copy in copies:
            copy.wait()
        for q, (x, y, z) in enumerate(find_ports(dims, sizes, ports_s)):
            near = (y >= -2) & (y < ny + 2) & (z >= 0) & (z < nz)
            at = jnp.where(y < 0, y + step, y)
            struck[q] = jnp.where((row == at) & (lane == z) & near, 1.0, 0.0)
            planes_struck.append(x + 2)
            for k, v in enumerate((x, y, z)):
                spots_ref[3 * q + k : 3 * q + k + 1, :] = jnp.full((1, 128), v, jnp.int32)
            for k in range(STEPS):
                gains_ref[STEPS * q + k : STEPS * q + k + 1, :] = jnp.full(
                    (1, 128), amps_s[k, q], jnp.float32
                )

    def spot(x, t, z):
        index = ((x * tiles + t) * lanes + z) * 8
        return pl.ds(index if isinstance(index, int) else pl.multiple_of(index, 8), 8)

    def own_tile(f, p, t, z):
        if isinstance(p, int) and not 2 <= p < nx + 2:
            return xh[f, z, pl.ds((p if p < 2 else p - nx) * ny + t * 8, 8), :]
        if f < 3:
            return e_v[f, spot(p - 2, t, z), :]
        if f < 6:
            return h_v[f - 3, spot(p - 2, t, z), :]
        return coef_v[spot(p - 2, t, z), :]

    def aligned(index):
        return index if isinstance(index, int) else pl.multiple_of(index, 8)

    def load(f, p):
        columns = []
        for z in range(lanes):
            column = [own_tile(f, p, t, z) for t in range(tiles)]
            column.append(yh[f, z, pl.ds(aligned(p * HALO), HALO), :])
            columns.append(jnp.concatenate(column, axis=0))
        return jnp.concatenate(columns, axis=1)

    def load_own(f, p):
        return jnp.concatenate(
            [
                jnp.concatenate([own_tile(f, p, t, z) for t in range(tiles)], axis=0)
                for z in range(lanes)
            ],
            axis=1,
        )

    def put(ref, f, x, v):
        for t in range(tiles):
            for z in range(lanes):
                ref[f, spot(x, t, z), :] = v[t * 8 : t * 8 + 8, z * 128 : z * 128 + 128]

    def y_up(v):
        return pltpu.roll(v, step - 1, 0)

    def y_down(v):
        return pltpu.roll(v, 1, 0)

    def z_up(v):
        return pltpu.roll(v, nz - 1, 1)

    def z_down(v):
        return pltpu.roll(v, 1, 1)

    def new_h(half, ex, ey, ez, ey_x, ez_x, hx, hy, hz):
        cx = (y_up(ez) - ez) - (z_up(ey) - ey)
        cy = (z_up(ex) - ex) - (ez_x - ez)
        cz = (ey_x - ey) - (y_up(ex) - ex)
        return hx - half * cx, hy - half * cy, hz - half * cz

    def curl_h(hx, hy, hz, hy_x, hz_x):
        cx = (hz - y_down(hz)) - (hy - z_down(hy))
        cy = (hx - z_down(hx)) - (hz - hz_x)
        cz = (hy - hy_x) - (hx - y_down(hx))
        return cx, cy, cz

    def half_of(p):
        if isinstance(p, int) and p < 2:
            return half_ref[...] * jnp.where(gx == 0, 0.0, 1.0)
        if isinstance(p, int) and p >= nx + 2:
            return half_ref[...] * jnp.where(gx == sizes[0] - 1, 0.0, 1.0)
        return half_ref[...]

    def first_h(p):
        e = [load(f, p) for f in range(3)]
        h = [load(3 + f, p) for f in range(3)]
        out = new_h(half_of(p), *e, load(1, p + 1), load(2, p + 1), *h)
        for f in range(3):
            h1[f, p] = out[f]

    def first_e(p):
        e = [load(f, p) for f in range(3)]
        curl = curl_h(*[h1[f, p] for f in range(3)], h1[1, p - 1], h1[2, p - 1])
        coef = load(6, p)
        out = [e[f] + coef * curl[f] for f in range(3)]
        for f in range(3):
            e1[f, p] = out[f]

    def second_h(p):
        e = [e1[f, p] for f in range(3)]
        h = [h1[f, p] for f in range(3)]
        out = new_h(half_of(p), *e, e1[1, p + 1], e1[2, p + 1], *h)
        h2[0, p] = out[0]
        h2[1, p, 0:ny] = out[1][:ny]
        h2[2, p] = out[2]

    def second_e(p):
        h = [h2[f, p] for f in range(3)]
        curl = curl_h(*h, h2[1, p - 1], h2[2, p - 1])
        coef = load_own(6, p)
        old = [e1[f, p, 0:ny, 0:nz] for f in range(3)]
        new = [old[f] + coef * curl[f][:ny, :nz] for f in range(3)]
        x = p - 2
        index = pl.ds(aligned(x * ny), ny)
        total = None
        for f in range(3):
            put(e_s, f, x, new[f])
            put(h_s, f, x, h[f][:ny, :nz])
            s = [snap_ref[t, f, index, :].astype(jnp.float32) for t in range(STEPS + 1)]
            one = [old[f] * (s[0] - s[1]), new[f] * (s[1] - s[2])]
            total = one if total is None else [total[k] + one[k] for k in range(2)]
        total = total[0] * clean[0] + total[1] * clean[1]
        folded = total[:, 0:128]
        for at in range(128, nz, 128):
            folded = folded + total[:, at : at + 128]
        sums[index, :] = folded

    group = 4
    behind_e, behind_h, behind_last = group, 2 * group + 1, 3 * group + 1

    def some(p, behind, least, most):
        planes = [p - behind + i for i in range(group)]
        return [q for q in planes if not isinstance(q, int) or least <= q <= most]

    def strike(first, second):
        hit = None
        for at in planes_struck:
            for planes in (first, second):
                if planes:
                    here = (at >= planes[0]) & (at <= planes[-1])
                    hit = here if hit is None else hit | here

        @pl.when(hit)
        def _():
            for k, at in enumerate(planes_struck):
                for p in first:
                    amp = jnp.where(at == p, amps_s[0, k], 0.0)
                    e1[2, p] = e1[2, p] + struck[k] * amp
                for p in second:
                    x = p - 2
                    amp = jnp.where(at == p, amps_s[1, k], 0.0)
                    index = pl.ds(aligned(x * ny), ny)
                    s = [snap_ref[t, 2, index, :].astype(jnp.float32) for t in (1, 2)]
                    folded = jnp.zeros((ny, 128), jnp.float32)
                    for z in range(lanes):
                        here = slice(z * 128, z * 128 + 128)
                        gain = struck[k, 0:ny, here] * amp
                        folded = folded + gain * clean[1, :, here] * (s[0] - s[1])[:, here]
                        for t in range(tiles):
                            here = spot(x, t, z)
                            e_s[2, here, :] = e_s[2, here, :] + gain[t * 8 : t * 8 + 8]
                    sums[index, :] = sums[index, :] + folded

    def one(p):
        last = some(p, behind_last, 2, nx + 1)
        first = some(p, behind_e, 1, nx + 2)
        for q in last:
            second_e(q)
        for q in some(p, behind_h, 1, nx + 1):
            second_h(q)
        for q in first:
            first_e(q)
        for q in some(p, 0, 0, nx + 2):
            first_h(q)
        if first + last:
            if not planes_struck:
                place_ports()
            strike(first, last)

    def body(k, carry):
        one(start + k * group)
        return carry

    start = -(-(2 + behind_last) // group) * group
    passes = (nx + 1 - group - start) // group + 1
    for p in range(0, start, group):
        one(p)
    lax.fori_loop(0, passes, body, 0)
    for p in range(start + passes * group, nx + 2 + behind_last, group):
        one(p)
    for b in range(nx * ny // 128):
        here = pl.ds(b * 128, 128)
        line_ref[:, here] = jnp.sum(jnp.transpose(sums[here, :]), axis=0, keepdims=True)


def finish_ends(
    dims, sizes, own_t, low_ref, high_ref, line_ref, mask_ref, spots_ref, gains_ref, *refs
):
    nx, ny, nz = dims
    step = ny + HALO
    parts = sizes[2]
    ends_ref = refs[0]
    grads = refs[1 : 1 + parts]
    strips, turned, rows_ref = refs[1 + parts :]
    gx, gy, gz = lax.axis_index("gx"), lax.axis_index("gy"), lax.axis_index("gz")
    padded = own_t.shape[1]
    row = lax.broadcasted_iota(jnp.int32, (8, padded), 0)
    lane = lax.broadcasted_iota(jnp.int32, (8, padded), 1) - HALO
    has_low, has_high = gz > 0, gz < sizes[2] - 1
    for k, (msg, ok, far, near) in enumerate(((low_ref, has_low, 2, 3), (high_ref, has_high, 5, 4))):
        for f in range(FIELDS):
            strips[k, f] = own_t[8 * f : 8 * f + 8, :]
            strips[k, f, far : far + 1, :] = jnp.where(ok, msg[8 + f : 9 + f, :], 0.0)
            strips[k, f, near : near + 1, :] = jnp.where(ok, msg[f : f + 1, :], 0.0)

    at = lane + 2
    p = steps_in(at, step)
    y = at - p * step - 2
    inside = ((p >= 2) | (gx > 0)) & ((p < nx + 2) | (gx < sizes[0] - 1))
    inside = inside & ((y >= 0) | (gy > 0)) & ((y < ny) | (gy < sizes[1] - 1))
    found = [
        tuple(spots_ref[3 * q + k : 3 * q + k + 1, 0:1] for k in range(3))
        for q in range(spots_ref.shape[0] // 3)
    ]

    def x_up(v):
        return pltpu.roll(v, padded - step, 1)

    def x_down(v):
        return pltpu.roll(v, step, 1)

    def y_up(v):
        return pltpu.roll(v, padded - 1, 1)

    def y_down(v):
        return pltpu.roll(v, 1, 1)

    def z_up(v):
        return pltpu.roll(v, 7, 0)

    def z_down(v):
        return pltpu.roll(v, 1, 0)

    total = None
    results = []
    for k in range(2):
        ex, ey, ez, hx, hy, hz, coef = (strips[k, f] for f in range(FIELDS))
        first = -4 if k == 0 else nz - 4
        good = ((row >= 4) | has_low) if k == 0 else ((row < 4) | has_high)
        half = jnp.where(inside & good, magnetic_step, 0.0)
        for s in range(STEPS):
            cx = (y_up(ez) - ez) - (z_up(ey) - ey)
            cy = (z_up(ex) - ex) - (x_up(ez) - ez)
            cz = (x_up(ey) - ey) - (y_up(ex) - ex)
            hx, hy, hz = hx - half * cx, hy - half * cy, hz - half * cz
            cx = (hz - y_down(hz)) - (hy - z_down(hy))
            cy = (hx - z_down(hx)) - (hz - x_down(hz))
            cz = (hy - x_down(hy)) - (hx - y_down(hx))
            ex, ey, ez = ex + coef * cx, ey + coef * cy, ez + coef * cz
            for q, (sx, sy, sz) in enumerate(found):
                near = (sx >= -2) & (sx < nx + 2) & (sy >= -2) & (sy < ny + 2)
                hit = (row == sz - first) & (at == (sx + 2) * step + sy + 2) & near
                ez = ez + jnp.where(hit, gains_ref[STEPS * q + s : STEPS * q + s + 1, 0:1], 0.0)
            if k == 0:
                mine = (row == 4) | ((row == 5) & (s == 1))
            else:
                mine = (row == 3) | ((row == 2) & (s == 1))
            for c, e in enumerate((ex, ey, ez)):
                tile = FIELDS + c + 3 * (1 - s)
                one = jnp.where(mine, e * own_t[8 * tile : 8 * tile + 8, :], 0.0)
                total = one if total is None else total + one
        results.append((ex, ey, ez, hx, hy, hz))
    for c in range(6):
        rows_ref[8 * c : 8 * c + 8, :] = jnp.where(row < 4, results[1][c], results[0][c])
    line = jnp.sum(total, axis=0, keepdims=True)
    column = columns_of([(line_ref[...], ny, 0), (line, step, 2 * step + HALO)], nx, ny)
    turned[...] = column * mask_ref[...].astype(jnp.float32)
    width = ny // parts
    for shift in range(parts):
        owner = partner_of(gz, shift, parts)
        grads[shift][...] = turned[pl.ds(owner * width, width), :]
    ends_ref[...] = rows_ref[...]


def write_out(dims, e_s, h_s, ends_ref, e_out, h_out, spare, e_v, h_v, ends_t, sems):
    nx, ny, nz = dims
    lanes = nz // 128
    tiles = ny // 8
    plane = ny * lanes
    step = ny + HALO
    lane = lax.broadcasted_iota(jnp.int32, (8, 128), 1)
    spare[...] = jnp.zeros(spare.shape, jnp.float32)
    spare[0 : ends_ref.shape[0], :] = ends_ref[...]
    for b in range(spare.shape[1] // 128):
        ends_t[b * 128 : (b + 1) * 128, :] = jnp.transpose(spare[:, b * 128 : (b + 1) * 128])

    def one(x, carry):
        for t in range(tiles):
            v = ends_t[pl.ds(pl.multiple_of((x + 2) * step + HALO + t * 8, 8), 8), :]
            for c in range(6):
                src, dst = (e_s, e_v) if c < 3 else (h_s, h_v)
                placed = pltpu.roll(v, 124 - 8 * c, 1)
                for z in range(lanes):
                    here = pl.ds(pl.multiple_of(((x * tiles + t) * lanes + z) * 8, 8), 8)
                    out = src[c % 3, here, :]
                    if z == 0:
                        out = jnp.where(lane < 2, placed, out)
                    if z == lanes - 1:
                        out = jnp.where(lane >= 126, placed, out)
                    dst[c % 3, here, :] = out
        return carry

    chunk = nx // 4
    copies = []
    for c in range(4):
        lax.fori_loop(c * chunk, (c + 1) * chunk, one, 0, unroll=True)
        here = pl.ds(c * chunk * plane, chunk * plane)
        for k, (src, dst) in enumerate(((e_v, e_out), (h_v, h_out))):
            copy = pltpu.make_async_copy(src.at[:, here], dst.at[:, here], sems.at[2 * c + k])
            copy.start()
            copies.append(copy)
    for copy in copies:
        copy.wait()


def params(limit=12):
    return pltpu.CompilerParams(vmem_limit_bytes=limit * 1024 * 1024)


def body(sizes, e_adjoint, h_adjoint, snapshots, material, permittivity, design_mask, ports, amplitudes):
    permittivity = in_hbm(permittivity)
    permittivity = in_hbm(permittivity)
    dims = material.shape
    nx, ny, nz = dims
    lanes = nz // 128
    tiles = ny // 8
    plane = ny * lanes
    cells = nx * ny
    step = ny + HALO
    padded = -(-((nx + 4) * step + HALO) // 128) * 128
    f32, i32 = jnp.float32, jnp.int32
    xs, ys = swaps(sizes[0]), swaps(sizes[1])
    block, cube = jax.ShapeDtypeStruct, pltpu.VMEM

    shapes = [block((9 * plane + ny, 128), f32) for _ in xs]
    shapes += [block((9 * lanes + 1, nx, 128), f32) for _ in ys]
    shapes += [block((lanes, 4 * FIELDS, 128), f32) for _ in xs for _ in ys]
    buffers = []
    for _ in xs:
        tile = (2, tiles, lanes, 8, 128)
        buffers += [cube((3, *tile), f32), cube((3, *tile), f32), cube(tile, i32)]
    for _ in ys:
        tile = (nx * lanes * 8, 128)
        buffers += [cube((3, *tile), f32), cube((3, *tile), f32), cube(tile, i32)]
    n_copies = 3 * (len(xs) + len(ys)) + 1
    shapes += [block((permittivity.shape[0], 128), f32)]
    *msgs, table = pl.pallas_call(
        functools.partial(send_faces, dims, sizes),
        out_shape=shapes,
        in_specs=[HBM, HBM, HBM, HBM],
        out_specs=[VM] * len(shapes),
        scratch_shapes=buffers
        + [pltpu.SMEM(permittivity.shape, f32), pltpu.SemaphoreType.DMA((n_copies,))],
        compiler_params=params(),
        name="send_faces",
    )(
        in_hbm(tiles_of(e_adjoint)),
        in_hbm(tiles_of(h_adjoint)),
        in_hbm(tiles_of(material)),
        permittivity,
    )
    e_v, h_v, m_v = in_vmem(tiled(e_adjoint)), in_vmem(tiled(h_adjoint)), in_vmem(tiled(material))
    snaps = in_hbm(snapshots.reshape(STEPS + 1, 3, cells, nz))
    coef_v, own_packed, s = pl.pallas_call(
        functools.partial(own_ends, dims),
        out_shape=[cube(m_v.shape, f32), cube((padded, 128), f32), cube(snaps.shape, snaps.dtype)],
        in_specs=[VM, VM, VM, HBM, VM],
        out_specs=[VM] * 3,
        scratch_shapes=[pltpu.SemaphoreType.DMA((3 * (STEPS + 1),))],
        compiler_params=params(),
        cost_estimate=pl.CostEstimate(flops=10**7, bytes_accessed=4 * 10**6, transcendentals=0),
        name="own_ends",
    )(e_v, h_v, m_v, snaps, table)

    both = ("gx", "gy")

    def meet(x, y, tx, ty):
        if tx[x] == x or ty[y] == y:
            return x * sizes[1] + y
        return tx[x] * sizes[1] + ty[y]

    tables = [("gx", list(enumerate(swap_table(sizes[0], o)))) for o in xs]
    tables += [("gy", list(enumerate(swap_table(sizes[1], o)))) for o in ys]
    for ox in xs:
        for oy in ys:
            tx, ty = swap_table(sizes[0], ox), swap_table(sizes[1], oy)
            pairs = [
                (x * sizes[1] + y, meet(x, y, tx, ty))
                for x in range(sizes[0])
                for y in range(sizes[1])
            ]
            tables.append((both, pairs))
    got = [lax.ppermute(msg, axis, pairs) for msg, (axis, pairs) in zip(msgs, tables)]

    xh, yh, own_t, up, down = pl.pallas_call(
        functools.partial(unpack_faces, dims, sizes),
        out_shape=[
            cube((FIELDS, lanes, 4 * ny, 128), f32),
            cube((FIELDS, lanes, (nx + 4) * HALO, 128), f32),
            cube((128, padded), f32),
            block((16, padded), f32),
            block((16, padded), f32),
        ],
        in_specs=[VM] * (1 + len(got)),
        out_specs=[VM] * 5,
        scratch_shapes=[
            pltpu.VMEM((padded, 128), f32),
            pltpu.VMEM((4 * ny, 128), f32),
            pltpu.VMEM(((nx + 4) * HALO, 128), f32),
        ],
        compiler_params=params(),
        name="unpack_faces",
    )(own_packed, *got)

    parts = sizes[2]
    low = lax.ppermute(up, "gz", [(i, (i + 1) % parts) for i in range(parts)])
    high = lax.ppermute(down, "gz", [(i, (i - 1) % parts) for i in range(parts)])

    ported = ports.shape[0]
    e_s, h_s, line, spots, gains = pl.pallas_call(
        functools.partial(march, dims, sizes),
        out_shape=[cube(e_v.shape, f32), cube(h_v.shape, f32), block((1, cells), f32)]
        + [block((3 * ported, 128), i32), block((STEPS * ported, 128), f32)],
        in_specs=[VM] * 6 + [HBM, HBM],
        out_specs=[VM] * 5,
        scratch_shapes=[
            pltpu.VMEM((3, nx + 4, step, nz), f32),
            pltpu.VMEM((3, nx + 4, step, nz), f32),
            pltpu.VMEM((3, nx + 4, step, nz), f32),
            pltpu.VMEM((step, nz), f32),
            pltpu.VMEM((ported, step, nz), f32),
            pltpu.VMEM((2, ny, nz), f32),
            pltpu.VMEM((cells, 128), f32),
            pltpu.SMEM(ports.shape, i32),
            pltpu.SMEM(amplitudes.shape, f32),
            pltpu.SemaphoreType.DMA((2,)),
        ],
        compiler_params=params(24),
        cost_estimate=pl.CostEstimate(flops=4 * 10**7, bytes_accessed=10**7, transcendentals=0),
        name="march",
    )(e_v, h_v, coef_v, xh, yh, s, in_hbm(ports), in_hbm(amplitudes))
    ends, *chunks = pl.pallas_call(
        functools.partial(finish_ends, dims, sizes),
        out_shape=[cube((48, padded), f32)] + [block((ny // parts, nx), f32)] * parts,
        in_specs=[VM] * 7,
        out_specs=[VM] * (1 + parts),
        scratch_shapes=[
            pltpu.VMEM((2, FIELDS, 8, padded), f32),
            pltpu.VMEM((ny, nx), f32),
            pltpu.VMEM((48, padded), f32),
        ],
        compiler_params=params(),
        name="finish_ends",
    )(own_t, low, high, line, design_mask.T, spots, gains)
    e_out, h_out = pl.pallas_call(
        functools.partial(write_out, dims),
        out_shape=[block(e_v.shape, f32), block(h_v.shape, f32)],
        in_specs=[VM] * 3,
        out_specs=[HBM] * 2,
        scratch_shapes=[
            pltpu.VMEM((128, padded), f32),
            pltpu.VMEM(e_v.shape, f32),
            pltpu.VMEM(h_v.shape, f32),
            pltpu.VMEM((padded, 128), f32),
            pltpu.SemaphoreType.DMA((8,)),
        ],
        compiler_params=params(),
        cost_estimate=pl.CostEstimate(flops=10**7, bytes_accessed=8 * 10**6, transcendentals=0),
        name="write_out",
    )(e_s, h_s, ends)
    gradient = chunks[0]
    for shift in range(1, parts):
        gradient = gradient + lax.ppermute(
            chunks[shift], "gz", [(i, partner_of(i, shift, parts)) for i in range(parts)]
        )
    return untiled(e_out, dims), untiled(h_out, dims), gradient.T


def solution(mesh):
    placed = (
        P(None, "gx", "gy", "gz"),
        P(None, "gx", "gy", "gz"),
        P(None, None, "gx", "gy", "gz"),
        P("gx", "gy", "gz"),
        P(),
        P("gx", "gy"),
        P(),
        P(),
    )
    sizes = tuple(mesh.shape[axis] for axis in ("gx", "gy", "gz"))
    return jax.shard_map(
        functools.partial(body, sizes),
        mesh=mesh,
        in_specs=placed,
        out_specs=(P(None, "gx", "gy", "gz"), P(None, "gx", "gy", "gz"), P("gx", ("gy", "gz"))),
        check_vma=False,
    )
```

```python
import functools

import jax
import jax.numpy as jnp
from jax import lax
from jax.experimental import pallas as pl
from jax.experimental.pallas import tpu as pltpu
from jax.sharding import PartitionSpec as P

STEPS = 2
FIELDS = 7
HALO = 8

magnetic_step = 0.5
electric_step = 0.5

VM = pl.BlockSpec(memory_space=pltpu.VMEM)


HBM = pl.BlockSpec(memory_space=pltpu.HBM)


def in_hbm(array):
    return pltpu.with_memory_space_constraint(array, pltpu.HBM)


def in_vmem(array):
    return pltpu.with_memory_space_constraint(array, pltpu.VMEM)


def swap_table(size, odd):
    table = list(range(size))
    for i in range(odd, size - 1, 2):
        table[i], table[i + 1] = i + 1, i
    return table


def swaps(size):
    return [odd for odd in (0, 1) if odd + 1 < size]


def partner_of(index, shift, size):
    if size & (size - 1) == 0:
        return index ^ shift
    return (index + shift) % size


def sends_up(index, odd):
    return lax.rem(index, 2) == odd


def has_partner(index, size, odd):
    up = sends_up(index, odd)
    return (up & (index + 1 < size)) | (jnp.logical_not(up) & (index >= 1))


def coef_table(perm_ref):
    return [
        electric_step / jnp.full((1, 1), perm_ref[i], jnp.float32) for i in range(perm_ref.shape[0])
    ]


def coef_of(material, table):
    out = jnp.zeros(material.shape, jnp.float32)
    for i, value in enumerate(table):
        out = jnp.where(material == i, value, out)
    return out


def tiled(array):
    *lead, nx, ny, nz = array.shape
    n = len(lead)
    split = array.reshape(*lead, nx, ny // 8, 8, nz // 128, 128)
    order = tuple(range(n + 2)) + (n + 3, n + 2, n + 4)
    return split.transpose(order).reshape(*lead, nx * ny * nz // 128, 128)


def untiled(array, dims):
    nx, ny, nz = dims
    lead = array.shape[:-2]
    n = len(lead)
    split = array.reshape(*lead, nx, ny // 8, nz // 128, 8, 128)
    order = tuple(range(n + 2)) + (n + 3, n + 2, n + 4)
    return split.transpose(order).reshape(*lead, nx, ny, nz)


def tiles_of(array):
    *lead, nx, ny, nz = array.shape
    return tiled(array).reshape(*lead, nx, ny // 8, nz // 128, 8, 128)


def send_faces(dims, sizes, e_ref, h_ref, m_ref, perm_ref, *refs):
    nx, ny, nz = dims
    lanes = nz // 128
    tiles = ny // 8
    plane = ny * lanes
    gx, gy = lax.axis_index("gx"), lax.axis_index("gy")
    xs, ys = swaps(sizes[0]), swaps(sizes[1])
    n_out = len(xs) + len(ys) + len(xs) * len(ys)
    outs, table_ref, refs = refs[:n_out], refs[n_out], refs[n_out + 1 :]
    x_bufs, refs = refs[: 3 * len(xs)], refs[3 * len(xs) :]
    y_bufs, (perm_s, sems) = refs[: 3 * len(ys)], refs[3 * len(ys) :]
    copies = []

    def start(src, dst):
        copy = pltpu.make_async_copy(src, dst, sems.at[len(copies)])
        copy.start()
        copies.append(copy)

    for i, odd in enumerate(ys):
        up = sends_up(gy, odd)
        t, r = jnp.where(up, tiles - 1, 0), jnp.where(up, 6, 0)
        for k, ref in enumerate((e_ref, h_ref, m_ref)):
            src = ref.at[:, t, :, pl.ds(r, 2), :] if k == 2 else ref.at[:, :, t, :, pl.ds(r, 2), :]
            dst = y_bufs[3 * i + k]
            dst = dst.reshape(*dst.shape[:-2], nx, lanes, 8, 128)
            start(src, dst.at[:, :, pl.ds(0, 2), :] if k == 2 else dst.at[:, :, :, pl.ds(0, 2), :])
    for i, odd in enumerate(xs):
        first = pl.ds(jnp.where(sends_up(gx, odd), nx - 2, 0), 2)
        for k, ref in enumerate((e_ref, h_ref, m_ref)):
            start(ref.at[first] if k == 2 else ref.at[:, first], x_bufs[3 * i + k])
    start(perm_ref, perm_s)
    copies.pop().wait()
    table = coef_table(perm_s)
    for k, value in enumerate(table):
        table_ref[k : k + 1, :] = jnp.broadcast_to(value, (1, 128))
    lane = lax.broadcasted_iota(jnp.int32, (8, 128), 1)
    lane_n = lax.broadcasted_iota(jnp.int32, (nx, 128), 1)

    def z_up(v, lane):
        out = []
        for z in range(lanes):
            after = pltpu.roll(v[z + 1], 127, 1) if z + 1 < lanes else jnp.zeros_like(v[z])
            out.append(jnp.where(lane < 127, pltpu.roll(v[z], 127, 1), after))
        return out

    def row_up(v):
        rows = v.shape[0]
        row = lax.broadcasted_iota(jnp.int32, v.shape, 0)
        return jnp.where(row < rows - 1, pltpu.roll(v, rows - 1, 0), 0.0)

    step = lanes * 8
    for i, odd in enumerate(ys):
        for copy in copies[3 * i : 3 * i + 3]:
            copy.wait()
        up = sends_up(gy, odd)
        near, far = jnp.where(up, 1, 0), jnp.where(up, 0, 1)
        down = jnp.where(up, 0.0, magnetic_step)
        e_b, h_b, m_b = y_bufs[3 * i : 3 * i + 3]
        out = outs[len(xs) + i]

        def at(ref, c, which):
            return [ref[c, pl.ds(z * 8 + which, nx, stride=step), :] for z in range(lanes)]

        def put(k, z, v):
            out[pl.ds((k * lanes + z) * nx, nx), :] = v

        e_n = [at(e_b, c, near) for c in range(3)]
        h_n = [at(h_b, c, near) for c in range(3)]
        ex_f, ey_f, ez_f = (at(e_b, c, far) for c in range(3))
        hx_f, hz_f = at(h_b, 0, far), at(h_b, 2, far)
        ey_z = z_up(ey_f, lane_n)
        for z in range(lanes):
            for c in range(3):
                put(c, z, e_n[c][z])
            put(3, z, h_n[0][z] - down * ez_f[z])
            put(4, z, h_n[1][z])
            put(5, z, h_n[2][z] + down * ex_f[z])
            put(6, z, coef_of(m_b[pl.ds(z * 8 + near, nx, stride=step), :], table))
            put(7, z, hx_f[z] + magnetic_step * (ez_f[z] + (ey_z[z] - ey_f[z])))
            put(8, z, hz_f[z] - magnetic_step * ((row_up(ey_f[z]) - ey_f[z]) + ex_f[z]))
        first = jnp.concatenate([ey_f[0], jnp.zeros((128 - nx, 128), jnp.float32)], axis=0)
        out[pl.ds(9 * lanes * nx, 8), :] = jnp.transpose(first)[0:8]
    for i, odd in enumerate(xs):
        for copy in copies[3 * (len(ys) + i) : 3 * (len(ys) + i) + 3]:
            copy.wait()
        up = sends_up(gx, odd)
        near, far = jnp.where(up, 1, 0), jnp.where(up, 0, 1)
        down = jnp.where(up, 0.0, magnetic_step)
        e_b, h_b, m_b = x_bufs[3 * i : 3 * i + 3]
        out = outs[i]

        def put(k, t, z, v):
            out[pl.ds(k * plane + (t * lanes + z) * 8, 8), :] = v

        ex_y = [
            row_up(jnp.concatenate([e_b[0, far, t, z] for t in range(tiles)], axis=0))
            for z in range(lanes)
        ]
        for t in range(tiles):
            ex_z = z_up([e_b[0, far, t, z] for z in range(lanes)], lane)
            for z in range(lanes):
                ex_f, ey_f, ez_f = (e_b[c, far, t, z] for c in range(3))
                for c in range(3):
                    put(c, t, z, e_b[c, near, t, z])
                put(3, t, z, h_b[0, near, t, z])
                put(4, t, z, h_b[1, near, t, z] + down * ez_f)
                put(5, t, z, h_b[2, near, t, z] - down * ey_f)
                put(6, t, z, coef_of(m_b[near, t, z], table))
                put(7, t, z, h_b[1, far, t, z] - magnetic_step * ((ex_z[z] - ex_f) + ez_f))
                ex_up = ex_y[z][t * 8 : t * 8 + 8]
                put(8, t, z, h_b[2, far, t, z] + magnetic_step * (ey_f + (ex_up - ex_f)))
            out[pl.ds(9 * plane + t * 8, 8), :] = e_b[0, far, t, 0]
        for j, odd_y in enumerate(ys):
            up = sends_up(gy, odd_y)
            t = jnp.where(up, tiles - 1, 0)
            rows = (jnp.where(up, 7, 0), jnp.where(up, 6, 1))
            out = outs[len(xs) + len(ys) + i * len(ys) + j]
            for z in range(lanes):
                for f in range(FIELDS):
                    for k in range(4):
                        where = (near, far)[k // 2], t, z, pl.ds(rows[k % 2], 1)
                        if f < 6:
                            line = (e_b, h_b)[f // 3][(f % 3, *where)]
                        else:
                            line = coef_of(m_b[where], table)
                        out[z, pl.ds(4 * f + k, 1), :] = line


def turn_ends(parts, lane, first_field, after_field):
    out = None
    for k in range(first_field, after_field):
        first, last = parts(k)
        turned = pltpu.roll(jnp.where(lane < 64, first, last), 8 * k + 4, 1)
        out = turned if out is None else jnp.where(lane >= 8 * k, turned, out)
    return out


def own_ends(dims, e_v, h_v, m_v, snap_hbm, table_ref, coef_v, packed, snap_ref, sems):
    nx, ny, nz = dims
    lanes = nz // 128
    step = ny + HALO
    copies = []
    for t in range(STEPS + 1):
        for c in range(3):
            copy = pltpu.make_async_copy(snap_hbm.at[t, c], snap_ref.at[t, c], sems.at[3 * t + c])
            copy.start()
            copies.append(copy)
    table = [table_ref[k : k + 1, :] for k in range(table_ref.shape[0])]
    lane = lax.broadcasted_iota(jnp.int32, (8, 128), 1)
    tiles = ny // 8

    def fields(x, carry):
        for t in range(tiles):
            here = [
                pl.ds(pl.multiple_of(((x * tiles + t) * lanes + z) * 8, 8), 8) for z in range(lanes)
            ]
            for z in range(lanes):
                coef_v[here[z], :] = coef_of(m_v[here[z], :], table)

            def parts(k):
                if k < 3:
                    return e_v[k, here[0], :], e_v[k, here[-1], :]
                if k < 6:
                    return h_v[k - 3, here[0], :], h_v[k - 3, here[-1], :]
                return coef_v[here[0], :], coef_v[here[-1], :]

            row = pl.multiple_of((x + 2) * step + HALO + t * 8, 8)
            packed[pl.ds(row, 8), :] = turn_ends(parts, lane, 0, FIELDS)
        return carry

    lax.fori_loop(0, nx, fields, 0, unroll=16)

    for copy in copies:
        copy.wait()

    def changes(x, carry):
        index = pl.ds(pl.multiple_of(x * ny, ny), ny)
        change = []
        for c in range(3):
            s = [
                [
                    snap_ref[t, c, index, z * 128 : z * 128 + 128].astype(jnp.float32)
                    for z in (0, lanes - 1)
                ]
                for t in range(STEPS + 1)
            ]
            change.append([[s[t][z] - s[t + 1][z] for z in range(2)] for t in range(STEPS)])
        for t in range(tiles):

            def parts(k):
                pair = change[(k - FIELDS) % 3][1 - (k - FIELDS) // 3]
                return tuple(v[t * 8 : t * 8 + 8] for v in pair)

            here = pl.ds(pl.multiple_of((x + 2) * step + HALO + t * 8, 8), 8)
            after = turn_ends(parts, lane, FIELDS, FIELDS + 6)
            packed[here, :] = jnp.where(lane < 8 * FIELDS, packed[here, :], after)
        return carry

    lax.fori_loop(0, nx, changes, 0, unroll=16)


def unpack_faces(dims, sizes, own_packed, *refs):
    nx, ny, nz = dims
    lanes = nz // 128
    tiles = ny // 8
    plane = ny * lanes
    step = ny + HALO
    gx, gy = lax.axis_index("gx"), lax.axis_index("gy")
    xs, ys = swaps(sizes[0]), swaps(sizes[1])
    n_msgs = len(xs) + len(ys) + len(xs) * len(ys)
    msgs = refs[:n_msgs]
    xh, yh, own_t, up_ref, down_ref, packed, x_raw, y_raw = refs[n_msgs:]
    xh[...] = jnp.zeros(xh.shape, jnp.float32)
    x_raw[...] = jnp.zeros(x_raw.shape, jnp.float32)
    y_raw[...] = jnp.zeros(y_raw.shape, jnp.float32)
    for f in range(FIELDS):
        for z in range(lanes):
            if len(ys) < 2 or f < 3:
                yh[f, z] = jnp.zeros(yh.shape[2:], jnp.float32)
            else:
                for p in (0, 1, nx + 2, nx + 3):
                    yh[f, z, pl.ds(p * HALO, HALO), :] = jnp.zeros((HALO, 128), jnp.float32)

    def planes(odd):
        high = sends_up(gx, odd)
        return jnp.where(high, 2, 1), jnp.where(high, 3, 0)

    def lines(odd):
        high = sends_up(gy, odd)
        return jnp.where(high, 0, HALO - 1), jnp.where(high, 1, HALO - 2)

    for i, odd in enumerate(xs):
        ok = has_partner(gx, sizes[0], odd)
        near, far = planes(odd)
        msg = msgs[i]
        for t in range(tiles):
            for z in range(lanes):
                for k, f in enumerate((0, 1, 2, 3, 4, 5, 6, 4, 5)):
                    q = near if k < FIELDS else far
                    xh[f, z, pl.ds(pl.multiple_of(q * ny + t * 8, 8), 8), :] = jnp.where(
                        ok, msg[pl.ds(k * plane + (t * lanes + z) * 8, 8), :], 0.0
                    )
            x_raw[pl.ds(pl.multiple_of(far * ny + t * 8, 8), 8), :] = jnp.where(
                ok & (far == 0), msg[pl.ds(9 * plane + t * 8, 8), :], 0.0
            )
    for i, odd in enumerate(ys):
        ok = has_partner(gy, sizes[1], odd)
        near, far = lines(odd)
        msg = msgs[len(xs) + i]
        for z in range(lanes):
            for k, f in enumerate((0, 1, 2, 3, 4, 5, 6, 3, 5)):
                r = near if k < FIELDS else far
                yh[f, z, pl.ds(2 * HALO + r, nx, stride=HALO), :] = jnp.where(
                    ok, msg[pl.ds((k * lanes + z) * nx, nx), :], 0.0
                )
        raw = jnp.where(ok & (far == HALO - 2), msg[pl.ds(9 * lanes * nx, 8), :], 0.0)
        raw = jnp.concatenate([raw, jnp.zeros((120, 128), jnp.float32)], axis=0)
        y_raw[pl.ds(2 * HALO + far, nx, stride=HALO), :] = jnp.transpose(raw)[0:nx]
    for i, ox in enumerate(xs):
        for j, oy in enumerate(ys):
            ok = has_partner(gx, sizes[0], ox) & has_partner(gy, sizes[1], oy)
            px, py = planes(ox), lines(oy)
            px = [jnp.where(q < 2, q, q + nx) for q in px]
            msg = msgs[len(xs) + len(ys) + i * len(ys) + j]
            for z in range(lanes):
                for f in range(FIELDS):
                    for k in range(4):
                        yh[f, z, pl.ds(px[k // 2] * HALO + py[k % 2], 1), :] = jnp.where(
                            ok, msg[z, pl.ds(4 * f + k, 1), :], 0.0
                        )

    lane = lax.broadcasted_iota(jnp.int32, (8, 128), 1)
    upper = lax.broadcasted_iota(jnp.int32, (8, 128), 0) < HALO // 2

    def halo_rows(p, before, here):
        def tile(f, z):
            if f == FIELDS:
                return y_raw[here, :]
            return jnp.where(upper, yh[f, z, before, :], yh[f, z, here, :])

        packed[pl.ds(p * step if isinstance(p, int) else pl.multiple_of(p * step, 8), HALO), :] = (
            turn_ends(lambda f: (tile(f, 0), tile(f, lanes - 1)), lane, 0, FIELDS + 1)
        )

    def one(p, carry):
        halo_rows(
            p,
            pl.ds(pl.multiple_of((p - 1) * HALO, 8), HALO),
            pl.ds(pl.multiple_of(p * HALO, 8), HALO),
        )
        return carry

    halo_rows(0, pl.ds(0, HALO), pl.ds(0, HALO))
    lax.fori_loop(1, nx + 4, one, 0, unroll=True)
    last = pl.ds((nx + 3) * HALO, HALO)
    halo_rows(nx + 4, last, last)
    for q, p in enumerate((0, 1, nx + 2, nx + 3)):
        for t in range(tiles):
            index = pl.ds(q * ny + t * 8, 8)

            def parts(f):
                if f == FIELDS:
                    return x_raw[index, :], x_raw[index, :]
                return xh[f, 0, index, :], xh[f, lanes - 1, index, :]

            packed[pl.ds(p * step + HALO + t * 8, 8), :] = turn_ends(parts, lane, 0, FIELDS + 1)
    for x in range(nx):
        index = pl.ds((x + 2) * step + HALO, ny)
        packed[index, :] = own_packed[index, :]
    after = (nx + 4) * step + HALO
    padded = packed.shape[0]
    if padded > after:
        packed[after:, :] = jnp.zeros((padded - after, 128), jnp.float32)
    for b in range(padded // 128):
        here = pl.ds(b * 128, 128)
        block = jnp.transpose(packed[here, :])
        own_t[:, here] = block
        for f in range(FIELDS):
            up_ref[f : f + 1, here] = block[8 * f + 3 : 8 * f + 4, :]
            up_ref[8 + f : 9 + f, here] = block[8 * f + 2 : 8 * f + 3, :]
            down = [block[8 * f + 4 + k : 8 * f + 5 + k, :] for k in range(2)]
            if f < 2:
                at = lax.broadcasted_iota(jnp.int32, (1, 128), 1) + b * 128
                raw = (at >= HALO) & (at < step) if f == 0 else lax.rem(at, step) < HALO
                tail = [block[8 * FIELDS + 4 + k : 8 * FIELDS + 5 + k, :] for k in range(2)]
                down = [down[k] + jnp.where(raw, tail[k], 0.0) for k in range(2)]
            down_ref[f : f + 1, here] = down[0]
            down_ref[8 + f : 9 + f, here] = down[1]
    for row in (7, 15):
        up_ref[row : row + 1, :] = jnp.zeros((1, padded), jnp.float32)
        down_ref[row : row + 1, :] = jnp.zeros((1, padded), jnp.float32)


def split_index(index, size):
    if size & (size - 1) == 0:
        return lax.shift_right_logical(index, size.bit_length() - 1), index & (size - 1)
    return lax.div(index, size), lax.rem(index, size)


def steps_in(index, step):
    return ((index.astype(jnp.float32) + 0.5) * (1.0 / step)).astype(jnp.int32)


def columns_of(lines, nx, ny):
    spread, pick = [], []
    for line, step, first in lines:
        size = line.shape[1]
        at = lax.broadcasted_iota(jnp.int32, (ny, size), 1) - first
        y = lax.broadcasted_iota(jnp.int32, (ny, size), 0)
        ok = (at >= 0) & (at < nx * step) & (at - steps_in(at, step) * step == y)
        spread.append(jnp.where(ok, line, 0.0))
        at = lax.broadcasted_iota(jnp.int32, (nx, size), 1) - first
        x = lax.broadcasted_iota(jnp.int32, (nx, size), 0) * step
        pick.append(jnp.where((at >= x) & (at < x + step), 1.0, 0.0))
    left = jnp.concatenate(spread, axis=1)
    thirds = []
    for _ in range(3):
        part = left.astype(jnp.bfloat16)
        left = left - part.astype(jnp.float32)
        thirds.append(part)
    out = lax.dot_general(
        jnp.concatenate(thirds, axis=0),
        jnp.concatenate(pick, axis=1).astype(jnp.bfloat16),
        (((1,), (1,)), ((), ())),
        preferred_element_type=jnp.float32,
    )
    return out[0:ny] + (out[ny : 2 * ny] + out[2 * ny : 3 * ny])


def find_ports(dims, sizes, ports_ref):
    nx, ny, nz = dims
    gx, gy, gz = lax.axis_index("gx"), lax.axis_index("gy"), lax.axis_index("gz")
    found = []
    for q in range(ports_ref.shape[0]):
        line, z = split_index(ports_ref[q], nz * sizes[2])
        x, y = split_index(line, ny * sizes[1])
        found.append((x - gx * nx, y - gy * ny, z - gz * nz))
    return found


def march(dims, sizes, e_v, h_v, coef_v, xh, yh, snap_ref, ports_ref, amps_ref, *refs):
    nx, ny, nz = dims
    lanes = nz // 128
    tiles = ny // 8
    step = ny + HALO
    e_s, h_s, line_ref, spots_ref, gains_ref, e1, h1, h2, half_ref, struck, clean, sums = refs[:12]
    ports_s, amps_s, sems = refs[12:]
    copies = [
        pltpu.make_async_copy(ports_ref, ports_s, sems.at[0]),
        pltpu.make_async_copy(amps_ref, amps_s, sems.at[1]),
    ]
    for copy in copies:
        copy.start()
    gx, gy = lax.axis_index("gx"), lax.axis_index("gy")
    row = lax.broadcasted_iota(jnp.int32, (step, nz), 0)
    lane = lax.broadcasted_iota(jnp.int32, (step, nz), 1)
    inside = (row < ny) | ((row < ny + 2) & (gy < sizes[1] - 1)) | ((row >= ny + 4) & (gy > 0))
    half_ref[...] = jnp.where(inside, magnetic_step, 0.0)
    for k in range(2):
        clean[k] = jnp.where((lane[:ny] > k) & (lane[:ny] < nz - 1 - k), 1.0, 0.0)

    planes_struck = []

    def place_ports():
        for copy in copies:
            copy.wait()
        for q, (x, y, z) in enumerate(find_ports(dims, sizes, ports_s)):
            near = (y >= -2) & (y < ny + 2) & (z >= 0) & (z < nz)
            at = jnp.where(y < 0, y + step, y)
            struck[q] = jnp.where((row == at) & (lane == z) & near, 1.0, 0.0)
            planes_struck.append(x + 2)
            for k, v in enumerate((x, y, z)):
                spots_ref[3 * q + k : 3 * q + k + 1, :] = jnp.full((1, 128), v, jnp.int32)
            for k in range(STEPS):
                gains_ref[STEPS * q + k : STEPS * q + k + 1, :] = jnp.full(
                    (1, 128), amps_s[k, q], jnp.float32
                )

    def spot(x, t, z):
        index = ((x * tiles + t) * lanes + z) * 8
        return pl.ds(index if isinstance(index, int) else pl.multiple_of(index, 8), 8)

    def own_tile(f, p, t, z):
        if isinstance(p, int) and not 2 <= p < nx + 2:
            return xh[f, z, pl.ds((p if p < 2 else p - nx) * ny + t * 8, 8), :]
        if f < 3:
            return e_v[f, spot(p - 2, t, z), :]
        if f < 6:
            return h_v[f - 3, spot(p - 2, t, z), :]
        return coef_v[spot(p - 2, t, z), :]

    def aligned(index):
        return index if isinstance(index, int) else pl.multiple_of(index, 8)

    def load(f, p):
        columns = []
        for z in range(lanes):
            column = [own_tile(f, p, t, z) for t in range(tiles)]
            column.append(yh[f, z, pl.ds(aligned(p * HALO), HALO), :])
            columns.append(jnp.concatenate(column, axis=0))
        return jnp.concatenate(columns, axis=1)

    def load_own(f, p):
        return jnp.concatenate(
            [
                jnp.concatenate([own_tile(f, p, t, z) for t in range(tiles)], axis=0)
                for z in range(lanes)
            ],
            axis=1,
        )

    def put(ref, f, x, v):
        for t in range(tiles):
            for z in range(lanes):
                ref[f, spot(x, t, z), :] = v[t * 8 : t * 8 + 8, z * 128 : z * 128 + 128]

    def y_up(v):
        return pltpu.roll(v, step - 1, 0)

    def y_down(v):
        return pltpu.roll(v, 1, 0)

    def z_up(v):
        return pltpu.roll(v, nz - 1, 1)

    def z_down(v):
        return pltpu.roll(v, 1, 1)

    def new_h(half, ex, ey, ez, ey_x, ez_x, hx, hy, hz):
        cx = (y_up(ez) - ez) - (z_up(ey) - ey)
        cy = (z_up(ex) - ex) - (ez_x - ez)
        cz = (ey_x - ey) - (y_up(ex) - ex)
        return hx - half * cx, hy - half * cy, hz - half * cz

    def curl_h(hx, hy, hz, hy_x, hz_x):
        cx = (hz - y_down(hz)) - (hy - z_down(hy))
        cy = (hx - z_down(hx)) - (hz - hz_x)
        cz = (hy - hy_x) - (hx - y_down(hx))
        return cx, cy, cz

    def half_of(p):
        if isinstance(p, int) and p < 2:
            return half_ref[...] * jnp.where(gx == 0, 0.0, 1.0)
        if isinstance(p, int) and p >= nx + 2:
            return half_ref[...] * jnp.where(gx == sizes[0] - 1, 0.0, 1.0)
        return half_ref[...]

    def first_h(p):
        e = [load(f, p) for f in range(3)]
        h = [load(3 + f, p) for f in range(3)]
        out = new_h(half_of(p), *e, load(1, p + 1), load(2, p + 1), *h)
        for f in range(3):
            h1[f, p] = out[f]

    def first_e(p):
        e = [load(f, p) for f in range(3)]
        curl = curl_h(*[h1[f, p] for f in range(3)], h1[1, p - 1], h1[2, p - 1])
        coef = load(6, p)
        out = [e[f] + coef * curl[f] for f in range(3)]
        for f in range(3):
            e1[f, p] = out[f]

    def second_h(p):
        e = [e1[f, p] for f in range(3)]
        h = [h1[f, p] for f in range(3)]
        out = new_h(half_of(p), *e, e1[1, p + 1], e1[2, p + 1], *h)
        h2[0, p] = out[0]
        h2[1, p, 0:ny] = out[1][:ny]
        h2[2, p] = out[2]

    def second_e(p):
        h = [h2[f, p] for f in range(3)]
        curl = curl_h(*h, h2[1, p - 1], h2[2, p - 1])
        coef = load_own(6, p)
        old = [e1[f, p, 0:ny, 0:nz] for f in range(3)]
        new = [old[f] + coef * curl[f][:ny, :nz] for f in range(3)]
        x = p - 2
        index = pl.ds(aligned(x * ny), ny)
        total = None
        for f in range(3):
            put(e_s, f, x, new[f])
            put(h_s, f, x, h[f][:ny, :nz])
            s = [snap_ref[t, f, index, :].astype(jnp.float32) for t in range(STEPS + 1)]
            one = [old[f] * (s[0] - s[1]), new[f] * (s[1] - s[2])]
            total = one if total is None else [total[k] + one[k] for k in range(2)]
        total = total[0] * clean[0] + total[1] * clean[1]
        folded = total[:, 0:128]
        for at in range(128, nz, 128):
            folded = folded + total[:, at : at + 128]
        sums[index, :] = folded

    group = 4
    behind_e, behind_h, behind_last = group, 2 * group + 1, 3 * group + 1

    def some(p, behind, least, most):
        planes = [p - behind + i for i in range(group)]
        return [q for q in planes if not isinstance(q, int) or least <= q <= most]

    def strike(first, second):
        hit = None
        for at in planes_struck:
            for planes in (first, second):
                if planes:
                    here = (at >= planes[0]) & (at <= planes[-1])
                    hit = here if hit is None else hit | here

        @pl.when(hit)
        def _():
            for k, at in enumerate(planes_struck):
                for p in first:
                    amp = jnp.where(at == p, amps_s[0, k], 0.0)
                    e1[2, p] = e1[2, p] + struck[k] * amp
                for p in second:
                    x = p - 2
                    amp = jnp.where(at == p, amps_s[1, k], 0.0)
                    index = pl.ds(aligned(x * ny), ny)
                    s = [snap_ref[t, 2, index, :].astype(jnp.float32) for t in (1, 2)]
                    folded = jnp.zeros((ny, 128), jnp.float32)
                    for z in range(lanes):
                        here = slice(z * 128, z * 128 + 128)
                        gain = struck[k, 0:ny, here] * amp
                        folded = folded + gain * clean[1, :, here] * (s[0] - s[1])[:, here]
                        for t in range(tiles):
                            here = spot(x, t, z)
                            e_s[2, here, :] = e_s[2, here, :] + gain[t * 8 : t * 8 + 8]
                    sums[index, :] = sums[index, :] + folded

    def one(p):
        last = some(p, behind_last, 2, nx + 1)
        first = some(p, behind_e, 1, nx + 2)
        for q in last:
            second_e(q)
        for q in some(p, behind_h, 1, nx + 1):
            second_h(q)
        for q in first:
            first_e(q)
        for q in some(p, 0, 0, nx + 2):
            first_h(q)
        if first + last:
            if not planes_struck:
                place_ports()
            strike(first, last)

    def body(k, carry):
        one(start + k * group)
        return carry

    start = -(-(2 + behind_last) // group) * group
    passes = (nx + 1 - group - start) // group + 1
    for p in range(0, start, group):
        one(p)
    lax.fori_loop(0, passes, body, 0)
    for p in range(start + passes * group, nx + 2 + behind_last, group):
        one(p)
    for b in range(nx * ny // 128):
        here = pl.ds(b * 128, 128)
        line_ref[:, here] = jnp.sum(jnp.transpose(sums[here, :]), axis=0, keepdims=True)


def finish_ends(
    dims, sizes, own_t, low_ref, high_ref, line_ref, mask_ref, spots_ref, gains_ref, *refs
):
    nx, ny, nz = dims
    step = ny + HALO
    parts = sizes[2]
    ends_ref = refs[0]
    grads = refs[1 : 1 + parts]
    strips, turned, rows_ref = refs[1 + parts :]
    gx, gy, gz = lax.axis_index("gx"), lax.axis_index("gy"), lax.axis_index("gz")
    padded = own_t.shape[1]
    row = lax.broadcasted_iota(jnp.int32, (8, padded), 0)
    lane = lax.broadcasted_iota(jnp.int32, (8, padded), 1) - HALO
    has_low, has_high = gz > 0, gz < sizes[2] - 1
    for k, (msg, ok, far, near) in enumerate(((low_ref, has_low, 2, 3), (high_ref, has_high, 5, 4))):
        for f in range(FIELDS):
            strips[k, f] = own_t[8 * f : 8 * f + 8, :]
            strips[k, f, far : far + 1, :] = jnp.where(ok, msg[8 + f : 9 + f, :], 0.0)
            strips[k, f, near : near + 1, :] = jnp.where(ok, msg[f : f + 1, :], 0.0)

    at = lane + 2
    p = steps_in(at, step)
    y = at - p * step - 2
    inside = ((p >= 2) | (gx > 0)) & ((p < nx + 2) | (gx < sizes[0] - 1))
    inside = inside & ((y >= 0) | (gy > 0)) & ((y < ny) | (gy < sizes[1] - 1))
    found = [
        tuple(spots_ref[3 * q + k : 3 * q + k + 1, 0:1] for k in range(3))
        for q in range(spots_ref.shape[0] // 3)
    ]

    def x_up(v):
        return pltpu.roll(v, padded - step, 1)

    def x_down(v):
        return pltpu.roll(v, step, 1)

    def y_up(v):
        return pltpu.roll(v, padded - 1, 1)

    def y_down(v):
        return pltpu.roll(v, 1, 1)

    def z_up(v):
        return pltpu.roll(v, 7, 0)

    def z_down(v):
        return pltpu.roll(v, 1, 0)

    total = None
    results = []
    for k in range(2):
        ex, ey, ez, hx, hy, hz, coef = (strips[k, f] for f in range(FIELDS))
        first = -4 if k == 0 else nz - 4
        good = ((row >= 4) | has_low) if k == 0 else ((row < 4) | has_high)
        half = jnp.where(inside & good, magnetic_step, 0.0)
        for s in range(STEPS):
            cx = (y_up(ez) - ez) - (z_up(ey) - ey)
            cy = (z_up(ex) - ex) - (x_up(ez) - ez)
            cz = (x_up(ey) - ey) - (y_up(ex) - ex)
            hx, hy, hz = hx - half * cx, hy - half * cy, hz - half * cz
            cx = (hz - y_down(hz)) - (hy - z_down(hy))
            cy = (hx - z_down(hx)) - (hz - x_down(hz))
            cz = (hy - x_down(hy)) - (hx - y_down(hx))
            ex, ey, ez = ex + coef * cx, ey + coef * cy, ez + coef * cz
            for q, (sx, sy, sz) in enumerate(found):
                near = (sx >= -2) & (sx < nx + 2) & (sy >= -2) & (sy < ny + 2)
                hit = (row == sz - first) & (at == (sx + 2) * step + sy + 2) & near
                ez = ez + jnp.where(hit, gains_ref[STEPS * q + s : STEPS * q + s + 1, 0:1], 0.0)
            if k == 0:
                mine = (row == 4) | ((row == 5) & (s == 1))
            else:
                mine = (row == 3) | ((row == 2) & (s == 1))
            for c, e in enumerate((ex, ey, ez)):
                tile = FIELDS + c + 3 * (1 - s)
                one = jnp.where(mine, e * own_t[8 * tile : 8 * tile + 8, :], 0.0)
                total = one if total is None else total + one
        results.append((ex, ey, ez, hx, hy, hz))
    for c in range(6):
        rows_ref[8 * c : 8 * c + 8, :] = jnp.where(row < 4, results[1][c], results[0][c])
    line = jnp.sum(total, axis=0, keepdims=True)
    column = columns_of([(line_ref[...], ny, 0), (line, step, 2 * step + HALO)], nx, ny)
    turned[...] = column * mask_ref[...].astype(jnp.float32)
    width = ny // parts
    for shift in range(parts):
        owner = partner_of(gz, shift, parts)
        grads[shift][...] = turned[pl.ds(owner * width, width), :]
    ends_ref[...] = rows_ref[...]


def write_out(dims, e_s, h_s, ends_ref, e_out, h_out, spare, e_v, h_v, ends_t, sems):
    nx, ny, nz = dims
    lanes = nz // 128
    tiles = ny // 8
    plane = ny * lanes
    step = ny + HALO
    lane = lax.broadcasted_iota(jnp.int32, (8, 128), 1)
    spare[...] = jnp.zeros(spare.shape, jnp.float32)
    spare[0 : ends_ref.shape[0], :] = ends_ref[...]
    for b in range(spare.shape[1] // 128):
        ends_t[b * 128 : (b + 1) * 128, :] = jnp.transpose(spare[:, b * 128 : (b + 1) * 128])

    def one(x, carry):
        for t in range(tiles):
            v = ends_t[pl.ds(pl.multiple_of((x + 2) * step + HALO + t * 8, 8), 8), :]
            for c in range(6):
                src, dst = (e_s, e_v) if c < 3 else (h_s, h_v)
                placed = pltpu.roll(v, 124 - 8 * c, 1)
                for z in range(lanes):
                    here = pl.ds(pl.multiple_of(((x * tiles + t) * lanes + z) * 8, 8), 8)
                    out = src[c % 3, here, :]
                    if z == 0:
                        out = jnp.where(lane < 2, placed, out)
                    if z == lanes - 1:
                        out = jnp.where(lane >= 126, placed, out)
                    dst[c % 3, here, :] = out
        return carry

    chunk = nx // 4
    copies = []
    for c in range(4):
        lax.fori_loop(c * chunk, (c + 1) * chunk, one, 0, unroll=True)
        here = pl.ds(c * chunk * plane, chunk * plane)
        for k, (src, dst) in enumerate(((e_v, e_out), (h_v, h_out))):
            copy = pltpu.make_async_copy(src.at[:, here], dst.at[:, here], sems.at[2 * c + k])
            copy.start()
            copies.append(copy)
    for copy in copies:
        copy.wait()


def params(limit=12):
    return pltpu.CompilerParams(vmem_limit_bytes=limit * 1024 * 1024)


def body(sizes, e_adjoint, h_adjoint, snapshots, material, permittivity, design_mask, ports, amplitudes):
    permittivity = in_hbm(permittivity)
    permittivity = in_hbm(permittivity)
    dims = material.shape
    nx, ny, nz = dims
    lanes = nz // 128
    tiles = ny // 8
    plane = ny * lanes
    cells = nx * ny
    step = ny + HALO
    padded = -(-((nx + 4) * step + HALO) // 128) * 128
    f32, i32 = jnp.float32, jnp.int32
    xs, ys = swaps(sizes[0]), swaps(sizes[1])
    block, cube = jax.ShapeDtypeStruct, pltpu.VMEM

    shapes = [block((9 * plane + ny, 128), f32) for _ in xs]
    shapes += [block((9 * lanes * nx + 8, 128), f32) for _ in ys]
    shapes += [block((lanes, 4 * FIELDS, 128), f32) for _ in xs for _ in ys]
    buffers = []
    for _ in xs:
        tile = (2, tiles, lanes, 8, 128)
        buffers += [cube((3, *tile), f32), cube((3, *tile), f32), cube(tile, i32)]
    for _ in ys:
        tile = (nx * lanes * 8, 128)
        buffers += [cube((3, *tile), f32), cube((3, *tile), f32), cube(tile, i32)]
    n_copies = 3 * (len(xs) + len(ys)) + 1
    shapes += [block((permittivity.shape[0], 128), f32)]
    *msgs, table = pl.pallas_call(
        functools.partial(send_faces, dims, sizes),
        out_shape=shapes,
        in_specs=[HBM, HBM, HBM, HBM],
        out_specs=[VM] * len(shapes),
        scratch_shapes=buffers
        + [pltpu.SMEM(permittivity.shape, f32), pltpu.SemaphoreType.DMA((n_copies,))],
        compiler_params=params(),
        name="send_faces",
    )(
        in_hbm(tiles_of(e_adjoint)),
        in_hbm(tiles_of(h_adjoint)),
        in_hbm(tiles_of(material)),
        permittivity,
    )
    e_v, h_v, m_v = in_vmem(tiled(e_adjoint)), in_vmem(tiled(h_adjoint)), in_vmem(tiled(material))
    snaps = in_hbm(snapshots.reshape(STEPS + 1, 3, cells, nz))
    coef_v, own_packed, s = pl.pallas_call(
        functools.partial(own_ends, dims),
        out_shape=[cube(m_v.shape, f32), cube((padded, 128), f32), cube(snaps.shape, snaps.dtype)],
        in_specs=[VM, VM, VM, HBM, VM],
        out_specs=[VM] * 3,
        scratch_shapes=[pltpu.SemaphoreType.DMA((3 * (STEPS + 1),))],
        compiler_params=params(),
        cost_estimate=pl.CostEstimate(flops=10**7, bytes_accessed=4 * 10**6, transcendentals=0),
        name="own_ends",
    )(e_v, h_v, m_v, snaps, table)

    both = ("gx", "gy")

    def meet(x, y, tx, ty):
        if tx[x] == x or ty[y] == y:
            return x * sizes[1] + y
        return tx[x] * sizes[1] + ty[y]

    tables = [("gx", list(enumerate(swap_table(sizes[0], o)))) for o in xs]
    tables += [("gy", list(enumerate(swap_table(sizes[1], o)))) for o in ys]
    for ox in xs:
        for oy in ys:
            tx, ty = swap_table(sizes[0], ox), swap_table(sizes[1], oy)
            pairs = [
                (x * sizes[1] + y, meet(x, y, tx, ty))
                for x in range(sizes[0])
                for y in range(sizes[1])
            ]
            tables.append((both, pairs))
    got = [lax.ppermute(msg, axis, pairs) for msg, (axis, pairs) in zip(msgs, tables)]

    xh, yh, own_t, up, down = pl.pallas_call(
        functools.partial(unpack_faces, dims, sizes),
        out_shape=[
            cube((FIELDS, lanes, 4 * ny, 128), f32),
            cube((FIELDS, lanes, (nx + 4) * HALO, 128), f32),
            cube((128, padded), f32),
            block((16, padded), f32),
            block((16, padded), f32),
        ],
        in_specs=[VM] * (1 + len(got)),
        out_specs=[VM] * 5,
        scratch_shapes=[
            pltpu.VMEM((padded, 128), f32),
            pltpu.VMEM((4 * ny, 128), f32),
            pltpu.VMEM(((nx + 4) * HALO, 128), f32),
        ],
        compiler_params=params(),
        name="unpack_faces",
    )(own_packed, *got)

    parts = sizes[2]
    low = lax.ppermute(up, "gz", [(i, (i + 1) % parts) for i in range(parts)])
    high = lax.ppermute(down, "gz", [(i, (i - 1) % parts) for i in range(parts)])

    ported = ports.shape[0]
    e_s, h_s, line, spots, gains = pl.pallas_call(
        functools.partial(march, dims, sizes),
        out_shape=[cube(e_v.shape, f32), cube(h_v.shape, f32), block((1, cells), f32)]
        + [block((3 * ported, 128), i32), block((STEPS * ported, 128), f32)],
        in_specs=[VM] * 6 + [HBM, HBM],
        out_specs=[VM] * 5,
        scratch_shapes=[
            pltpu.VMEM((3, nx + 4, step, nz), f32),
            pltpu.VMEM((3, nx + 4, step, nz), f32),
            pltpu.VMEM((3, nx + 4, step, nz), f32),
            pltpu.VMEM((step, nz), f32),
            pltpu.VMEM((ported, step, nz), f32),
            pltpu.VMEM((2, ny, nz), f32),
            pltpu.VMEM((cells, 128), f32),
            pltpu.SMEM(ports.shape, i32),
            pltpu.SMEM(amplitudes.shape, f32),
            pltpu.SemaphoreType.DMA((2,)),
        ],
        compiler_params=params(24),
        cost_estimate=pl.CostEstimate(flops=4 * 10**7, bytes_accessed=10**7, transcendentals=0),
        name="march",
    )(e_v, h_v, coef_v, xh, yh, s, in_hbm(ports), in_hbm(amplitudes))
    ends, *chunks = pl.pallas_call(
        functools.partial(finish_ends, dims, sizes),
        out_shape=[cube((48, padded), f32)] + [block((ny // parts, nx), f32)] * parts,
        in_specs=[VM] * 7,
        out_specs=[VM] * (1 + parts),
        scratch_shapes=[
            pltpu.VMEM((2, FIELDS, 8, padded), f32),
            pltpu.VMEM((ny, nx), f32),
            pltpu.VMEM((48, padded), f32),
        ],
        compiler_params=params(),
        name="finish_ends",
    )(own_t, low, high, line, design_mask.T, spots, gains)
    e_out, h_out = pl.pallas_call(
        functools.partial(write_out, dims),
        out_shape=[block(e_v.shape, f32), block(h_v.shape, f32)],
        in_specs=[VM] * 3,
        out_specs=[HBM] * 2,
        scratch_shapes=[
            pltpu.VMEM((128, padded), f32),
            pltpu.VMEM(e_v.shape, f32),
            pltpu.VMEM(h_v.shape, f32),
            pltpu.VMEM((padded, 128), f32),
            pltpu.SemaphoreType.DMA((8,)),
        ],
        compiler_params=params(),
        cost_estimate=pl.CostEstimate(flops=10**7, bytes_accessed=8 * 10**6, transcendentals=0),
        name="write_out",
    )(e_s, h_s, ends)
    gradient = chunks[0]
    for shift in range(1, parts):
        gradient = gradient + lax.ppermute(
            chunks[shift], "gz", [(i, partner_of(i, shift, parts)) for i in range(parts)]
        )
    return untiled(e_out, dims), untiled(h_out, dims), gradient.T


def solution(mesh):
    placed = (
        P(None, "gx", "gy", "gz"),
        P(None, "gx", "gy", "gz"),
        P(None, None, "gx", "gy", "gz"),
        P("gx", "gy", "gz"),
        P(),
        P("gx", "gy"),
        P(),
        P(),
    )
    sizes = tuple(mesh.shape[axis] for axis in ("gx", "gy", "gz"))
    return jax.shard_map(
        functools.partial(body, sizes),
        mesh=mesh,
        in_specs=placed,
        out_specs=(P(None, "gx", "gy", "gz"), P(None, "gx", "gy", "gz"), P("gx", ("gy", "gz"))),
        check_vma=False,
    )
```

```python
import functools

import jax
import jax.numpy as jnp
from jax import lax
from jax.experimental import pallas as pl
from jax.experimental.pallas import tpu as pltpu
from jax.sharding import PartitionSpec as P

STEPS = 2
FIELDS = 7
HALO = 8

magnetic_step = 0.5
electric_step = 0.5

VM = pl.BlockSpec(memory_space=pltpu.VMEM)


HBM = pl.BlockSpec(memory_space=pltpu.HBM)


def in_hbm(array):
    return pltpu.with_memory_space_constraint(array, pltpu.HBM)


def in_vmem(array):
    return pltpu.with_memory_space_constraint(array, pltpu.VMEM)


def swap_table(size, odd):
    table = list(range(size))
    for i in range(odd, size - 1, 2):
        table[i], table[i + 1] = i + 1, i
    return table


def swaps(size):
    return [odd for odd in (0, 1) if odd + 1 < size]


def partner_of(index, shift, size):
    if size & (size - 1) == 0:
        return index ^ shift
    return (index + shift) % size


def sends_up(index, odd):
    return lax.rem(index, 2) == odd


def has_partner(index, size, odd):
    up = sends_up(index, odd)
    return (up & (index + 1 < size)) | (jnp.logical_not(up) & (index >= 1))


def coef_table(perm_ref):
    return [
        electric_step / jnp.full((1, 1), perm_ref[i], jnp.float32) for i in range(perm_ref.shape[0])
    ]


def coef_of(material, table):
    out = jnp.zeros(material.shape, jnp.float32)
    for i, value in enumerate(table):
        out = jnp.where(material == i, value, out)
    return out


def tiled(array):
    *lead, nx, ny, nz = array.shape
    n = len(lead)
    split = array.reshape(*lead, nx, ny // 8, 8, nz // 128, 128)
    order = tuple(range(n + 2)) + (n + 3, n + 2, n + 4)
    return split.transpose(order).reshape(*lead, nx * ny * nz // 128, 128)


def untiled(array, dims):
    nx, ny, nz = dims
    lead = array.shape[:-2]
    n = len(lead)
    split = array.reshape(*lead, nx, ny // 8, nz // 128, 8, 128)
    order = tuple(range(n + 2)) + (n + 3, n + 2, n + 4)
    return split.transpose(order).reshape(*lead, nx, ny, nz)


def tiles_of(array):
    *lead, nx, ny, nz = array.shape
    return tiled(array).reshape(*lead, nx, ny // 8, nz // 128, 8, 128)


def send_faces(dims, sizes, e_ref, h_ref, m_ref, perm_ref, *refs):
    nx, ny, nz = dims
    lanes = nz // 128
    tiles = ny // 8
    plane = ny * lanes
    gx, gy = lax.axis_index("gx"), lax.axis_index("gy")
    xs, ys = swaps(sizes[0]), swaps(sizes[1])
    n_out = len(xs) + len(ys) + len(xs) * len(ys)
    outs, table_ref, refs = refs[:n_out], refs[n_out], refs[n_out + 1 :]
    x_bufs, refs = refs[: 3 * len(xs)], refs[3 * len(xs) :]
    y_bufs, (perm_s, sems) = refs[: 3 * len(ys)], refs[3 * len(ys) :]
    copies = []

    def start(src, dst):
        copy = pltpu.make_async_copy(src, dst, sems.at[len(copies)])
        copy.start()
        copies.append(copy)

    for i, odd in enumerate(ys):
        up = sends_up(gy, odd)
        t, r = jnp.where(up, tiles - 1, 0), jnp.where(up, 6, 0)
        for k, ref in enumerate((e_ref, h_ref, m_ref)):
            src = ref.at[:, t, :, pl.ds(r, 2), :] if k == 2 else ref.at[:, :, t, :, pl.ds(r, 2), :]
            dst = y_bufs[3 * i + k]
            dst = dst.reshape(*dst.shape[:-2], nx + 1, lanes, 8, 128)
            here = (pl.ds(0, nx), slice(None), pl.ds(0, 2), slice(None))
            start(src, dst.at[here] if k == 2 else dst.at[(slice(None), *here)])
    for i, odd in enumerate(xs):
        first = pl.ds(jnp.where(sends_up(gx, odd), nx - 2, 0), 2)
        for k, ref in enumerate((e_ref, h_ref, m_ref)):
            start(ref.at[first] if k == 2 else ref.at[:, first], x_bufs[3 * i + k])
    start(perm_ref, perm_s)
    copies.pop().wait()
    table = coef_table(perm_s)
    for k, value in enumerate(table):
        table_ref[k : k + 1, :] = jnp.broadcast_to(value, (1, 128))
    lane = lax.broadcasted_iota(jnp.int32, (8, 128), 1)
    lane_n = lax.broadcasted_iota(jnp.int32, (nx, 128), 1)

    def z_up(v, lane):
        out = []
        for z in range(lanes):
            after = pltpu.roll(v[z + 1], 127, 1) if z + 1 < lanes else jnp.zeros_like(v[z])
            out.append(jnp.where(lane < 127, pltpu.roll(v[z], 127, 1), after))
        return out

    def row_up(v):
        rows = v.shape[0]
        row = lax.broadcasted_iota(jnp.int32, v.shape, 0)
        return jnp.where(row < rows - 1, pltpu.roll(v, rows - 1, 0), 0.0)

    step = lanes * 8
    for i, odd in enumerate(ys):
        for copy in copies[3 * i : 3 * i + 3]:
            copy.wait()
        up = sends_up(gy, odd)
        near, far = jnp.where(up, 1, 0), jnp.where(up, 0, 1)
        down = jnp.where(up, 0.0, magnetic_step)
        e_b, h_b, m_b = y_bufs[3 * i : 3 * i + 3]
        out = outs[len(xs) + i]

        def at(ref, c, which):
            return [ref[c, pl.ds(z * 8 + which, nx, stride=step), :] for z in range(lanes)]

        def put(k, z, v):
            out[pl.ds((k * lanes + z) * nx, nx), :] = v

        e_n = [at(e_b, c, near) for c in range(3)]
        h_n = [at(h_b, c, near) for c in range(3)]
        ex_f, ey_f, ez_f = (at(e_b, c, far) for c in range(3))
        hx_f, hz_f = at(h_b, 0, far), at(h_b, 2, far)
        ey_z = z_up(ey_f, lane_n)
        for z in range(lanes):
            for c in range(3):
                put(c, z, e_n[c][z])
            put(3, z, h_n[0][z] - down * ez_f[z])
            put(4, z, h_n[1][z])
            put(5, z, h_n[2][z] + down * ex_f[z])
            put(6, z, coef_of(m_b[pl.ds(z * 8 + near, nx, stride=step), :], table))
            put(7, z, hx_f[z] + magnetic_step * (ez_f[z] + (ey_z[z] - ey_f[z])))
            put(8, z, hz_f[z] - magnetic_step * ((row_up(ey_f[z]) - ey_f[z]) + ex_f[z]))
        first = jnp.concatenate([ey_f[0], jnp.zeros((128 - nx, 128), jnp.float32)], axis=0)
        out[pl.ds(9 * lanes * nx, 8), :] = jnp.transpose(first)[0:8]
    for i, odd in enumerate(xs):
        for copy in copies[3 * (len(ys) + i) : 3 * (len(ys) + i) + 3]:
            copy.wait()
        up = sends_up(gx, odd)
        near, far = jnp.where(up, 1, 0), jnp.where(up, 0, 1)
        down = jnp.where(up, 0.0, magnetic_step)
        e_b, h_b, m_b = x_bufs[3 * i : 3 * i + 3]
        out = outs[i]

        def put(k, t, z, v):
            out[pl.ds(k * plane + (t * lanes + z) * 8, 8), :] = v

        ex_y = [
            row_up(jnp.concatenate([e_b[0, far, t, z] for t in range(tiles)], axis=0))
            for z in range(lanes)
        ]
        for t in range(tiles):
            ex_z = z_up([e_b[0, far, t, z] for z in range(lanes)], lane)
            for z in range(lanes):
                ex_f, ey_f, ez_f = (e_b[c, far, t, z] for c in range(3))
                for c in range(3):
                    put(c, t, z, e_b[c, near, t, z])
                put(3, t, z, h_b[0, near, t, z])
                put(4, t, z, h_b[1, near, t, z] + down * ez_f)
                put(5, t, z, h_b[2, near, t, z] - down * ey_f)
                put(6, t, z, coef_of(m_b[near, t, z], table))
                put(7, t, z, h_b[1, far, t, z] - magnetic_step * ((ex_z[z] - ex_f) + ez_f))
                ex_up = ex_y[z][t * 8 : t * 8 + 8]
                put(8, t, z, h_b[2, far, t, z] + magnetic_step * (ey_f + (ex_up - ex_f)))
            out[pl.ds(9 * plane + t * 8, 8), :] = e_b[0, far, t, 0]
        for j, odd_y in enumerate(ys):
            up = sends_up(gy, odd_y)
            t = jnp.where(up, tiles - 1, 0)
            rows = (jnp.where(up, 7, 0), jnp.where(up, 6, 1))
            out = outs[len(xs) + len(ys) + i * len(ys) + j]
            for z in range(lanes):
                for f in range(FIELDS):
                    for k in range(4):
                        where = (near, far)[k // 2], t, z, pl.ds(rows[k % 2], 1)
                        if f < 6:
                            line = (e_b, h_b)[f // 3][(f % 3, *where)]
                        else:
                            line = coef_of(m_b[where], table)
                        out[z, pl.ds(4 * f + k, 1), :] = line


def turn_ends(parts, lane, first_field, after_field):
    out = None
    for k in range(first_field, after_field):
        first, last = parts(k)
        turned = pltpu.roll(jnp.where(lane < 64, first, last), 8 * k + 4, 1)
        out = turned if out is None else jnp.where(lane >= 8 * k, turned, out)
    return out


def own_ends(dims, e_v, h_v, m_v, snap_hbm, table_ref, coef_v, packed, snap_ref, sems):
    nx, ny, nz = dims
    lanes = nz // 128
    step = ny + HALO
    copies = []
    for t in range(STEPS + 1):
        for c in range(3):
            copy = pltpu.make_async_copy(snap_hbm.at[t, c], snap_ref.at[t, c], sems.at[3 * t + c])
            copy.start()
            copies.append(copy)
    table = [table_ref[k : k + 1, :] for k in range(table_ref.shape[0])]
    lane = lax.broadcasted_iota(jnp.int32, (8, 128), 1)
    tiles = ny // 8

    def fields(x, carry):
        for t in range(tiles):
            here = [
                pl.ds(pl.multiple_of(((x * tiles + t) * lanes + z) * 8, 8), 8) for z in range(lanes)
            ]
            for z in range(lanes):
                coef_v[here[z], :] = coef_of(m_v[here[z], :], table)

            def parts(k):
                if k < 3:
                    return e_v[k, here[0], :], e_v[k, here[-1], :]
                if k < 6:
                    return h_v[k - 3, here[0], :], h_v[k - 3, here[-1], :]
                return coef_v[here[0], :], coef_v[here[-1], :]

            row = pl.multiple_of((x + 2) * step + HALO + t * 8, 8)
            packed[pl.ds(row, 8), :] = turn_ends(parts, lane, 0, FIELDS)
        return carry

    lax.fori_loop(0, nx, fields, 0, unroll=16)

    for copy in copies:
        copy.wait()

    def changes(x, carry):
        index = pl.ds(pl.multiple_of(x * ny, ny), ny)
        change = []
        for c in range(3):
            s = [
                [
                    snap_ref[t, c, index, z * 128 : z * 128 + 128].astype(jnp.float32)
                    for z in (0, lanes - 1)
                ]
                for t in range(STEPS + 1)
            ]
            change.append([[s[t][z] - s[t + 1][z] for z in range(2)] for t in range(STEPS)])
        for t in range(tiles):

            def parts(k):
                pair = change[(k - FIELDS) % 3][1 - (k - FIELDS) // 3]
                return tuple(v[t * 8 : t * 8 + 8] for v in pair)

            here = pl.ds(pl.multiple_of((x + 2) * step + HALO + t * 8, 8), 8)
            after = turn_ends(parts, lane, FIELDS, FIELDS + 6)
            packed[here, :] = jnp.where(lane < 8 * FIELDS, packed[here, :], after)
        return carry

    lax.fori_loop(0, nx, changes, 0, unroll=16)


def unpack_faces(dims, sizes, own_packed, *refs):
    nx, ny, nz = dims
    lanes = nz // 128
    tiles = ny // 8
    plane = ny * lanes
    step = ny + HALO
    gx, gy = lax.axis_index("gx"), lax.axis_index("gy")
    xs, ys = swaps(sizes[0]), swaps(sizes[1])
    n_msgs = len(xs) + len(ys) + len(xs) * len(ys)
    msgs = refs[:n_msgs]
    xh, yh, own_t, up_ref, down_ref, packed, x_raw, y_raw = refs[n_msgs:]
    xh[...] = jnp.zeros(xh.shape, jnp.float32)
    x_raw[...] = jnp.zeros(x_raw.shape, jnp.float32)
    y_raw[...] = jnp.zeros(y_raw.shape, jnp.float32)
    for f in range(FIELDS):
        for z in range(lanes):
            if len(ys) < 2 or f < 3:
                yh[f, z] = jnp.zeros(yh.shape[2:], jnp.float32)
            else:
                for p in (0, 1, nx + 2, nx + 3):
                    yh[f, z, pl.ds(p * HALO, HALO), :] = jnp.zeros((HALO, 128), jnp.float32)

    def planes(odd):
        high = sends_up(gx, odd)
        return jnp.where(high, 2, 1), jnp.where(high, 3, 0)

    def lines(odd):
        high = sends_up(gy, odd)
        return jnp.where(high, 0, HALO - 1), jnp.where(high, 1, HALO - 2)

    for i, odd in enumerate(xs):
        ok = has_partner(gx, sizes[0], odd)
        near, far = planes(odd)
        msg = msgs[i]
        for t in range(tiles):
            for z in range(lanes):
                for k, f in enumerate((0, 1, 2, 3, 4, 5, 6, 4, 5)):
                    q = near if k < FIELDS else far
                    xh[f, z, pl.ds(pl.multiple_of(q * ny + t * 8, 8), 8), :] = jnp.where(
                        ok, msg[pl.ds(k * plane + (t * lanes + z) * 8, 8), :], 0.0
                    )
            x_raw[pl.ds(pl.multiple_of(far * ny + t * 8, 8), 8), :] = jnp.where(
                ok & (far == 0), msg[pl.ds(9 * plane + t * 8, 8), :], 0.0
            )
    for i, odd in enumerate(ys):
        ok = has_partner(gy, sizes[1], odd)
        near, far = lines(odd)
        msg = msgs[len(xs) + i]
        for z in range(lanes):
            for k, f in enumerate((0, 1, 2, 3, 4, 5, 6, 3, 5)):
                r = near if k < FIELDS else far
                yh[f, z, pl.ds(2 * HALO + r, nx, stride=HALO), :] = jnp.where(
                    ok, msg[pl.ds((k * lanes + z) * nx, nx), :], 0.0
                )
        raw = jnp.where(ok & (far == HALO - 2), msg[pl.ds(9 * lanes * nx, 8), :], 0.0)
        raw = jnp.concatenate([raw, jnp.zeros((120, 128), jnp.float32)], axis=0)
        y_raw[pl.ds(2 * HALO + far, nx, stride=HALO), :] = jnp.transpose(raw)[0:nx]
    for i, ox in enumerate(xs):
        for j, oy in enumerate(ys):
            ok = has_partner(gx, sizes[0], ox) & has_partner(gy, sizes[1], oy)
            px, py = planes(ox), lines(oy)
            px = [jnp.where(q < 2, q, q + nx) for q in px]
            msg = msgs[len(xs) + len(ys) + i * len(ys) + j]
            for z in range(lanes):
                for f in range(FIELDS):
                    for k in range(4):
                        yh[f, z, pl.ds(px[k // 2] * HALO + py[k % 2], 1), :] = jnp.where(
                            ok, msg[z, pl.ds(4 * f + k, 1), :], 0.0
                        )

    lane = lax.broadcasted_iota(jnp.int32, (8, 128), 1)
    upper = lax.broadcasted_iota(jnp.int32, (8, 128), 0) < HALO // 2

    def halo_rows(p, before, here):
        def tile(f, z):
            if f == FIELDS:
                return y_raw[here, :]
            return jnp.where(upper, yh[f, z, before, :], yh[f, z, here, :])

        packed[pl.ds(p * step if isinstance(p, int) else pl.multiple_of(p * step, 8), HALO), :] = (
            turn_ends(lambda f: (tile(f, 0), tile(f, lanes - 1)), lane, 0, FIELDS + 1)
        )

    def one(p, carry):
        halo_rows(
            p,
            pl.ds(pl.multiple_of((p - 1) * HALO, 8), HALO),
            pl.ds(pl.multiple_of(p * HALO, 8), HALO),
        )
        return carry

    halo_rows(0, pl.ds(0, HALO), pl.ds(0, HALO))
    lax.fori_loop(1, nx + 4, one, 0, unroll=True)
    last = pl.ds((nx + 3) * HALO, HALO)
    halo_rows(nx + 4, last, last)
    for q, p in enumerate((0, 1, nx + 2, nx + 3)):
        for t in range(tiles):
            index = pl.ds(q * ny + t * 8, 8)

            def parts(f):
                if f == FIELDS:
                    return x_raw[index, :], x_raw[index, :]
                return xh[f, 0, index, :], xh[f, lanes - 1, index, :]

            packed[pl.ds(p * step + HALO + t * 8, 8), :] = turn_ends(parts, lane, 0, FIELDS + 1)
    for x in range(nx):
        index = pl.ds((x + 2) * step + HALO, ny)
        packed[index, :] = own_packed[index, :]
    after = (nx + 4) * step + HALO
    padded = packed.shape[0]
    if padded > after:
        packed[after:, :] = jnp.zeros((padded - after, 128), jnp.float32)
    for b in range(padded // 128):
        here = pl.ds(b * 128, 128)
        block = jnp.transpose(packed[here, :])
        own_t[:, here] = block
        for f in range(FIELDS):
            up_ref[f : f + 1, here] = block[8 * f + 3 : 8 * f + 4, :]
            up_ref[8 + f : 9 + f, here] = block[8 * f + 2 : 8 * f + 3, :]
            down = [block[8 * f + 4 + k : 8 * f + 5 + k, :] for k in range(2)]
            if f < 2:
                at = lax.broadcasted_iota(jnp.int32, (1, 128), 1) + b * 128
                raw = (at >= HALO) & (at < step) if f == 0 else lax.rem(at, step) < HALO
                tail = [block[8 * FIELDS + 4 + k : 8 * FIELDS + 5 + k, :] for k in range(2)]
                down = [down[k] + jnp.where(raw, tail[k], 0.0) for k in range(2)]
            down_ref[f : f + 1, here] = down[0]
            down_ref[8 + f : 9 + f, here] = down[1]
    for row in (7, 15):
        up_ref[row : row + 1, :] = jnp.zeros((1, padded), jnp.float32)
        down_ref[row : row + 1, :] = jnp.zeros((1, padded), jnp.float32)


def split_index(index, size):
    if size & (size - 1) == 0:
        return lax.shift_right_logical(index, size.bit_length() - 1), index & (size - 1)
    return lax.div(index, size), lax.rem(index, size)


def steps_in(index, step):
    return ((index.astype(jnp.float32) + 0.5) * (1.0 / step)).astype(jnp.int32)


def columns_of(lines, nx, ny):
    spread, pick = [], []
    for line, step, first in lines:
        size = line.shape[1]
        at = lax.broadcasted_iota(jnp.int32, (ny, size), 1) - first
        y = lax.broadcasted_iota(jnp.int32, (ny, size), 0)
        ok = (at >= 0) & (at < nx * step) & (at - steps_in(at, step) * step == y)
        spread.append(jnp.where(ok, line, 0.0))
        at = lax.broadcasted_iota(jnp.int32, (nx, size), 1) - first
        x = lax.broadcasted_iota(jnp.int32, (nx, size), 0) * step
        pick.append(jnp.where((at >= x) & (at < x + step), 1.0, 0.0))
    left = jnp.concatenate(spread, axis=1)
    thirds = []
    for _ in range(3):
        part = left.astype(jnp.bfloat16)
        left = left - part.astype(jnp.float32)
        thirds.append(part)
    out = lax.dot_general(
        jnp.concatenate(thirds, axis=0),
        jnp.concatenate(pick, axis=1).astype(jnp.bfloat16),
        (((1,), (1,)), ((), ())),
        preferred_element_type=jnp.float32,
    )
    return out[0:ny] + (out[ny : 2 * ny] + out[2 * ny : 3 * ny])


def find_ports(dims, sizes, ports_ref):
    nx, ny, nz = dims
    gx, gy, gz = lax.axis_index("gx"), lax.axis_index("gy"), lax.axis_index("gz")
    found = []
    for q in range(ports_ref.shape[0]):
        line, z = split_index(ports_ref[q], nz * sizes[2])
        x, y = split_index(line, ny * sizes[1])
        found.append((x - gx * nx, y - gy * ny, z - gz * nz))
    return found


def march(dims, sizes, e_v, h_v, coef_v, xh, yh, snap_ref, ports_ref, amps_ref, *refs):
    nx, ny, nz = dims
    lanes = nz // 128
    tiles = ny // 8
    step = ny + HALO
    e_s, h_s, line_ref, spots_ref, gains_ref, e1, h1, h2, half_ref, struck, clean, sums = refs[:12]
    ports_s, amps_s, sems = refs[12:]
    copies = [
        pltpu.make_async_copy(ports_ref, ports_s, sems.at[0]),
        pltpu.make_async_copy(amps_ref, amps_s, sems.at[1]),
    ]
    for copy in copies:
        copy.start()
    gx, gy = lax.axis_index("gx"), lax.axis_index("gy")
    row = lax.broadcasted_iota(jnp.int32, (step, nz), 0)
    lane = lax.broadcasted_iota(jnp.int32, (step, nz), 1)
    inside = (row < ny) | ((row < ny + 2) & (gy < sizes[1] - 1)) | ((row >= ny + 4) & (gy > 0))
    half_ref[...] = jnp.where(inside, magnetic_step, 0.0)
    for k in range(2):
        clean[k] = jnp.where((lane[:ny] > k) & (lane[:ny] < nz - 1 - k), 1.0, 0.0)

    planes_struck = []

    def place_ports():
        for copy in copies:
            copy.wait()
        for q, (x, y, z) in enumerate(find_ports(dims, sizes, ports_s)):
            near = (y >= -2) & (y < ny + 2) & (z >= 0) & (z < nz)
            at = jnp.where(y < 0, y + step, y)
            struck[q] = jnp.where((row == at) & (lane == z) & near, 1.0, 0.0)
            planes_struck.append(x + 2)
            for k, v in enumerate((x, y, z)):
                spots_ref[3 * q + k : 3 * q + k + 1, :] = jnp.full((1, 128), v, jnp.int32)
            for k in range(STEPS):
                gains_ref[STEPS * q + k : STEPS * q + k + 1, :] = jnp.full(
                    (1, 128), amps_s[k, q], jnp.float32
                )

    def spot(x, t, z):
        index = ((x * tiles + t) * lanes + z) * 8
        return pl.ds(index if isinstance(index, int) else pl.multiple_of(index, 8), 8)

    def own_tile(f, p, t, z):
        if isinstance(p, int) and not 2 <= p < nx + 2:
            return xh[f, z, pl.ds((p if p < 2 else p - nx) * ny + t * 8, 8), :]
        if f < 3:
            return e_v[f, spot(p - 2, t, z), :]
        if f < 6:
            return h_v[f - 3, spot(p - 2, t, z), :]
        return coef_v[spot(p - 2, t, z), :]

    def aligned(index):
        return index if isinstance(index, int) else pl.multiple_of(index, 8)

    def load(f, p):
        columns = []
        for z in range(lanes):
            column = [own_tile(f, p, t, z) for t in range(tiles)]
            column.append(yh[f, z, pl.ds(aligned(p * HALO), HALO), :])
            columns.append(jnp.concatenate(column, axis=0))
        return jnp.concatenate(columns, axis=1)

    def load_own(f, p):
        return jnp.concatenate(
            [
                jnp.concatenate([own_tile(f, p, t, z) for t in range(tiles)], axis=0)
                for z in range(lanes)
            ],
            axis=1,
        )

    def put(ref, f, x, v):
        for t in range(tiles):
            for z in range(lanes):
                ref[f, spot(x, t, z), :] = v[t * 8 : t * 8 + 8, z * 128 : z * 128 + 128]

    def y_up(v):
        return pltpu.roll(v, step - 1, 0)

    def y_down(v):
        return pltpu.roll(v, 1, 0)

    def z_up(v):
        return pltpu.roll(v, nz - 1, 1)

    def z_down(v):
        return pltpu.roll(v, 1, 1)

    def new_h(half, ex, ey, ez, ey_x, ez_x, hx, hy, hz):
        cx = (y_up(ez) - ez) - (z_up(ey) - ey)
        cy = (z_up(ex) - ex) - (ez_x - ez)
        cz = (ey_x - ey) - (y_up(ex) - ex)
        return hx - half * cx, hy - half * cy, hz - half * cz

    def curl_h(hx, hy, hz, hy_x, hz_x):
        cx = (hz - y_down(hz)) - (hy - z_down(hy))
        cy = (hx - z_down(hx)) - (hz - hz_x)
        cz = (hy - hy_x) - (hx - y_down(hx))
        return cx, cy, cz

    def half_of(p):
        if isinstance(p, int) and p < 2:
            return half_ref[...] * jnp.where(gx == 0, 0.0, 1.0)
        if isinstance(p, int) and p >= nx + 2:
            return half_ref[...] * jnp.where(gx == sizes[0] - 1, 0.0, 1.0)
        return half_ref[...]

    def first_h(p):
        e = [load(f, p) for f in range(3)]
        h = [load(3 + f, p) for f in range(3)]
        out = new_h(half_of(p), *e, load(1, p + 1), load(2, p + 1), *h)
        for f in range(3):
            h1[f, p] = out[f]

    def first_e(p):
        e = [load(f, p) for f in range(3)]
        curl = curl_h(*[h1[f, p] for f in range(3)], h1[1, p - 1], h1[2, p - 1])
        coef = load(6, p)
        out = [e[f] + coef * curl[f] for f in range(3)]
        for f in range(3):
            e1[f, p] = out[f]

    def second_h(p):
        e = [e1[f, p] for f in range(3)]
        h = [h1[f, p] for f in range(3)]
        out = new_h(half_of(p), *e, e1[1, p + 1], e1[2, p + 1], *h)
        h2[0, p] = out[0]
        h2[1, p, 0:ny] = out[1][:ny]
        h2[2, p] = out[2]

    def second_e(p):
        h = [h2[f, p] for f in range(3)]
        curl = curl_h(*h, h2[1, p - 1], h2[2, p - 1])
        coef = load_own(6, p)
        old = [e1[f, p, 0:ny, 0:nz] for f in range(3)]
        new = [old[f] + coef * curl[f][:ny, :nz] for f in range(3)]
        x = p - 2
        index = pl.ds(aligned(x * ny), ny)
        total = None
        for f in range(3):
            put(e_s, f, x, new[f])
            put(h_s, f, x, h[f][:ny, :nz])
            s = [snap_ref[t, f, index, :].astype(jnp.float32) for t in range(STEPS + 1)]
            one = [old[f] * (s[0] - s[1]), new[f] * (s[1] - s[2])]
            total = one if total is None else [total[k] + one[k] for k in range(2)]
        total = total[0] * clean[0] + total[1] * clean[1]
        folded = total[:, 0:128]
        for at in range(128, nz, 128):
            folded = folded + total[:, at : at + 128]
        sums[index, :] = folded

    group = 4
    behind_e, behind_h, behind_last = group, 2 * group + 1, 3 * group + 1

    def some(p, behind, least, most):
        planes = [p - behind + i for i in range(group)]
        return [q for q in planes if not isinstance(q, int) or least <= q <= most]

    def strike(first, second):
        hit = None
        for at in planes_struck:
            for planes in (first, second):
                if planes:
                    here = (at >= planes[0]) & (at <= planes[-1])
                    hit = here if hit is None else hit | here

        @pl.when(hit)
        def _():
            for k, at in enumerate(planes_struck):
                for p in first:
                    amp = jnp.where(at == p, amps_s[0, k], 0.0)
                    e1[2, p] = e1[2, p] + struck[k] * amp
                for p in second:
                    x = p - 2
                    amp = jnp.where(at == p, amps_s[1, k], 0.0)
                    index = pl.ds(aligned(x * ny), ny)
                    s = [snap_ref[t, 2, index, :].astype(jnp.float32) for t in (1, 2)]
                    folded = jnp.zeros((ny, 128), jnp.float32)
                    for z in range(lanes):
                        here = slice(z * 128, z * 128 + 128)
                        gain = struck[k, 0:ny, here] * amp
                        folded = folded + gain * clean[1, :, here] * (s[0] - s[1])[:, here]
                        for t in range(tiles):
                            here = spot(x, t, z)
                            e_s[2, here, :] = e_s[2, here, :] + gain[t * 8 : t * 8 + 8]
                    sums[index, :] = sums[index, :] + folded

    def one(p):
        last = some(p, behind_last, 2, nx + 1)
        first = some(p, behind_e, 1, nx + 2)
        for q in last:
            second_e(q)
        for q in some(p, behind_h, 1, nx + 1):
            second_h(q)
        for q in first:
            first_e(q)
        for q in some(p, 0, 0, nx + 2):
            first_h(q)
        if first + last:
            if not planes_struck:
                place_ports()
            strike(first, last)

    def body(k, carry):
        one(start + k * group)
        return carry

    start = -(-(2 + behind_last) // group) * group
    passes = (nx + 1 - group - start) // group + 1
    for p in range(0, start, group):
        one(p)
    lax.fori_loop(0, passes, body, 0)
    for p in range(start + passes * group, nx + 2 + behind_last, group):
        one(p)
    for b in range(nx * ny // 128):
        here = pl.ds(b * 128, 128)
        line_ref[:, here] = jnp.sum(jnp.transpose(sums[here, :]), axis=0, keepdims=True)


def finish_ends(
    dims, sizes, own_t, low_ref, high_ref, line_ref, mask_ref, spots_ref, gains_ref, *refs
):
    nx, ny, nz = dims
    step = ny + HALO
    parts = sizes[2]
    ends_ref = refs[0]
    grads = refs[1 : 1 + parts]
    strips, turned, rows_ref = refs[1 + parts :]
    gx, gy, gz = lax.axis_index("gx"), lax.axis_index("gy"), lax.axis_index("gz")
    padded = own_t.shape[1]
    row = lax.broadcasted_iota(jnp.int32, (8, padded), 0)
    lane = lax.broadcasted_iota(jnp.int32, (8, padded), 1) - HALO
    has_low, has_high = gz > 0, gz < sizes[2] - 1
    for k, (msg, ok, far, near) in enumerate(((low_ref, has_low, 2, 3), (high_ref, has_high, 5, 4))):
        for f in range(FIELDS):
            strips[k, f] = own_t[8 * f : 8 * f + 8, :]
            strips[k, f, far : far + 1, :] = jnp.where(ok, msg[8 + f : 9 + f, :], 0.0)
            strips[k, f, near : near + 1, :] = jnp.where(ok, msg[f : f + 1, :], 0.0)

    at = lane + 2
    p = steps_in(at, step)
    y = at - p * step - 2
    inside = ((p >= 2) | (gx > 0)) & ((p < nx + 2) | (gx < sizes[0] - 1))
    inside = inside & ((y >= 0) | (gy > 0)) & ((y < ny) | (gy < sizes[1] - 1))
    found = [
        tuple(spots_ref[3 * q + k : 3 * q + k + 1, 0:1] for k in range(3))
        for q in range(spots_ref.shape[0] // 3)
    ]

    def x_up(v):
        return pltpu.roll(v, padded - step, 1)

    def x_down(v):
        return pltpu.roll(v, step, 1)

    def y_up(v):
        return pltpu.roll(v, padded - 1, 1)

    def y_down(v):
        return pltpu.roll(v, 1, 1)

    def z_up(v):
        return pltpu.roll(v, 7, 0)

    def z_down(v):
        return pltpu.roll(v, 1, 0)

    total = None
    results = []
    for k in range(2):
        ex, ey, ez, hx, hy, hz, coef = (strips[k, f] for f in range(FIELDS))
        first = -4 if k == 0 else nz - 4
        good = ((row >= 4) | has_low) if k == 0 else ((row < 4) | has_high)
        half = jnp.where(inside & good, magnetic_step, 0.0)
        for s in range(STEPS):
            cx = (y_up(ez) - ez) - (z_up(ey) - ey)
            cy = (z_up(ex) - ex) - (x_up(ez) - ez)
            cz = (x_up(ey) - ey) - (y_up(ex) - ex)
            hx, hy, hz = hx - half * cx, hy - half * cy, hz - half * cz
            cx = (hz - y_down(hz)) - (hy - z_down(hy))
            cy = (hx - z_down(hx)) - (hz - x_down(hz))
            cz = (hy - x_down(hy)) - (hx - y_down(hx))
            ex, ey, ez = ex + coef * cx, ey + coef * cy, ez + coef * cz
            for q, (sx, sy, sz) in enumerate(found):
                near = (sx >= -2) & (sx < nx + 2) & (sy >= -2) & (sy < ny + 2)
                hit = (row == sz - first) & (at == (sx + 2) * step + sy + 2) & near
                ez = ez + jnp.where(hit, gains_ref[STEPS * q + s : STEPS * q + s + 1, 0:1], 0.0)
            if k == 0:
                mine = (row == 4) | ((row == 5) & (s == 1))
            else:
                mine = (row == 3) | ((row == 2) & (s == 1))
            for c, e in enumerate((ex, ey, ez)):
                tile = FIELDS + c + 3 * (1 - s)
                one = jnp.where(mine, e * own_t[8 * tile : 8 * tile + 8, :], 0.0)
                total = one if total is None else total + one
        results.append((ex, ey, ez, hx, hy, hz))
    for c in range(6):
        rows_ref[8 * c : 8 * c + 8, :] = jnp.where(row < 4, results[1][c], results[0][c])
    line = jnp.sum(total, axis=0, keepdims=True)
    column = columns_of([(line_ref[...], ny, 0), (line, step, 2 * step + HALO)], nx, ny)
    turned[0:ny, :] = column * mask_ref[...].astype(jnp.float32)
    turned[ny:, :] = jnp.zeros((8, nx), jnp.float32)
    width = ny // parts
    for shift in range(parts):
        owner = partner_of(gz, shift, parts)
        grads[shift][...] = turned[pl.ds(owner * width, width), :]
    ends_ref[...] = rows_ref[...]


def write_out(dims, e_s, h_s, ends_ref, e_out, h_out, spare, e_v, h_v, ends_t, sems):
    nx, ny, nz = dims
    lanes = nz // 128
    tiles = ny // 8
    plane = ny * lanes
    step = ny + HALO
    lane = lax.broadcasted_iota(jnp.int32, (8, 128), 1)
    spare[...] = jnp.zeros(spare.shape, jnp.float32)
    spare[0 : ends_ref.shape[0], :] = ends_ref[...]
    for b in range(spare.shape[1] // 128):
        ends_t[b * 128 : (b + 1) * 128, :] = jnp.transpose(spare[:, b * 128 : (b + 1) * 128])

    def one(x, carry):
        for t in range(tiles):
            v = ends_t[pl.ds(pl.multiple_of((x + 2) * step + HALO + t * 8, 8), 8), :]
            for c in range(6):
                src, dst = (e_s, e_v) if c < 3 else (h_s, h_v)
                placed = pltpu.roll(v, 124 - 8 * c, 1)
                for z in range(lanes):
                    here = pl.ds(pl.multiple_of(((x * tiles + t) * lanes + z) * 8, 8), 8)
                    out = src[c % 3, here, :]
                    if z == 0:
                        out = jnp.where(lane < 2, placed, out)
                    if z == lanes - 1:
                        out = jnp.where(lane >= 126, placed, out)
                    dst[c % 3, here, :] = out
        return carry

    chunk = nx // 4
    copies = []
    for c in range(4):
        lax.fori_loop(c * chunk, (c + 1) * chunk, one, 0, unroll=True)
        here = pl.ds(c * chunk * plane, chunk * plane)
        for k, (src, dst) in enumerate(((e_v, e_out), (h_v, h_out))):
            copy = pltpu.make_async_copy(src.at[:, here], dst.at[:, here], sems.at[2 * c + k])
            copy.start()
            copies.append(copy)
    for copy in copies:
        copy.wait()


def params(limit=12):
    return pltpu.CompilerParams(vmem_limit_bytes=limit * 1024 * 1024)


def body(sizes, e_adjoint, h_adjoint, snapshots, material, permittivity, design_mask, ports, amplitudes):
    permittivity = in_hbm(permittivity)
    permittivity = in_hbm(permittivity)
    dims = material.shape
    nx, ny, nz = dims
    lanes = nz // 128
    tiles = ny // 8
    plane = ny * lanes
    cells = nx * ny
    step = ny + HALO
    padded = -(-((nx + 4) * step + HALO) // 128) * 128
    f32, i32 = jnp.float32, jnp.int32
    xs, ys = swaps(sizes[0]), swaps(sizes[1])
    block, cube = jax.ShapeDtypeStruct, pltpu.VMEM

    shapes = [block((9 * plane + ny, 128), f32) for _ in xs]
    shapes += [block((9 * lanes * nx + 8, 128), f32) for _ in ys]
    shapes += [block((lanes, 4 * FIELDS, 128), f32) for _ in xs for _ in ys]
    buffers = []
    for _ in xs:
        tile = (2, tiles, lanes, 8, 128)
        buffers += [cube((3, *tile), f32), cube((3, *tile), f32), cube(tile, i32)]
    for _ in ys:
        tile = ((nx + 1) * lanes * 8, 128)
        buffers += [cube((3, *tile), f32), cube((3, *tile), f32), cube(tile, i32)]
    n_copies = 3 * (len(xs) + len(ys)) + 1
    shapes += [block((permittivity.shape[0], 128), f32)]
    *msgs, table = pl.pallas_call(
        functools.partial(send_faces, dims, sizes),
        out_shape=shapes,
        in_specs=[HBM, HBM, HBM, HBM],
        out_specs=[VM] * len(shapes),
        scratch_shapes=buffers
        + [pltpu.SMEM(permittivity.shape, f32), pltpu.SemaphoreType.DMA((n_copies,))],
        compiler_params=params(),
        name="send_faces",
    )(
        in_hbm(tiles_of(e_adjoint)),
        in_hbm(tiles_of(h_adjoint)),
        in_hbm(tiles_of(material)),
        permittivity,
    )
    e_v, h_v, m_v = in_vmem(tiled(e_adjoint)), in_vmem(tiled(h_adjoint)), in_vmem(tiled(material))
    snaps = in_hbm(snapshots.reshape(STEPS + 1, 3, cells, nz))
    coef_v, own_packed, s = pl.pallas_call(
        functools.partial(own_ends, dims),
        out_shape=[cube(m_v.shape, f32), cube((padded, 128), f32), cube(snaps.shape, snaps.dtype)],
        in_specs=[VM, VM, VM, HBM, VM],
        out_specs=[VM] * 3,
        scratch_shapes=[pltpu.SemaphoreType.DMA((3 * (STEPS + 1),))],
        compiler_params=params(),
        cost_estimate=pl.CostEstimate(flops=10**7, bytes_accessed=4 * 10**6, transcendentals=0),
        name="own_ends",
    )(e_v, h_v, m_v, snaps, table)

    both = ("gx", "gy")

    def meet(x, y, tx, ty):
        if tx[x] == x or ty[y] == y:
            return x * sizes[1] + y
        return tx[x] * sizes[1] + ty[y]

    tables = [("gx", list(enumerate(swap_table(sizes[0], o)))) for o in xs]
    tables += [("gy", list(enumerate(swap_table(sizes[1], o)))) for o in ys]
    for ox in xs:
        for oy in ys:
            tx, ty = swap_table(sizes[0], ox), swap_table(sizes[1], oy)
            pairs = [
                (x * sizes[1] + y, meet(x, y, tx, ty))
                for x in range(sizes[0])
                for y in range(sizes[1])
            ]
            tables.append((both, pairs))
    got = [lax.ppermute(msg, axis, pairs) for msg, (axis, pairs) in zip(msgs, tables)]

    xh, yh, own_t, up, down = pl.pallas_call(
        functools.partial(unpack_faces, dims, sizes),
        out_shape=[
            cube((FIELDS, lanes, 4 * ny, 128), f32),
            cube((FIELDS, lanes, (nx + 4) * HALO, 128), f32),
            cube((128, padded), f32),
            block((16, padded), f32),
            block((16, padded), f32),
        ],
        in_specs=[VM] * (1 + len(got)),
        out_specs=[VM] * 5,
        scratch_shapes=[
            pltpu.VMEM((padded, 128), f32),
            pltpu.VMEM((4 * ny, 128), f32),
            pltpu.VMEM(((nx + 4) * HALO, 128), f32),
        ],
        compiler_params=params(),
        name="unpack_faces",
    )(own_packed, *got)

    parts = sizes[2]
    low = lax.ppermute(up, "gz", [(i, (i + 1) % parts) for i in range(parts)])
    high = lax.ppermute(down, "gz", [(i, (i - 1) % parts) for i in range(parts)])

    ported = ports.shape[0]
    e_s, h_s, line, spots, gains = pl.pallas_call(
        functools.partial(march, dims, sizes),
        out_shape=[cube(e_v.shape, f32), cube(h_v.shape, f32), block((1, cells), f32)]
        + [block((3 * ported, 128), i32), block((STEPS * ported, 128), f32)],
        in_specs=[VM] * 6 + [HBM, HBM],
        out_specs=[VM] * 5,
        scratch_shapes=[
            pltpu.VMEM((3, nx + 4, step, nz), f32),
            pltpu.VMEM((3, nx + 4, step, nz), f32),
            pltpu.VMEM((3, nx + 4, step, nz), f32),
            pltpu.VMEM((step, nz), f32),
            pltpu.VMEM((ported, step, nz), f32),
            pltpu.VMEM((2, ny, nz), f32),
            pltpu.VMEM((cells, 128), f32),
            pltpu.SMEM(ports.shape, i32),
            pltpu.SMEM(amplitudes.shape, f32),
            pltpu.SemaphoreType.DMA((2,)),
        ],
        compiler_params=params(24),
        cost_estimate=pl.CostEstimate(flops=4 * 10**7, bytes_accessed=10**7, transcendentals=0),
        name="march",
    )(e_v, h_v, coef_v, xh, yh, s, in_hbm(ports), in_hbm(amplitudes))
    ends, *chunks = pl.pallas_call(
        functools.partial(finish_ends, dims, sizes),
        out_shape=[cube((48, padded), f32)] + [block((ny // parts, nx), f32)] * parts,
        in_specs=[VM] * 7,
        out_specs=[VM] * (1 + parts),
        scratch_shapes=[
            pltpu.VMEM((2, FIELDS, 8, padded), f32),
            pltpu.VMEM((ny + 8, nx), f32),
            pltpu.VMEM((48, padded), f32),
        ],
        compiler_params=params(),
        name="finish_ends",
    )(own_t, low, high, line, design_mask.T, spots, gains)
    e_out, h_out = pl.pallas_call(
        functools.partial(write_out, dims),
        out_shape=[block(e_v.shape, f32), block(h_v.shape, f32)],
        in_specs=[VM] * 3,
        out_specs=[HBM] * 2,
        scratch_shapes=[
            pltpu.VMEM((128, padded), f32),
            pltpu.VMEM(e_v.shape, f32),
            pltpu.VMEM(h_v.shape, f32),
            pltpu.VMEM((padded, 128), f32),
            pltpu.SemaphoreType.DMA((8,)),
        ],
        compiler_params=params(),
        cost_estimate=pl.CostEstimate(flops=10**7, bytes_accessed=8 * 10**6, transcendentals=0),
        name="write_out",
    )(e_s, h_s, ends)
    gradient = chunks[0]
    for shift in range(1, parts):
        gradient = gradient + lax.ppermute(
            chunks[shift], "gz", [(i, partner_of(i, shift, parts)) for i in range(parts)]
        )
    return untiled(e_out, dims), untiled(h_out, dims), gradient.T


def solution(mesh):
    placed = (
        P(None, "gx", "gy", "gz"),
        P(None, "gx", "gy", "gz"),
        P(None, None, "gx", "gy", "gz"),
        P("gx", "gy", "gz"),
        P(),
        P("gx", "gy"),
        P(),
        P(),
    )
    sizes = tuple(mesh.shape[axis] for axis in ("gx", "gy", "gz"))
    return jax.shard_map(
        functools.partial(body, sizes),
        mesh=mesh,
        in_specs=placed,
        out_specs=(P(None, "gx", "gy", "gz"), P(None, "gx", "gy", "gz"), P("gx", ("gy", "gz"))),
        check_vma=False,
    )
```
